512 devices in a mesh: gx: 4 (over x), gy: 8 (over z), gz: 16 (over y, core).
Axes of the slice: x: 4, y: 8, z: 8, core: 2. Of those that a mesh axis runs over, the one named last changes fastest.
Arguments:
- right_side: float32 [128, 256, 512], P('gz', 'gy', 'gx'), may hold values from -6 to 6
- guess: float32 [128, 256, 512], P('gz', 'gy', 'gx'), may hold values from -6 to 6
- coefficient: float32 [128, 256, 512], P('gz', 'gy', 'gx'), may hold values from 0.3 to 3
Outputs:
- solution: float32 [128, 256, 512], P('gz', 'gy', 'gx')
- residual: float32 [128, 256, 512], P('gz', 'gy', 'gx')
The draws below stay inside these ranges and needn't reach their ends.
All inputs are finite; a program needn't handle non-finite values.
Results may differ from the reference program's by a relative error of at most 0.00035.
Values sent between devices are 32-bit elements; how exact they have to be, the bound alone decides.
No kernel may reach another device: no remote copies, remote signals or barrier semaphores. Data moves between devices by JAX's collectives and lax.ppermute only.
A program may use at most 64 MiB of HBM per device.

```python
import math
import jax
import jax.numpy as jnp
from jax import lax

DEG = 2
ITERS = 6
NZ = 128
NY = 256
NX = 512


def draw_right_side(key, part):
    key = jax.random.fold_in(key, 7)
    grid_shape = (NZ, NY, NX)
    return jnp.clip(jax.random.normal(key, grid_shape, jnp.float32), -6.0, 6.0)


def shard_levels(rng, extent, split, least, top_value):
    level = 1.0
    for dim, shards_of in split:
        draws = jax.random.uniform(jax.random.fold_in(jax.random.fold_in(rng, 6), dim), (shards_of,), jnp.float32, least / len(split), top_value / len(split))
        level = level * jnp.repeat(jnp.exp(draws), extent[dim] // shards_of).reshape((-1,) + (1,) * (len(extent) - 1 - dim))
    return level


def normal_values(stream_key, dims, width, reach, shards=(), kind=jnp.bfloat16):
    result = width * jax.random.normal(stream_key, dims, jnp.float32)
    if shards:
        result = result * shard_levels(stream_key, dims, shards, -0.22, 0.18)
    return jnp.clip(result, -reach, reach).astype(kind)


def setup_inputs(seed: int = 0) -> dict:
    streams_of = jax.random.split(jax.random.key(seed), 4)
    right_side = draw_right_side(jax.random.fold_in(streams_of[3], 71), 0)
    guess = normal_values(streams_of[1], (NZ, NY, NX), 1.0, 6.0, ((0, 16), (1, 8), (2, 4)), jnp.float32)
    coefficient = jnp.clip(jnp.exp(math.log(3.0) - 2.3025851 * jax.random.uniform(streams_of[2], (NZ, NY, NX), jnp.float32) ** shard_levels(streams_of[2], (NZ, NY, NX), ((0, 16), (1, 8), (2, 4)), -0.2, 0.2)), 0.3, 3.0)
    return {"right_side": right_side, "guess": guess, "coefficient": coefficient}


lower_bound = 0.5
upper_bound = 2.0


def neighbours(padded):
    centre = padded[1:-1, 1:-1, 1:-1]
    others = [padded[2:, 1:-1, 1:-1], padded[:-2, 1:-1, 1:-1], padded[1:-1, 2:, 1:-1], padded[1:-1, :-2, 1:-1], padded[1:-1, 1:-1, 2:], padded[1:-1, 1:-1, :-2]]
    return others, centre


def stencil(source_padded, coeff_padded, scale):
    values, centre_value = neighbours(source_padded)
    coeffs, centre_coeff = neighbours(coeff_padded)
    total = jnp.zeros_like(centre_value)
    for value, coeff in zip(values, coeffs):
        total = total + 0.5 * (centre_coeff + coeff) * (centre_value - value)
    return scale * total


def diagonal_of(coeff_padded, scale):
    coeffs, centre_coeff = neighbours(coeff_padded)
    total = jnp.zeros_like(centre_coeff)
    for coeff in coeffs:
        total = total + 0.5 * (centre_coeff + coeff)
    return scale * total


def coarsen(source):
    depth, rows, cols = source.shape
    return source.reshape(depth // 2, 2, rows // 2, 2, cols // 2, 2).mean(axis=(1, 3, 5))


def refine_axis(padded, dimension):
    count = padded.shape[dimension] - 2
    before = lax.slice_in_dim(padded, 0, count, axis=dimension)
    centre = lax.slice_in_dim(padded, 1, count + 1, axis=dimension)
    after = lax.slice_in_dim(padded, 2, count + 2, axis=dimension)
    stacked = jnp.stack([0.75 * centre + 0.25 * before, 0.75 * centre + 0.25 * after], axis=dimension + 1)
    new_shape = list(centre.shape)
    new_shape[dimension] = 2 * count
    return stacked.reshape(new_shape)


def prolong(padded):
    for dimension in range(3):
        padded = refine_axis(padded, dimension)
    return padded


def chebyshev(current, remainder, apply_op, inverse):
    theta = 0.5 * (upper_bound + lower_bound)
    delta = 0.5 * (upper_bound - lower_bound)
    sigma = theta / delta
    rho = 1.0 / sigma
    update = remainder * inverse / theta
    current = current + update
    remainder = remainder - apply_op(update)
    for repeat in range(DEG - 1):
        rho_next = 1.0 / (2.0 * sigma - rho)
        update = (rho_next * rho) * update + (2.0 * rho_next / delta) * (remainder * inverse)
        current = current + update
        remainder = remainder - apply_op(update)
        rho = rho_next
    return current, remainder


def reference(right_side, guess, coefficient):
    kappa_one = coarsen(coefficient)
    kappa_two = coarsen(kappa_one)
    fine_coeff = jnp.pad(coefficient, 1)
    middle_coeff = jnp.pad(kappa_one, 1)
    coarse_coeff = jnp.pad(kappa_two, 1)

    def apply_fine(source):
        return stencil(jnp.pad(source, 1), fine_coeff, 1.0)

    def apply_middle(source):
        return stencil(jnp.pad(source, 1), middle_coeff, 0.25)

    def apply_coarse(source):
        return stencil(jnp.pad(source, 1), coarse_coeff, 0.0625)

    fine_inverse = 1.0 / diagonal_of(fine_coeff, 1.0)
    middle_inverse = 1.0 / diagonal_of(middle_coeff, 0.25)

    fine_iterate, fine_rest = chebyshev(guess, right_side - apply_fine(guess), apply_fine, fine_inverse)
    middle_rhs = coarsen(fine_rest)
    middle_iterate, middle_rest = chebyshev(jnp.zeros_like(middle_rhs), middle_rhs, apply_middle, middle_inverse)
    coarse_rhs = coarsen(middle_rest)

    answer = jnp.zeros_like(coarse_rhs)
    remainder = coarse_rhs
    direction = coarse_rhs
    norm_now = jnp.sum(remainder * remainder)
    for repeat in range(ITERS):
        image = apply_coarse(direction)
        alpha = norm_now / jnp.sum(direction * image)
        answer = answer + alpha * direction
        remainder = remainder - alpha * image
        norm_next = jnp.sum(remainder * remainder)
        direction = remainder + (norm_next / norm_now) * direction
        norm_now = norm_next

    middle_iterate = middle_iterate + prolong(jnp.pad(answer, 1))
    middle_iterate, middle_rest = chebyshev(middle_iterate, middle_rhs - apply_middle(middle_iterate), apply_middle, middle_inverse)
    solution = fine_iterate + prolong(jnp.pad(middle_iterate, 1))
    solution, residual = chebyshev(solution, right_side - apply_fine(solution), apply_fine, fine_inverse)
    return solution, residual
```

```python
import jax
import jax.numpy as jnp
from jax import lax
from jax.experimental import pallas as pl
from jax.experimental.pallas import tpu as pltpu
from jax.sharding import PartitionSpec as P


ITERS = 6
THETA = 1.25
DELTA = 0.75
SIGMA = THETA / DELTA
RHO = 1.0 / SIGMA
RHO_NEXT = 1.0 / (2.0 * SIGMA - RHO)
FIRST = 1.0 / THETA
KEEP = RHO_NEXT * RHO
GAIN = 2.0 * RHO_NEXT / DELTA

F32 = jnp.float32
BF16 = jnp.bfloat16
VMEM = pl.BlockSpec(memory_space=pltpu.VMEM)
LIMIT = 40 * 1024 * 1024


def shift(value, by, axis):
    return pltpu.roll(value, by % value.shape[axis], axis)


def ahead(value, axis):
    return shift(value, -1, axis)


def behind(value, axis):
    return shift(value, 1, axis)


def iota(shape, axis):
    return lax.broadcasted_iota(jnp.int32, shape, axis)


def exact_dot(value, matrix):
    high = value.astype(BF16)
    rest = value - high.astype(F32)
    middle = rest.astype(BF16)
    low = (rest - middle.astype(F32)).astype(BF16)
    parts = [jnp.dot(part, matrix, preferred_element_type=F32) for part in (low, middle, high)]
    return parts[0] + parts[1] + parts[2]


def pick(condition, number):
    return jnp.where(condition, jnp.float32(number), jnp.float32(0.0))


def refine_matrix(size, out_size):
    parent = iota((size, out_size), 0)
    child = iota((size, out_size), 1)
    own = lax.shift_right_arithmetic(child, 1)
    other = (own + 2 * (child & 1) - 1 + size) & (size - 1)
    wide = out_size // 2
    if wide < size:
        own = jnp.where(child >= out_size * 3 // 4, own + size - wide, own)
        other = (own + 2 * (child & 1) - 1 + size) & (size - 1)
    return (pick(parent == own, 0.75) + pick(parent == other, 0.25)).astype(BF16)


def xpack_kernel(mid, low, high, ylow, yhigh, window, to_left, to_right):
    for a in range(3):
        window[a * 24 : a * 24 + 8, 1:5] = low[a].reshape(8, 4, 8, 128)
        window[a * 24 + 8 : a * 24 + 16, 1:5] = mid[a].reshape(8, 4, 8, 128)
        window[a * 24 + 16 : a * 24 + 24, 1:5] = high[a].reshape(8, 4, 8, 128)
        window[a * 24 : a * 24 + 24, 0] = ylow[a]
        window[a * 24 : a * 24 + 24, 5] = yhigh[a]
    slot = lax.shift_right_logical(iota((8, 128), 1), 3)

    def group(i, carry):
        for packed in range(3):
            left = jnp.zeros((8, 128), F32)
            right = jnp.zeros((8, 128), F32)
            for s in range(16):
                j = packed * 16 + s
                tile = window[8 * i + j // 6, j % 6]
                left = jnp.where(slot == s, shift(tile, 8 * s, 1), left)
                right = jnp.where(slot == s, shift(tile, 8 * s + 8, 1), right)
            to_left[3 * i + packed] = left
            to_right[3 * i + packed] = right
        return carry

    lax.fori_loop(0, 9, group, 0)


def plane(ref, z):
    return ref[pl.ds(6 * z, 6)].reshape(48, 256)


def put(ref, z, value):
    ref[pl.ds(6 * z, 6)] = value.reshape(6, 8, 256)


def inner_flux(v, wx, wy):
    fx = wx * (ahead(v, 1) - v)
    fy = wy * (ahead(v, 0) - v)
    return (fx - behind(fx, 1)) + (fy - behind(fy, 0))


def sweep(first, last, source, wx, wy, wz, step):
    v = plane(source, first)
    carry = (v, plane(wz, first - 1) * (v - plane(source, first - 1)))

    def body(z, carry):
        v, below = carry
        after = plane(source, z + 1)
        above = plane(wz, z) * (after - v)
        step(z, v, inner_flux(v, plane(wx, z), plane(wy, z)) + (above - below))
        return (after, above)

    lax.fori_loop(first, last + 1, body, carry)


def zpair(low_face):
    pad = jnp.zeros((1,) + low_face.shape[1:], F32)
    return jnp.concatenate([low_face, pad], 0) - jnp.concatenate([pad, low_face], 0)


def middle_weights(kappa):
    half = 0.125 * kappa
    wx = half + ahead(half, 2)
    wy = half + ahead(half, 1)
    wz = half[:-1] + half[1:]
    pad = jnp.zeros((1,) + half.shape[1:], F32)
    diag = wx + behind(wx, 2) + wy + behind(wy, 1)
    diag = diag + jnp.concatenate([wz, pad], 0) + jnp.concatenate([pad, wz], 0)
    inside = kappa > 0.0
    inverse = jnp.where(inside, 1.0 / jnp.where(inside, diag, 1.0), 0.0)
    return wx, wy, wz, inverse


def middle_minus(v, weights):
    wx, wy, wz, _ = weights
    fx = wx * (ahead(v, 2) - v)
    fy = wy * (ahead(v, 1) - v)
    return (fx - behind(fx, 2)) + (fy - behind(fy, 1)) + zpair(wz * (v[1:] - v[:-1]))


def down_kernel(
    window, from_left, from_right,
    share, um_out, mr_out, k1_out, iterate, right, wx, wy, wz, inverse,
    kappa, guess, rest, update, second, sums_a, sums_b, line,
):
    lane = iota((8, 128), 1)

    def unpack(i, dest, base):
        for packed in range(3):
            hi = from_right[base * 9 + 3 * i + packed]
            lo = from_left[base * 9 + 3 * i + packed]
            for s in range(16):
                j = packed * 16 + s
                edge = jnp.where(lane < 8, shift(hi, -8 * s, 1), 0.0)
                edge = jnp.where(lane >= 120, shift(lo, 120 - 8 * s, 1), edge)
                dest[48 * i + j, :, 0:128] = window[base * 24 + 8 * i + j // 6, j % 6]
                dest[48 * i + j, :, 128:256] = edge

    def unpack_all(i, carry):
        unpack(i, guess, 0)
        unpack(i, right, 1)
        unpack(i, kappa, 2)
        return carry

    lax.fori_loop(0, 3, unpack_all, 0)

    def weights(z, carry):
        half, below = carry
        after = 0.5 * plane(kappa, z + 1)
        x = half + ahead(half, 1)
        y = half + ahead(half, 0)
        above = half + after
        diag = x + behind(x, 1) + y + behind(y, 0) + above + below
        inside = half > 0.0
        put(wx, z, x)
        put(wy, z, y)
        put(wz, z, above)
        put(inverse, z, jnp.where(inside, 1.0 / jnp.where(inside, diag, 1.0), 0.0))
        return (after, above)

    half0 = 0.5 * plane(kappa, 0)
    half1 = 0.5 * plane(kappa, 1)
    put(wz, 0, half0 + half1)
    lax.fori_loop(1, 23, weights, (half1, half0 + half1))

    def first(z, v, minus):
        r = plane(right, z) + minus
        put(rest, z, r)
        put(update, z, FIRST * r * plane(inverse, z))

    sweep(1, 22, guess, wx, wy, wz, first)

    def next_step(z, v, minus):
        r = plane(rest, z) + minus
        d = KEEP * v + GAIN * (r * plane(inverse, z))
        put(rest, z, r)
        put(second, z, d)
        put(iterate, z, plane(guess, z) + v + d)

    sweep(2, 21, update, wx, wy, wz, next_step)

    def last(z, v, minus):
        put(rest, z, plane(rest, z) + minus)

    sweep(3, 20, second, wx, wy, wz, last)

    def add_pairs(ref, start, count, at):
        def body(m, carry):
            pair = plane(ref, start + 2 * m) + plane(ref, start + 2 * m + 1)
            rows = pl.ds(pl.multiple_of((at + m) * 48, 48), 48)
            sums_a[rows, :] = pair[:, :128]
            sums_b[rows, :] = pair[:, 128:]
            return carry

        lax.fori_loop(0, count, body, 0)

    add_pairs(rest, 4, 8, 0)
    add_pairs(kappa, 0, 12, 8)

    def fold(ref):
        return ref[pl.ds(0, 480, stride=2), :] + ref[pl.ds(1, 480, stride=2), :]

    coarsen = pick(lax.shift_right_logical(iota((256, 128), 0), 1) == iota((256, 128), 1), 0.125)
    both = exact_dot(jnp.concatenate([fold(sums_a), fold(sums_b)], 1), coarsen.astype(BF16))
    both = both.reshape(20, 24, 128)
    kappa_one = both[8:]
    pad = jnp.zeros((2, 24, 128), F32)
    rhs = jnp.concatenate([pad, both[:8], pad], 0)
    weights_one = middle_weights(kappa_one)
    inverse_one = weights_one[3]
    d = FIRST * (rhs * inverse_one)
    r = rhs + middle_minus(d, weights_one)
    d2 = KEEP * d + GAIN * (r * inverse_one)
    r = r + middle_minus(d2, weights_one)
    um_out[...] = d + d2
    mr_out[...] = rhs
    k1_out[...] = kappa_one

    cell = iota((128, 128), 0)
    place = iota((128, 128), 1)
    total = jnp.zeros((24, 128), F32)
    for q, field in enumerate((r[4] + r[5], r[6] + r[7], kappa_one[4] + kappa_one[5], kappa_one[6] + kappa_one[7])):
        to = (cell < 64) & (lax.shift_right_logical(cell, 1) + 32 * q == place)
        total = total + exact_dot(field, pick(to, 0.125).astype(BF16))
    line[...] = total
    cells = line[pl.ds(4, 8, stride=2), :] + line[pl.ds(5, 8, stride=2), :]
    cells = pltpu.roll(cells, 32 * lax.axis_index("gx"), 1)
    share[...] = jnp.broadcast_to(cells[None], (128, 8, 128))


def cplane(ref, z):
    return ref[pl.ds(8 * z, 8)].reshape(64, 128)


def cput(ref, z, value):
    ref[pl.ds(8 * z, 8)] = value.reshape(8, 8, 128)


def coarse_kernel(gathered, out, kappa, wx, wy, wz, diag, rest, direction, image, answer):
    lane = iota((8, 128), 1)
    group = lax.shift_right_logical(lane, 5)
    nothing = jnp.zeros((64, 128), F32)
    for ref in (kappa, direction):
        cput(ref, 0, nothing)
        cput(ref, 33, nothing)
    cput(wz, 0, nothing)
    answer[...] = jnp.zeros_like(answer)

    def assemble(gz, carry):
        for gy in range(8):
            pieces = [gathered[gx, gy * 16 + gz] for gx in range(4)]
            for q in range(4):
                merged = pieces[0]
                for gx in range(1, 4):
                    merged = jnp.where(group == (q + gx) % 4, pieces[gx], merged)
                merged = shift(merged, -32 * q, 1)
                if q < 2:
                    rest[(2 * gz + q) * 8 + gy] = merged
                    direction[(2 * gz + q + 1) * 8 + gy] = merged
                else:
                    kappa[(2 * gz + q - 1) * 8 + gy] = merged
        return carry

    lax.fori_loop(0, 16, assemble, 0)
    inner_x = iota((64, 128), 1) < 127
    inner_y = iota((64, 128), 0) < 63
    first_x = iota((64, 128), 1) > 0
    first_y = iota((64, 128), 0) > 0

    def weights(z, total):
        half = 0.03125 * cplane(kappa, z + 1)
        before = 0.03125 * cplane(kappa, z)
        after = 0.03125 * cplane(kappa, z + 2)
        x = jnp.where(inner_x, ahead(half, 1), 0.0)
        y = jnp.where(inner_y, ahead(half, 0), 0.0)
        cput(wx, z, jnp.where(inner_x, half + x, 0.0))
        cput(wy, z, jnp.where(inner_y, half + y, 0.0))
        cput(wz, z + 1, half + after)
        x = x + jnp.where(first_x, behind(half, 1), 0.0)
        y = y + jnp.where(first_y, behind(half, 0), 0.0)
        cput(diag, z, 6.0 * half + x + y + (before + after))
        r = cplane(rest, z)
        return total + (r * r).reshape(8, 8, 128).sum(0)

    zero = jnp.zeros((8, 128), F32)

    def whole(total):
        return jnp.sum(jnp.sum(total, axis=0, keepdims=True), axis=1, keepdims=True)

    norm = whole(lax.fori_loop(0, 32, weights, zero))

    def apply(z, total):
        v = cplane(direction, z + 1)
        x = cplane(wx, z)
        y = cplane(wy, z)
        w = cplane(diag, z) * v
        w = w - (x * ahead(v, 1) + behind(x * v, 1))
        w = w - (y * ahead(v, 0) + behind(y * v, 0))
        w = w - (cplane(wz, z + 1) * cplane(direction, z + 2) + cplane(wz, z) * cplane(direction, z))
        cput(image, z, w)
        return total + (v * w).reshape(8, 8, 128).sum(0)

    def add_answer(z, alpha):
        at = pl.ds((z + 3) * 10 + 1, 8)
        answer[at] = answer[at] + (alpha * cplane(direction, z + 1)).reshape(8, 8, 128)

    for repeat in range(ITERS):
        alpha = norm / whole(lax.fori_loop(0, 32, apply, zero))
        if repeat + 1 < ITERS:

            def step(z, total):
                add_answer(z, alpha)
                r = cplane(rest, z) - alpha * cplane(image, z)
                cput(rest, z, r)
                return total + (r * r).reshape(8, 8, 128).sum(0)

            norm_next = whole(lax.fori_loop(0, 32, step, zero))
            beta = norm_next / norm

            def turn(z, carry):
                cput(direction, z + 1, cplane(rest, z) + beta * cplane(direction, z + 1))
                return carry

            lax.fori_loop(0, 32, turn, 0)
            norm = norm_next
        else:

            def finish(z, carry):
                add_answer(z, alpha)
                return carry

            lax.fori_loop(0, 32, finish, 0)

    gx = lax.axis_index("gx")
    gy = lax.axis_index("gy")
    gz = lax.axis_index("gz")
    wide = iota((24, 128), 1)
    position = jnp.where(wide < 64, wide, wide - 128) + 32 * gx
    known = (position >= 0) & (position < 128)
    for z in range(8):
        block = answer[pl.ds((2 * gz + z) * 10 + gy, 3)].reshape(24, 128)
        out[z] = jnp.where(known, pltpu.roll(block, (128 - 32 * gx) & 127, 1), 0.0)


def up_kernel(
    coarse, um, mr, k1, iterate, right, wx, wy, wz, inverse,
    solution_out, residual_out,
    line, fine_a, fine_b, current, rest, update, second,
):
    c = coarse[...]
    even = 0.75 * c[1:7] + 0.25 * c[0:6]
    odd = 0.75 * c[1:7] + 0.25 * c[2:8]
    c = jnp.stack([even, odd], 1).reshape(12, 24, 128)
    matrix = refine_matrix(128, 128)
    line[pl.ds(0, 288, stride=2), :] = exact_dot((0.75 * c + 0.25 * behind(c, 1)).reshape(288, 128), matrix)
    line[pl.ds(1, 288, stride=2), :] = exact_dot((0.75 * c + 0.25 * ahead(c, 1)).reshape(288, 128), matrix)
    correction = shift(line[...].reshape(12, 48, 128), -12, 1)[:, :24]

    kappa_one = k1[...]
    weights = middle_weights(kappa_one)
    inverse_one = weights[3]
    u = jnp.where(kappa_one > 0.0, um[...] + correction, 0.0)
    r = mr[...] + middle_minus(u, weights)
    d = FIRST * (r * inverse_one)
    u = u + d
    r = r + middle_minus(d, weights)
    u = u + (KEEP * d + GAIN * (r * inverse_one))

    even = 0.75 * u[2:10] + 0.25 * u[1:9]
    odd = 0.75 * u[2:10] + 0.25 * u[3:11]
    m = jnp.stack([even, odd], 1).reshape(16, 24, 128)
    matrix = refine_matrix(128, 256)
    for parity, near in enumerate((behind(m, 1), ahead(m, 1))):
        value = exact_dot((0.75 * m + 0.25 * near).reshape(384, 128), matrix)
        fine_a[pl.ds(parity, 384, stride=2), :] = value[:, :128]
        fine_b[pl.ds(parity, 384, stride=2), :] = value[:, 128:]

    def begin(z, carry):
        rows = pl.ds(pl.multiple_of((z - 4) * 48, 48), 48)
        fine = jnp.concatenate([fine_a[rows, :], fine_b[rows, :]], 1)
        put(current, z, jnp.where(plane(inverse, z) > 0.0, plane(iterate, z) + fine, 0.0))
        return carry

    lax.fori_loop(4, 20, begin, 0)

    def first(z, v, minus):
        r = plane(right, z) + minus
        put(rest, z, r)
        put(update, z, FIRST * r * plane(inverse, z))

    sweep(5, 18, current, wx, wy, wz, first)

    def next_step(z, v, minus):
        r = plane(rest, z) + minus
        d = KEEP * v + GAIN * (r * plane(inverse, z))
        put(rest, z, r)
        put(second, z, d)
        put(current, z, plane(current, z) + v + d)

    sweep(6, 17, update, wx, wy, wz, next_step)

    def last(z, v, minus):
        residual_out[z - 8] = (plane(rest, z) + minus)[8:40, :128]
        solution_out[z - 8] = plane(current, z)[8:40, :128]

    sweep(8, 15, second, wx, wy, wz, last)


def run(kernel, outs, scratch, *args):
    return pl.pallas_call(
        kernel,
        out_shape=[jax.ShapeDtypeStruct(shape, F32) for shape in outs],
        in_specs=[VMEM] * len(args),
        out_specs=[VMEM] * len(outs),
        scratch_shapes=[pltpu.VMEM(shape, F32) for shape in scratch],
        compiler_params=pltpu.CompilerParams(vmem_limit_bytes=LIMIT),
    )(*args)


def up(axis):
    return [(i, i + 1) for i in range(lax.axis_size(axis) - 1)]


def down(axis):
    return [(i + 1, i) for i in range(lax.axis_size(axis) - 1)]


def both_ways(to_low, to_high, axis):
    return lax.ppermute(to_high, axis, up(axis)), lax.ppermute(to_low, axis, down(axis))


def local(right_side, guess, coefficient):
    mine = jnp.stack([guess, right_side, coefficient])
    low, high = both_ways(mine, mine, "gz")
    column = jnp.concatenate([low, mine, high], 1)
    ylow, yhigh = both_ways(column[:, :, :8], column[:, :, 24:], "gy")
    window, to_left, to_right = run(
        xpack_kernel, [(72, 6, 8, 128), (27, 8, 128), (27, 8, 128)], [], mine, low, high, ylow, yhigh
    )
    from_left, from_right = both_ways(to_left, to_right, "gx")

    fine = (144, 8, 256)
    middle = (12, 24, 128)
    share, um, mr, k1, *arrays = run(
        down_kernel,
        [(128, 8, 128), middle, middle, middle] + [fine] * 6,
        [fine] * 5 + [(960, 128)] * 2 + [(24, 128)],
        window, from_left, from_right,
    )
    plane_of = lax.all_to_all(share, ("gy", "gz"), 0, 0)
    whole = lax.all_to_all(jnp.broadcast_to(plane_of[None], (4, 128, 8, 128)), "gx", 0, 0)

    pair = jnp.stack([um, mr])[:, 4:8, 4:20, :64]
    low, high = both_ways(pair, pair, "gz")
    pair = jnp.concatenate([low, pair, high], 1)
    low, high = both_ways(pair[:, :, :4], pair[:, :, 12:], "gy")
    pair = jnp.concatenate([low, pair, high], 2)
    low, high = both_ways(pair[..., :4], pair[..., 60:], "gx")
    pair = jnp.concatenate([pair, high, jnp.zeros((2, 12, 24, 56), F32), low], 3)

    coarse_grid = (256, 8, 128)
    padded = (272, 8, 128)
    coarse = run(
        coarse_kernel,
        [(8, 24, 128)],
        [padded] + [coarse_grid] * 2 + [padded] + [coarse_grid] * 2 + [padded, coarse_grid, (380, 8, 128)],
        whole,
    )[0]
    solution, residual = run(
        up_kernel,
        [(8, 32, 128)] * 2,
        [(576, 128)] + [(768, 128)] * 2 + [fine] * 4,
        coarse, pair[0], pair[1], k1, *arrays,
    )
    return solution, residual


def solution(mesh):
    spec = P("gz", "gy", "gx")
    return jax.shard_map(
        local, mesh=mesh, in_specs=(spec, spec, spec), out_specs=(spec, spec), check_vma=False
    )
```

```python
import jax
import jax.numpy as jnp
from jax import lax
from jax.experimental import pallas as pl
from jax.experimental.pallas import tpu as pltpu
from jax.sharding import PartitionSpec as P


ITERS = 6
THETA = 1.25
DELTA = 0.75
SIGMA = THETA / DELTA
RHO = 1.0 / SIGMA
RHO_NEXT = 1.0 / (2.0 * SIGMA - RHO)
FIRST = 1.0 / THETA
KEEP = RHO_NEXT * RHO
GAIN = 2.0 * RHO_NEXT / DELTA

F32 = jnp.float32
BF16 = jnp.bfloat16
VMEM = pl.BlockSpec(memory_space=pltpu.VMEM)
LIMIT = 20 * 1024 * 1024


def loop(first, end, body, carry, unroll=8):
    count = end - first
    while count % unroll:
        unroll -= 1

    def several(i, carry):
        for k in range(unroll):
            carry = body(first + i * unroll + k, carry)
        return carry

    return lax.fori_loop(0, count // unroll, several, carry)


def shift(value, by, axis):
    return pltpu.roll(value, by % value.shape[axis], axis)


def ahead(value, axis):
    return shift(value, -1, axis)


def behind(value, axis):
    return shift(value, 1, axis)


def iota(shape, axis):
    return lax.broadcasted_iota(jnp.int32, shape, axis)


def exact_dot(value, matrix):
    high = value.astype(BF16)
    rest = value - high.astype(F32)
    middle = rest.astype(BF16)
    low = (rest - middle.astype(F32)).astype(BF16)
    parts = [jnp.dot(part, matrix, preferred_element_type=F32) for part in (low, middle, high)]
    return parts[0] + parts[1] + parts[2]


def pick(condition, number):
    return jnp.where(condition, jnp.float32(number), jnp.float32(0.0))


def refine_matrix(size, out_size):
    parent = iota((size, out_size), 0)
    child = iota((size, out_size), 1)
    own = lax.shift_right_arithmetic(child, 1)
    other = (own + 2 * (child & 1) - 1 + size) & (size - 1)
    wide = out_size // 2
    if wide < size:
        own = jnp.where(child >= out_size * 3 // 4, own + size - wide, own)
        other = (own + 2 * (child & 1) - 1 + size) & (size - 1)
    return (pick(parent == own, 0.75) + pick(parent == other, 0.25)).astype(BF16)


def xpack_kernel(mid, low, high, ylow, yhigh, window, to_left, to_right):
    for a in range(3):
        window[a * 24 : a * 24 + 8, 1:5] = low[a].reshape(8, 4, 8, 128)
        window[a * 24 + 8 : a * 24 + 16, 1:5] = mid[a].reshape(8, 4, 8, 128)
        window[a * 24 + 16 : a * 24 + 24, 1:5] = high[a].reshape(8, 4, 8, 128)
        window[a * 24 : a * 24 + 24, 0] = ylow[a]
        window[a * 24 : a * 24 + 24, 5] = yhigh[a]
    slot = lax.shift_right_logical(iota((8, 128), 1), 3)

    def group(i, carry):
        for packed in range(3):
            left = jnp.zeros((8, 128), F32)
            right = jnp.zeros((8, 128), F32)
            for s in range(16):
                j = packed * 16 + s
                tile = window[8 * i + j // 6, j % 6]
                left = jnp.where(slot == s, shift(tile, 8 * s, 1), left)
                right = jnp.where(slot == s, shift(tile, 8 * s + 8, 1), right)
            to_left[3 * i + packed] = left
            to_right[3 * i + packed] = right
        return carry

    loop(0, 9, group, 0)


def plane(ref, z):
    return ref[pl.ds(6 * z, 6)].reshape(48, 256)


def put(ref, z, value):
    ref[pl.ds(6 * z, 6)] = value.reshape(6, 8, 256)


def inner_flux(v, wx, wy):
    fx = wx * (ahead(v, 1) - v)
    fy = wy * (ahead(v, 0) - v)
    return (fx - behind(fx, 1)) + (fy - behind(fy, 0))


def sweep(first, last, source, wx, wy, wz, step):
    v = plane(source, first)
    carry = (v, plane(wz, first - 1) * (v - plane(source, first - 1)))

    def body(z, carry):
        v, below = carry
        after = plane(source, z + 1)
        above = plane(wz, z) * (after - v)
        step(z, v, inner_flux(v, plane(wx, z), plane(wy, z)) + (above - below))
        return (after, above)

    loop(first, last + 1, body, carry)


def zpair(low_face):
    pad = jnp.zeros((1,) + low_face.shape[1:], F32)
    return jnp.concatenate([low_face, pad], 0) - jnp.concatenate([pad, low_face], 0)


def middle_weights(kappa):
    half = 0.125 * kappa
    wx = half + ahead(half, 2)
    wy = half + ahead(half, 1)
    wz = half[:-1] + half[1:]
    pad = jnp.zeros((1,) + half.shape[1:], F32)
    diag = wx + behind(wx, 2) + wy + behind(wy, 1)
    diag = diag + jnp.concatenate([wz, pad], 0) + jnp.concatenate([pad, wz], 0)
    inside = kappa > 0.0
    inverse = jnp.where(inside, 1.0 / jnp.where(inside, diag, 1.0), 0.0)
    return wx, wy, wz, inverse


def middle_minus(v, weights):
    wx, wy, wz, _ = weights
    fx = wx * (ahead(v, 2) - v)
    fy = wy * (ahead(v, 1) - v)
    return (fx - behind(fx, 2)) + (fy - behind(fy, 1)) + zpair(wz * (v[1:] - v[:-1]))


def down_kernel(
    window, from_left, from_right,
    share, pair_out, k1_out, iterate, right, wx, wy, wz, inverse,
    kappa, guess, rest, update, second, sums_a, sums_b, line,
):
    lane = iota((8, 128), 1)

    def unpack(i, dest, base):
        for packed in range(3):
            hi = from_right[base * 9 + 3 * i + packed]
            lo = from_left[base * 9 + 3 * i + packed]
            for s in range(16):
                j = packed * 16 + s
                edge = jnp.where(lane < 8, shift(hi, -8 * s, 1), 0.0)
                edge = jnp.where(lane >= 120, shift(lo, 120 - 8 * s, 1), edge)
                dest[48 * i + j, :, 0:128] = window[base * 24 + 8 * i + j // 6, j % 6]
                dest[48 * i + j, :, 128:256] = edge

    def unpack_all(i, carry):
        unpack(i, guess, 0)
        unpack(i, right, 1)
        unpack(i, kappa, 2)
        return carry

    loop(0, 3, unpack_all, 0)

    def weights(z, carry):
        half, below = carry
        after = 0.5 * plane(kappa, z + 1)
        x = half + ahead(half, 1)
        y = half + ahead(half, 0)
        above = half + after
        diag = x + behind(x, 1) + y + behind(y, 0) + above + below
        inside = half > 0.0
        put(wx, z, x)
        put(wy, z, y)
        put(wz, z, above)
        put(inverse, z, jnp.where(inside, 1.0 / jnp.where(inside, diag, 1.0), 0.0))
        return (after, above)

    half0 = 0.5 * plane(kappa, 0)
    half1 = 0.5 * plane(kappa, 1)
    put(wz, 0, half0 + half1)
    loop(1, 23, weights, (half1, half0 + half1))

    def first(z, v, minus):
        r = plane(right, z) + minus
        put(rest, z, r)
        put(update, z, FIRST * r * plane(inverse, z))

    sweep(1, 22, guess, wx, wy, wz, first)

    def next_step(z, v, minus):
        r = plane(rest, z) + minus
        d = KEEP * v + GAIN * (r * plane(inverse, z))
        put(rest, z, r)
        put(second, z, d)
        put(iterate, z, plane(guess, z) + v + d)

    sweep(2, 21, update, wx, wy, wz, next_step)

    def last(z, v, minus):
        put(rest, z, plane(rest, z) + minus)

    sweep(3, 20, second, wx, wy, wz, last)

    def add_pairs(ref, start, count, at):
        def body(m, carry):
            pair = plane(ref, start + 2 * m) + plane(ref, start + 2 * m + 1)
            rows = pl.ds(pl.multiple_of((at + m) * 48, 48), 48)
            sums_a[rows, :] = pair[:, :128]
            sums_b[rows, :] = pair[:, 128:]
            return carry

        loop(0, count, body, 0)

    add_pairs(rest, 4, 8, 0)
    add_pairs(kappa, 0, 12, 8)

    def fold(ref):
        return ref[pl.ds(0, 480, stride=2), :] + ref[pl.ds(1, 480, stride=2), :]

    coarsen = pick(lax.shift_right_logical(iota((256, 128), 0), 1) == iota((256, 128), 1), 0.125)
    both = exact_dot(jnp.concatenate([fold(sums_a), fold(sums_b)], 1), coarsen.astype(BF16))
    both = both.reshape(20, 24, 128)
    kappa_one = both[8:]
    pad = jnp.zeros((2, 24, 128), F32)
    rhs = jnp.concatenate([pad, both[:8], pad], 0)
    weights_one = middle_weights(kappa_one)
    inverse_one = weights_one[3]
    d = FIRST * (rhs * inverse_one)
    r = rhs + middle_minus(d, weights_one)
    d2 = KEEP * d + GAIN * (r * inverse_one)
    r = r + middle_minus(d2, weights_one)
    wide = iota((12, 24, 128), 2)
    um = d + d2
    pair = jnp.where(wide < 64, um, shift(rhs, 64, 2))
    pair_out[...] = pair
    k1_out[...] = kappa_one

    cell = iota((128, 128), 0)
    place = iota((128, 128), 1)
    total = jnp.zeros((24, 128), F32)
    for q, field in enumerate((r[4] + r[5], r[6] + r[7], kappa_one[4] + kappa_one[5], kappa_one[6] + kappa_one[7])):
        to = (cell < 64) & (lax.shift_right_logical(cell, 1) + 32 * q == place)
        total = total + exact_dot(field, pick(to, 0.125).astype(BF16))
    line[...] = total
    cells = line[pl.ds(4, 8, stride=2), :] + line[pl.ds(5, 8, stride=2), :]
    cells = pltpu.roll(cells, 32 * lax.axis_index("gx"), 1)
    for slot in range(16):
        share[slot, 4] = cells
    gz = lax.axis_index("gz")
    for step, planes in ((1, (um[4], um[5], um[6], rhs[5])), (-1, (um[5], um[6], um[7], rhs[6]))):
        for k, value in enumerate(planes):
            rows = shift(value, -4, 0)
            share[(gz + step) & 15, k] = jnp.where(lane < 64, rows[:8], shift(rows[8:16], 64, 1))


def turn_kernel(gathered, pair, share, pair_out):
    lane = iota((8, 128), 1)
    row = iota((8, 128), 0)
    gy = lax.axis_index("gy")
    gz = lax.axis_index("gz")
    wide = iota((24, 128), 1)

    def spread(tile):
        value = jnp.concatenate([tile, shift(tile, 64, 1), jnp.zeros((8, 128), F32)], 0)
        return shift(value, 4, 0)

    planes = [pair[z] for z in range(12)]
    for step, first, where_rhs in ((-1, 0, 1), (1, 9, 10)):
        for k in range(3):
            planes[first + k] = jnp.where(wide < 64, spread(gathered[(gz + step) & 15, k]), planes[first + k])
        value = shift(spread(gathered[(gz + step) & 15, 3]), 64, 1)
        planes[where_rhs] = jnp.where(wide < 64, planes[where_rhs], value)
    for z in range(12):
        pair_out[z] = planes[z]
    for slot in range(8):
        for g in range(16):
            share[slot, 6 + g] = gathered[g, 4]
    for k in range(6):
        one, two = planes[2 * k], planes[2 * k + 1]
        share[(gy - 1) & 7, k] = jnp.where(row < 4, shift(one[0:8], 4, 0), two[0:8])
        share[(gy + 1) & 7, k] = jnp.where(row < 4, one[16:24], shift(two[16:24], 4, 0))


def cross_kernel(gathered, pair, share, pair_out):
    lane = iota((8, 128), 1)
    row = iota((8, 128), 0)
    slot_of = lax.shift_right_logical(lane, 3)
    gx = lax.axis_index("gx")
    gy = lax.axis_index("gy")
    tiles = []
    for k in range(6):
        low = gathered[(gy - 1) & 7, k]
        high = gathered[(gy + 1) & 7, k]
        for odd in range(2):
            value = pair[2 * k + odd]
            above = low if odd == 0 else shift(low, 4, 0)
            below = shift(high, 4, 0) if odd == 0 else high
            tiles.append(jnp.where(row < 4, above, value[0:8]))
            tiles.append(value[8:16])
            tiles.append(jnp.where(row < 4, value[16:24], below))
    for z in range(12):
        for t in range(3):
            pair_out[z, 8 * t : 8 * t + 8] = tiles[3 * z + t]
    for packed in range(3):
        left = jnp.zeros((8, 128), F32)
        right = jnp.zeros((8, 128), F32)
        for s, tile in enumerate(tiles[16 * packed : 16 * packed + 16]):
            here = slot_of == s
            first = (lane & 7) < 4
            left = jnp.where(here, jnp.where(first, shift(tile, 8 * s, 1), shift(tile, 8 * s - 60, 1)), left)
            right = jnp.where(here, jnp.where(first, shift(tile, 8 * s - 60, 1), shift(tile, 8 * s - 120, 1)), right)
        share[(gx - 1) & 3, packed] = left
        share[(gx + 1) & 3, packed] = right
    for slot in range(4):
        for g in range(8):
            share[slot, 3 + 16 * g : 19 + 16 * g] = gathered[g, 6:22]


def cplane(ref, z):
    return ref[pl.ds(8 * z, 8)].reshape(64, 128)


def cput(ref, z, value):
    ref[pl.ds(8 * z, 8)] = value.reshape(8, 8, 128)


def conjugate(gathered, kappa, wx, wy, wz, diag, rest, direction, image, answer):
    lane = iota((8, 128), 1)
    group = lax.shift_right_logical(lane, 5)
    nothing = jnp.zeros((64, 128), F32)
    for ref in (kappa, direction):
        cput(ref, 0, nothing)
        cput(ref, 33, nothing)
    cput(wz, 0, nothing)
    answer[...] = jnp.zeros_like(answer)

    def assemble(gz, carry):
        for gy in range(8):
            pieces = [gathered[gx, 3 + gy * 16 + gz] for gx in range(4)]
            for q in range(4):
                merged = pieces[0]
                for gx in range(1, 4):
                    merged = jnp.where(group == (q + gx) % 4, pieces[gx], merged)
                merged = shift(merged, -32 * q, 1)
                if q < 2:
                    rest[(2 * gz + q) * 8 + gy] = merged
                    direction[(2 * gz + q + 1) * 8 + gy] = merged
                else:
                    kappa[(2 * gz + q - 1) * 8 + gy] = merged
        return carry

    loop(0, 16, assemble, 0)
    inner_x = iota((64, 128), 1) < 127
    inner_y = iota((64, 128), 0) < 63
    first_x = iota((64, 128), 1) > 0
    first_y = iota((64, 128), 0) > 0

    def weights(z, total):
        half = 0.03125 * cplane(kappa, z + 1)
        before = 0.03125 * cplane(kappa, z)
        after = 0.03125 * cplane(kappa, z + 2)
        x = jnp.where(inner_x, ahead(half, 1), 0.0)
        y = jnp.where(inner_y, ahead(half, 0), 0.0)
        cput(wx, z, jnp.where(inner_x, half + x, 0.0))
        cput(wy, z, jnp.where(inner_y, half + y, 0.0))
        cput(wz, z + 1, half + after)
        x = x + jnp.where(first_x, behind(half, 1), 0.0)
        y = y + jnp.where(first_y, behind(half, 0), 0.0)
        cput(diag, z, 6.0 * half + x + y + (before + after))
        r = cplane(rest, z)
        return total + (r * r).reshape(8, 8, 128).sum(0)

    zero = jnp.zeros((8, 128), F32)

    def whole(total):
        return jnp.sum(jnp.sum(total, axis=0, keepdims=True), axis=1, keepdims=True)

    norm = whole(loop(0, 32, weights, zero))

    def apply(z, total):
        v = cplane(direction, z + 1)
        x = cplane(wx, z)
        y = cplane(wy, z)
        w = cplane(diag, z) * v
        w = w - (x * ahead(v, 1) + behind(x * v, 1))
        w = w - (y * ahead(v, 0) + behind(y * v, 0))
        w = w - (cplane(wz, z + 1) * cplane(direction, z + 2) + cplane(wz, z) * cplane(direction, z))
        cput(image, z, w)
        return total + (v * w).reshape(8, 8, 128).sum(0)

    def add_answer(z, alpha):
        at = pl.ds((z + 3) * 10 + 1, 8)
        answer[at] = answer[at] + (alpha * cplane(direction, z + 1)).reshape(8, 8, 128)

    for repeat in range(ITERS):
        alpha = norm / whole(loop(0, 32, apply, zero))
        if repeat + 1 < ITERS:

            def step(z, total):
                add_answer(z, alpha)
                r = cplane(rest, z) - alpha * cplane(image, z)
                cput(rest, z, r)
                return total + (r * r).reshape(8, 8, 128).sum(0)

            norm_next = whole(loop(0, 32, step, zero))
            beta = norm_next / norm

            def turn(z, carry):
                cput(direction, z + 1, cplane(rest, z) + beta * cplane(direction, z + 1))
                return carry

            loop(0, 32, turn, 0)
            norm = norm_next
        else:

            def finish(z, carry):
                add_answer(z, alpha)
                return carry

            loop(0, 32, finish, 0)

    gx = lax.axis_index("gx")
    gy = lax.axis_index("gy")
    gz = lax.axis_index("gz")
    wide = iota((24, 128), 1)
    position = jnp.where(wide < 64, wide, wide - 128) + 32 * gx
    known = (position >= 0) & (position < 128)
    planes = []
    for z in range(8):
        block = answer[pl.ds((2 * gz + z) * 10 + gy, 3)].reshape(24, 128)
        planes.append(jnp.where(known, pltpu.roll(block, (128 - 32 * gx) & 127, 1), 0.0))
    return jnp.stack(planes)


def middle_fields(gathered, pair):
    lane = iota((8, 128), 1)
    gx = lax.axis_index("gx")
    both = [[], []]
    for v in range(36):
        packed, s = v // 16, v % 16
        low = gathered[(gx - 1) & 3, packed]
        high = gathered[(gx + 1) & 3, packed]
        tile = pair[v // 3, 8 * (v % 3) : 8 * (v % 3) + 8]
        for k in range(2):
            own = shift(tile, 64 * k, 1) if k else tile
            edge = jnp.where(lane < 68, shift(high, 64 - 8 * s - 4 * k, 1), shift(low, 124 - 8 * s - 4 * k, 1))
            both[k].append(jnp.where(lane < 64, own, edge))
    return [jnp.stack(tiles).reshape(12, 24, 128) for tiles in both]


def up_kernel(
    gathered, pair, k1, iterate, right, wx, wy, wz, inverse,
    solution_out, residual_out,
    line, fine_a, fine_b, current, rest, update, second, *grids,
):
    c = conjugate(gathered, *grids)
    um, mr = middle_fields(gathered, pair)
    even = 0.75 * c[1:7] + 0.25 * c[0:6]
    odd = 0.75 * c[1:7] + 0.25 * c[2:8]
    c = jnp.stack([even, odd], 1).reshape(12, 24, 128)
    matrix = refine_matrix(128, 128)
    line[pl.ds(0, 288, stride=2), :] = exact_dot((0.75 * c + 0.25 * behind(c, 1)).reshape(288, 128), matrix)
    line[pl.ds(1, 288, stride=2), :] = exact_dot((0.75 * c + 0.25 * ahead(c, 1)).reshape(288, 128), matrix)
    correction = shift(line[...].reshape(12, 48, 128), -12, 1)[:, :24]

    kappa_one = k1[...]
    weights = middle_weights(kappa_one)
    inverse_one = weights[3]
    u = jnp.where(kappa_one > 0.0, um + correction, 0.0)
    r = mr + middle_minus(u, weights)
    d = FIRST * (r * inverse_one)
    u = u + d
    r = r + middle_minus(d, weights)
    u = u + (KEEP * d + GAIN * (r * inverse_one))

    even = 0.75 * u[2:10] + 0.25 * u[1:9]
    odd = 0.75 * u[2:10] + 0.25 * u[3:11]
    m = jnp.stack([even, odd], 1).reshape(16, 24, 128)
    matrix = refine_matrix(128, 256)
    for parity, near in enumerate((behind(m, 1), ahead(m, 1))):
        value = exact_dot((0.75 * m + 0.25 * near).reshape(384, 128), matrix)
        fine_a[pl.ds(parity, 384, stride=2), :] = value[:, :128]
        fine_b[pl.ds(parity, 384, stride=2), :] = value[:, 128:]

    def begin(z, carry):
        rows = pl.ds(pl.multiple_of((z - 4) * 48, 48), 48)
        fine = jnp.concatenate([fine_a[rows, :], fine_b[rows, :]], 1)
        put(current, z, jnp.where(plane(inverse, z) > 0.0, plane(iterate, z) + fine, 0.0))
        return carry

    loop(4, 20, begin, 0)

    def first(z, v, minus):
        r = plane(right, z) + minus
        put(rest, z, r)
        put(update, z, FIRST * r * plane(inverse, z))

    sweep(5, 18, current, wx, wy, wz, first)

    def next_step(z, v, minus):
        r = plane(rest, z) + minus
        d = KEEP * v + GAIN * (r * plane(inverse, z))
        put(rest, z, r)
        put(second, z, d)
        put(current, z, plane(current, z) + v + d)

    sweep(6, 17, update, wx, wy, wz, next_step)

    def last(z, v, minus):
        residual_out[z - 8] = (plane(rest, z) + minus)[8:40, :128]
        solution_out[z - 8] = plane(current, z)[8:40, :128]

    sweep(8, 15, second, wx, wy, wz, last)


def run(kernel, outs, scratch, *args):
    return pl.pallas_call(
        kernel,
        out_shape=[jax.ShapeDtypeStruct(shape, F32) for shape in outs],
        in_specs=[VMEM] * len(args),
        out_specs=[VMEM] * len(outs),
        scratch_shapes=[pltpu.VMEM(shape, F32) for shape in scratch],
        compiler_params=pltpu.CompilerParams(vmem_limit_bytes=LIMIT),
    )(*args)


FINE = (144, 8, 256)
MIDDLE = (12, 24, 128)
COARSE = (256, 8, 128)
PADDED = (272, 8, 128)
XPACK = ([(72, 6, 8, 128), (27, 8, 128), (27, 8, 128)], [])
DOWN = ([(16, 5, 8, 128), MIDDLE, MIDDLE] + [FINE] * 6, [FINE] * 5 + [(960, 128)] * 2 + [(24, 128)])
TURN = ([(8, 22, 8, 128), MIDDLE], [])
CROSS = ([(4, 131, 8, 128), MIDDLE], [])
UP = (
    [(8, 32, 128)] * 2,
    [(576, 128)] + [(768, 128)] * 2 + [FINE] * 4
    + [PADDED] + [COARSE] * 2 + [PADDED] + [COARSE] * 2 + [PADDED, COARSE, (380, 8, 128)],
)


def up(axis):
    return [(i, i + 1) for i in range(lax.axis_size(axis) - 1)]


def down(axis):
    return [(i + 1, i) for i in range(lax.axis_size(axis) - 1)]


def both_ways(to_low, to_high, axis):
    return lax.ppermute(to_high, axis, up(axis)), lax.ppermute(to_low, axis, down(axis))


def local(right_side, guess, coefficient):
    mine = jnp.stack([guess, right_side, coefficient])
    low, high = both_ways(mine, mine, "gz")
    column = jnp.concatenate([low, mine, high], 1)
    ylow, yhigh = both_ways(column[:, :, :8], column[:, :, 24:], "gy")
    window, to_left, to_right = run(
        xpack_kernel, *XPACK, mine, low, high, ylow, yhigh
    )
    from_left, from_right = both_ways(to_left, to_right, "gx")

    share, pair, k1, *arrays = run(down_kernel, *DOWN, window, from_left, from_right)
    share, pair = run(turn_kernel, *TURN, lax.all_to_all(share, "gz", 0, 0), pair)
    share, pair = run(cross_kernel, *CROSS, lax.all_to_all(share, "gy", 0, 0), pair)
    return run(up_kernel, *UP, lax.all_to_all(share, "gx", 0, 0), pair, k1, *arrays)


def solution(mesh):
    spec = P("gz", "gy", "gx")
    return jax.shard_map(
        local, mesh=mesh, in_specs=(spec, spec, spec), out_specs=(spec, spec), check_vma=False
    )
```

```python
import jax
import jax.numpy as jnp
from jax import lax
from jax.experimental import pallas as pl
from jax.experimental.pallas import tpu as pltpu
from jax.sharding import PartitionSpec as P


ITERS = 6
THETA = 1.25
DELTA = 0.75
SIGMA = THETA / DELTA
RHO = 1.0 / SIGMA
RHO_NEXT = 1.0 / (2.0 * SIGMA - RHO)
FIRST = 1.0 / THETA
KEEP = RHO_NEXT * RHO
GAIN = 2.0 * RHO_NEXT / DELTA

F32 = jnp.float32
BF16 = jnp.bfloat16
VMEM = pl.BlockSpec(memory_space=pltpu.VMEM)
LIMIT = 20 * 1024 * 1024


def loop(first, end, body, carry, unroll=8):
    count = end - first
    while count % unroll:
        unroll -= 1

    def several(i, carry):
        for k in range(unroll):
            carry = body(first + i * unroll + k, carry)
        return carry

    return lax.fori_loop(0, count // unroll, several, carry)


def shift(value, by, axis):
    return pltpu.roll(value, by % value.shape[axis], axis)


def ahead(value, axis):
    return shift(value, -1, axis)


def behind(value, axis):
    return shift(value, 1, axis)


def iota(shape, axis):
    return lax.broadcasted_iota(jnp.int32, shape, axis)


def exact_dot(value, matrix):
    high = value.astype(BF16)
    rest = value - high.astype(F32)
    middle = rest.astype(BF16)
    low = (rest - middle.astype(F32)).astype(BF16)
    parts = [jnp.dot(part, matrix, preferred_element_type=F32) for part in (low, middle, high)]
    return parts[0] + parts[1] + parts[2]


def pick(condition, number):
    return jnp.where(condition, jnp.float32(number), jnp.float32(0.0))


def refine_matrix(size, out_size):
    parent = iota((size, out_size), 0)
    child = iota((size, out_size), 1)
    own = lax.shift_right_arithmetic(child, 1)
    other = (own + 2 * (child & 1) - 1 + size) & (size - 1)
    wide = out_size // 2
    if wide < size:
        own = jnp.where(child >= out_size * 3 // 4, own + size - wide, own)
        other = (own + 2 * (child & 1) - 1 + size) & (size - 1)
    return (pick(parent == own, 0.75) + pick(parent == other, 0.25)).astype(BF16)


def xpack_kernel(mid, low, high, ylow, yhigh, window, to_left, to_right):
    for a in range(3):
        window[a * 24 : a * 24 + 8, 1:5] = low[a].reshape(8, 4, 8, 128)
        window[a * 24 + 8 : a * 24 + 16, 1:5] = mid[a].reshape(8, 4, 8, 128)
        window[a * 24 + 16 : a * 24 + 24, 1:5] = high[a].reshape(8, 4, 8, 128)
        window[a * 24 : a * 24 + 24, 0] = ylow[a]
        window[a * 24 : a * 24 + 24, 5] = yhigh[a]
    slot = lax.shift_right_logical(iota((8, 128), 1), 3)

    def group(i, carry):
        for packed in range(3):
            left = jnp.zeros((8, 128), F32)
            right = jnp.zeros((8, 128), F32)
            for s in range(16):
                j = packed * 16 + s
                tile = window[8 * i + j // 6, j % 6]
                left = jnp.where(slot == s, shift(tile, 8 * s, 1), left)
                right = jnp.where(slot == s, shift(tile, 8 * s + 8, 1), right)
            to_left[3 * i + packed] = left
            to_right[3 * i + packed] = right
        return carry

    loop(0, 9, group, 0)


def plane(ref, z):
    return ref[pl.ds(6 * z, 6)].reshape(48, 256)


def put(ref, z, value):
    ref[pl.ds(6 * z, 6)] = value.reshape(6, 8, 256)


def inner_flux(v, wx, wy):
    fx = wx * (ahead(v, 1) - v)
    fy = wy * (ahead(v, 0) - v)
    return (fx - behind(fx, 1)) + (fy - behind(fy, 0))


def sweep(first, last, source, wx, wy, wz, step):
    v = plane(source, first)
    carry = (v, plane(wz, first - 1) * (v - plane(source, first - 1)))

    def body(z, carry):
        v, below = carry
        after = plane(source, z + 1)
        above = plane(wz, z) * (after - v)
        step(z, v, inner_flux(v, plane(wx, z), plane(wy, z)) + (above - below))
        return (after, above)

    loop(first, last + 1, body, carry)


def zpair(low_face):
    pad = jnp.zeros((1,) + low_face.shape[1:], F32)
    return jnp.concatenate([low_face, pad], 0) - jnp.concatenate([pad, low_face], 0)


def middle_weights(kappa):
    half = 0.125 * kappa
    wx = half + ahead(half, 2)
    wy = half + ahead(half, 1)
    wz = half[:-1] + half[1:]
    pad = jnp.zeros((1,) + half.shape[1:], F32)
    diag = wx + behind(wx, 2) + wy + behind(wy, 1)
    diag = diag + jnp.concatenate([wz, pad], 0) + jnp.concatenate([pad, wz], 0)
    inside = kappa > 0.0
    inverse = jnp.where(inside, 1.0 / jnp.where(inside, diag, 1.0), 0.0)
    return wx, wy, wz, inverse


def middle_minus(v, weights):
    wx, wy, wz, _ = weights
    fx = wx * (ahead(v, 2) - v)
    fy = wy * (ahead(v, 1) - v)
    return (fx - behind(fx, 2)) + (fy - behind(fy, 1)) + zpair(wz * (v[1:] - v[:-1]))


def down_kernel(
    window, from_left, from_right,
    share, pair_out, k1_out, iterate, right, wx, wy, wz, inverse,
    kappa, guess, rest, update, second, sums_a, sums_b, line,
):
    lane = iota((8, 128), 1)

    def unpack(i, dest, base):
        for packed in range(3):
            hi = from_right[base * 9 + 3 * i + packed]
            lo = from_left[base * 9 + 3 * i + packed]
            for s in range(16):
                j = packed * 16 + s
                edge = jnp.where(lane < 8, shift(hi, -8 * s, 1), 0.0)
                edge = jnp.where(lane >= 120, shift(lo, 120 - 8 * s, 1), edge)
                dest[48 * i + j, :, 0:128] = window[base * 24 + 8 * i + j // 6, j % 6]
                dest[48 * i + j, :, 128:256] = edge

    def unpack_all(i, carry):
        unpack(i, guess, 0)
        unpack(i, right, 1)
        unpack(i, kappa, 2)
        return carry

    loop(0, 3, unpack_all, 0)

    def weights(z, carry):
        half, below = carry
        after = 0.5 * plane(kappa, z + 1)
        x = half + ahead(half, 1)
        y = half + ahead(half, 0)
        above = half + after
        diag = x + behind(x, 1) + y + behind(y, 0) + above + below
        inside = half > 0.0
        put(wx, z, x)
        put(wy, z, y)
        put(wz, z, above)
        put(inverse, z, jnp.where(inside, 1.0 / jnp.where(inside, diag, 1.0), 0.0))
        return (after, above)

    half0 = 0.5 * plane(kappa, 0)
    half1 = 0.5 * plane(kappa, 1)
    put(wz, 0, half0 + half1)
    loop(1, 23, weights, (half1, half0 + half1))

    def first(z, v, minus):
        r = plane(right, z) + minus
        put(rest, z, r)
        put(update, z, FIRST * r * plane(inverse, z))

    sweep(1, 22, guess, wx, wy, wz, first)

    def next_step(z, v, minus):
        r = plane(rest, z) + minus
        d = KEEP * v + GAIN * (r * plane(inverse, z))
        put(rest, z, r)
        put(second, z, d)
        put(iterate, z, plane(guess, z) + v + d)

    sweep(2, 21, update, wx, wy, wz, next_step)

    def last(z, v, minus):
        put(rest, z, plane(rest, z) + minus)

    sweep(3, 20, second, wx, wy, wz, last)

    def add_pairs(ref, start, count, at):
        def body(m, carry):
            pair = plane(ref, start + 2 * m) + plane(ref, start + 2 * m + 1)
            rows = pl.ds(pl.multiple_of((at + m) * 48, 48), 48)
            sums_a[rows, :] = pair[:, :128]
            sums_b[rows, :] = pair[:, 128:]
            return carry

        loop(0, count, body, 0)

    add_pairs(rest, 4, 8, 0)
    add_pairs(kappa, 0, 12, 8)

    def fold(ref):
        return ref[pl.ds(0, 480, stride=2), :] + ref[pl.ds(1, 480, stride=2), :]

    coarsen = pick(lax.shift_right_logical(iota((256, 128), 0), 1) == iota((256, 128), 1), 0.125)
    both = exact_dot(jnp.concatenate([fold(sums_a), fold(sums_b)], 1), coarsen.astype(BF16))
    both = both.reshape(20, 24, 128)
    kappa_one = both[8:]
    pad = jnp.zeros((2, 24, 128), F32)
    rhs = jnp.concatenate([pad, both[:8], pad], 0)
    weights_one = middle_weights(kappa_one)
    inverse_one = weights_one[3]
    d = FIRST * (rhs * inverse_one)
    r = rhs + middle_minus(d, weights_one)
    d2 = KEEP * d + GAIN * (r * inverse_one)
    r = r + middle_minus(d2, weights_one)
    wide = iota((12, 24, 128), 2)
    um = d + d2
    pair = jnp.where(wide < 64, um, shift(rhs, 64, 2))
    pair_out[...] = pair
    k1_out[...] = kappa_one

    cell = iota((128, 128), 0)
    place = iota((128, 128), 1)
    total = jnp.zeros((24, 128), F32)
    for q, field in enumerate((r[4] + r[5], r[6] + r[7], kappa_one[4] + kappa_one[5], kappa_one[6] + kappa_one[7])):
        to = (cell < 64) & (lax.shift_right_logical(cell, 1) + 32 * q == place)
        total = total + exact_dot(field, pick(to, 0.125).astype(BF16))
    line[...] = total
    cells = line[pl.ds(4, 8, stride=2), :] + line[pl.ds(5, 8, stride=2), :]
    cells = pltpu.roll(cells, 32 * lax.axis_index("gx"), 1)
    for slot in range(16):
        share[slot, 4] = cells
    gz = lax.axis_index("gz")
    for step, planes in ((1, (um[4], um[5], um[6], rhs[5])), (-1, (um[5], um[6], um[7], rhs[6]))):
        for k, value in enumerate(planes):
            rows = shift(value, -4, 0)
            share[(gz + step) & 15, k] = jnp.where(lane < 64, rows[:8], shift(rows[8:16], 64, 1))


def turn_kernel(gathered, pair, share, pair_out):
    lane = iota((8, 128), 1)
    row = iota((8, 128), 0)
    gy = lax.axis_index("gy")
    gz = lax.axis_index("gz")
    wide = iota((24, 128), 1)

    def spread(tile):
        value = jnp.concatenate([tile, shift(tile, 64, 1), jnp.zeros((8, 128), F32)], 0)
        return shift(value, 4, 0)

    planes = [pair[z] for z in range(12)]
    for step, first, where_rhs in ((-1, 0, 1), (1, 9, 10)):
        for k in range(3):
            planes[first + k] = jnp.where(wide < 64, spread(gathered[(gz + step) & 15, k]), planes[first + k])
        value = shift(spread(gathered[(gz + step) & 15, 3]), 64, 1)
        planes[where_rhs] = jnp.where(wide < 64, planes[where_rhs], value)
    for z in range(12):
        pair_out[z] = planes[z]
    for g in range(8):
        piece = gathered[2 * g + (gz & 1), 4]
        for slot in range(8):
            share[slot, 6 + g] = piece
    for k in range(6):
        one, two = planes[2 * k], planes[2 * k + 1]
        share[(gy - 1) & 7, k] = jnp.where(row < 4, shift(one[0:8], 4, 0), two[0:8])
        share[(gy + 1) & 7, k] = jnp.where(row < 4, one[16:24], shift(two[16:24], 4, 0))


def cross_kernel(gathered, pair, share, pair_out):
    lane = iota((8, 128), 1)
    row = iota((8, 128), 0)
    slot_of = lax.shift_right_logical(lane, 3)
    gx = lax.axis_index("gx")
    gy = lax.axis_index("gy")
    tiles = []
    for k in range(6):
        low = gathered[(gy - 1) & 7, k]
        high = gathered[(gy + 1) & 7, k]
        for odd in range(2):
            value = pair[2 * k + odd]
            above = low if odd == 0 else shift(low, 4, 0)
            below = shift(high, 4, 0) if odd == 0 else high
            tiles.append(jnp.where(row < 4, above, value[0:8]))
            tiles.append(value[8:16])
            tiles.append(jnp.where(row < 4, value[16:24], below))
    for z in range(12):
        for t in range(3):
            pair_out[z, 8 * t : 8 * t + 8] = tiles[3 * z + t]
    for packed in range(3):
        left = jnp.zeros((8, 128), F32)
        right = jnp.zeros((8, 128), F32)
        for s, tile in enumerate(tiles[16 * packed : 16 * packed + 16]):
            here = slot_of == s
            first = (lane & 7) < 4
            left = jnp.where(here, jnp.where(first, shift(tile, 8 * s, 1), shift(tile, 8 * s - 60, 1)), left)
            right = jnp.where(here, jnp.where(first, shift(tile, 8 * s - 60, 1), shift(tile, 8 * s - 120, 1)), right)
        share[(gx - 1) & 3, packed] = left
        share[(gx + 1) & 3, packed] = right
    for slot in range(4):
        for g in range(8):
            share[slot, 3 + 8 * g : 11 + 8 * g] = gathered[g, 6:14]


def cplane(ref, z):
    return ref[pl.ds(8 * z, 8)].reshape(64, 128)


def cput(ref, z, value):
    ref[pl.ds(8 * z, 8)] = value.reshape(8, 8, 128)


def conjugate(gathered, other, kappa, wx, wy, wz, diag, rest, direction, image, answer):
    lane = iota((8, 128), 1)
    group = lax.shift_right_logical(lane, 5)
    nothing = jnp.zeros((64, 128), F32)
    for ref in (kappa, direction):
        cput(ref, 0, nothing)
        cput(ref, 33, nothing)
    cput(wz, 0, nothing)
    answer[...] = jnp.zeros_like(answer)

    for source, parity in ((gathered, lax.axis_index("gz") & 1), (other, 1 - (lax.axis_index("gz") & 1))):

        def assemble(g, carry):
            gz = 2 * g + parity
            for gy in range(8):
                pieces = [source[gx, 3 + gy * 8 + g] for gx in range(4)]
                for q in range(4):
                    merged = pieces[0]
                    for gx in range(1, 4):
                        merged = jnp.where(group == (q + gx) % 4, pieces[gx], merged)
                    merged = shift(merged, -32 * q, 1)
                    if q < 2:
                        rest[(2 * gz + q) * 8 + gy] = merged
                        direction[(2 * gz + q + 1) * 8 + gy] = merged
                    else:
                        kappa[(2 * gz + q - 1) * 8 + gy] = merged
            return carry

        loop(0, 8, assemble, 0, 2)
    inner_x = iota((64, 128), 1) < 127
    inner_y = iota((64, 128), 0) < 63
    first_x = iota((64, 128), 1) > 0
    first_y = iota((64, 128), 0) > 0

    def weights(z, total):
        half = 0.03125 * cplane(kappa, z + 1)
        before = 0.03125 * cplane(kappa, z)
        after = 0.03125 * cplane(kappa, z + 2)
        x = jnp.where(inner_x, ahead(half, 1), 0.0)
        y = jnp.where(inner_y, ahead(half, 0), 0.0)
        cput(wx, z, jnp.where(inner_x, half + x, 0.0))
        cput(wy, z, jnp.where(inner_y, half + y, 0.0))
        cput(wz, z + 1, half + after)
        x = x + jnp.where(first_x, behind(half, 1), 0.0)
        y = y + jnp.where(first_y, behind(half, 0), 0.0)
        cput(diag, z, 6.0 * half + x + y + (before + after))
        r = cplane(rest, z)
        return total + (r * r).reshape(8, 8, 128).sum(0)

    zero = jnp.zeros((8, 128), F32)

    def whole(total):
        return jnp.sum(jnp.sum(total, axis=0, keepdims=True), axis=1, keepdims=True)

    norm = whole(loop(0, 32, weights, zero))

    def apply(z, total):
        v = cplane(direction, z + 1)
        x = cplane(wx, z)
        y = cplane(wy, z)
        w = cplane(diag, z) * v
        w = w - (x * ahead(v, 1) + behind(x * v, 1))
        w = w - (y * ahead(v, 0) + behind(y * v, 0))
        w = w - (cplane(wz, z + 1) * cplane(direction, z + 2) + cplane(wz, z) * cplane(direction, z))
        cput(image, z, w)
        return total + (v * w).reshape(8, 8, 128).sum(0)

    def add_answer(z, alpha):
        at = pl.ds((z + 3) * 10 + 1, 8)
        answer[at] = answer[at] + (alpha * cplane(direction, z + 1)).reshape(8, 8, 128)

    for repeat in range(ITERS):
        alpha = norm / whole(loop(0, 32, apply, zero))
        if repeat + 1 < ITERS:

            def step(z, total):
                add_answer(z, alpha)
                r = cplane(rest, z) - alpha * cplane(image, z)
                cput(rest, z, r)
                return total + (r * r).reshape(8, 8, 128).sum(0)

            norm_next = whole(loop(0, 32, step, zero))
            beta = norm_next / norm

            def turn(z, carry):
                cput(direction, z + 1, cplane(rest, z) + beta * cplane(direction, z + 1))
                return carry

            loop(0, 32, turn, 0)
            norm = norm_next
        else:

            def finish(z, carry):
                add_answer(z, alpha)
                return carry

            loop(0, 32, finish, 0)

    gx = lax.axis_index("gx")
    gy = lax.axis_index("gy")
    gz = lax.axis_index("gz")
    wide = iota((24, 128), 1)
    position = jnp.where(wide < 64, wide, wide - 128) + 32 * gx
    known = (position >= 0) & (position < 128)
    planes = []
    for z in range(8):
        block = answer[pl.ds((2 * gz + z) * 10 + gy, 3)].reshape(24, 128)
        planes.append(jnp.where(known, pltpu.roll(block, (128 - 32 * gx) & 127, 1), 0.0))
    return jnp.stack(planes)


def middle_fields(gathered, pair):
    lane = iota((8, 128), 1)
    gx = lax.axis_index("gx")
    both = [[], []]
    for v in range(36):
        packed, s = v // 16, v % 16
        low = gathered[(gx - 1) & 3, packed]
        high = gathered[(gx + 1) & 3, packed]
        tile = pair[v // 3, 8 * (v % 3) : 8 * (v % 3) + 8]
        for k in range(2):
            own = shift(tile, 64 * k, 1) if k else tile
            edge = jnp.where(lane < 68, shift(high, 64 - 8 * s - 4 * k, 1), shift(low, 124 - 8 * s - 4 * k, 1))
            both[k].append(jnp.where(lane < 64, own, edge))
    return [jnp.stack(tiles).reshape(12, 24, 128) for tiles in both]


def up_kernel(
    gathered, other, pair, k1, iterate, right, wx, wy, wz, inverse,
    solution_out, residual_out,
    line, fine_a, fine_b, current, rest, update, second, *grids,
):
    c = conjugate(gathered, other, *grids)
    um, mr = middle_fields(gathered, pair)
    even = 0.75 * c[1:7] + 0.25 * c[0:6]
    odd = 0.75 * c[1:7] + 0.25 * c[2:8]
    c = jnp.stack([even, odd], 1).reshape(12, 24, 128)
    matrix = refine_matrix(128, 128)
    line[pl.ds(0, 288, stride=2), :] = exact_dot((0.75 * c + 0.25 * behind(c, 1)).reshape(288, 128), matrix)
    line[pl.ds(1, 288, stride=2), :] = exact_dot((0.75 * c + 0.25 * ahead(c, 1)).reshape(288, 128), matrix)
    correction = shift(line[...].reshape(12, 48, 128), -12, 1)[:, :24]

    kappa_one = k1[...]
    weights = middle_weights(kappa_one)
    inverse_one = weights[3]
    u = jnp.where(kappa_one > 0.0, um + correction, 0.0)
    r = mr + middle_minus(u, weights)
    d = FIRST * (r * inverse_one)
    u = u + d
    r = r + middle_minus(d, weights)
    u = u + (KEEP * d + GAIN * (r * inverse_one))

    even = 0.75 * u[2:10] + 0.25 * u[1:9]
    odd = 0.75 * u[2:10] + 0.25 * u[3:11]
    m = jnp.stack([even, odd], 1).reshape(16, 24, 128)
    matrix = refine_matrix(128, 256)
    for parity, near in enumerate((behind(m, 1), ahead(m, 1))):
        value = exact_dot((0.75 * m + 0.25 * near).reshape(384, 128), matrix)
        fine_a[pl.ds(parity, 384, stride=2), :] = value[:, :128]
        fine_b[pl.ds(parity, 384, stride=2), :] = value[:, 128:]

    def begin(z, carry):
        rows = pl.ds(pl.multiple_of((z - 4) * 48, 48), 48)
        fine = jnp.concatenate([fine_a[rows, :], fine_b[rows, :]], 1)
        put(current, z, jnp.where(plane(inverse, z) > 0.0, plane(iterate, z) + fine, 0.0))
        return carry

    loop(4, 20, begin, 0)

    def first(z, v, minus):
        r = plane(right, z) + minus
        put(rest, z, r)
        put(update, z, FIRST * r * plane(inverse, z))

    sweep(5, 18, current, wx, wy, wz, first)

    def next_step(z, v, minus):
        r = plane(rest, z) + minus
        d = KEEP * v + GAIN * (r * plane(inverse, z))
        put(rest, z, r)
        put(second, z, d)
        put(current, z, plane(current, z) + v + d)

    sweep(6, 17, update, wx, wy, wz, next_step)

    def last(z, v, minus):
        residual_out[z - 8] = (plane(rest, z) + minus)[8:40, :128]
        solution_out[z - 8] = plane(current, z)[8:40, :128]

    sweep(8, 15, second, wx, wy, wz, last)


def run(kernel, outs, scratch, *args):
    return pl.pallas_call(
        kernel,
        out_shape=[jax.ShapeDtypeStruct(shape, F32) for shape in outs],
        in_specs=[VMEM] * len(args),
        out_specs=[VMEM] * len(outs),
        scratch_shapes=[pltpu.VMEM(shape, F32) for shape in scratch],
        compiler_params=pltpu.CompilerParams(vmem_limit_bytes=LIMIT),
    )(*args)


FINE = (144, 8, 256)
MIDDLE = (12, 24, 128)
COARSE = (256, 8, 128)
PADDED = (272, 8, 128)
XPACK = ([(72, 6, 8, 128), (27, 8, 128), (27, 8, 128)], [])
DOWN = ([(16, 5, 8, 128), MIDDLE, MIDDLE] + [FINE] * 6, [FINE] * 5 + [(960, 128)] * 2 + [(24, 128)])
TURN = ([(8, 14, 8, 128), MIDDLE], [])
CROSS = ([(4, 67, 8, 128), MIDDLE], [])
UP = (
    [(8, 32, 128)] * 2,
    [(576, 128)] + [(768, 128)] * 2 + [FINE] * 4
    + [PADDED] + [COARSE] * 2 + [PADDED] + [COARSE] * 2 + [PADDED, COARSE, (380, 8, 128)],
)


def up(axis):
    return [(i, i + 1) for i in range(lax.axis_size(axis) - 1)]


def down(axis):
    return [(i + 1, i) for i in range(lax.axis_size(axis) - 1)]


def both_ways(to_low, to_high, axis):
    return lax.ppermute(to_high, axis, up(axis)), lax.ppermute(to_low, axis, down(axis))


def local(right_side, guess, coefficient):
    mine = jnp.stack([guess, right_side, coefficient])
    low, high = both_ways(mine, mine, "gz")
    column = jnp.concatenate([low, mine, high], 1)
    ylow, yhigh = both_ways(column[:, :, :8], column[:, :, 24:], "gy")
    window, to_left, to_right = run(
        xpack_kernel, *XPACK, mine, low, high, ylow, yhigh
    )
    from_left, from_right = both_ways(to_left, to_right, "gx")

    share, pair, k1, *arrays = run(down_kernel, *DOWN, window, from_left, from_right)
    share, pair = run(turn_kernel, *TURN, lax.all_to_all(share, "gz", 0, 0), pair)
    share, pair = run(cross_kernel, *CROSS, lax.all_to_all(share, "gy", 0, 0), pair)
    whole = lax.all_to_all(share, "gx", 0, 0)
    other = lax.ppermute(whole, "gz", [(i, i ^ 1) for i in range(16)])
    return run(up_kernel, *UP, whole, other, pair, k1, *arrays)


def solution(mesh):
    spec = P("gz", "gy", "gx")
    return jax.shard_map(
        local, mesh=mesh, in_specs=(spec, spec, spec), out_specs=(spec, spec), check_vma=False
    )
```

```python
import jax
import jax.numpy as jnp
from jax import lax
from jax.experimental import pallas as pl
from jax.experimental.pallas import tpu as pltpu
from jax.sharding import PartitionSpec as P


ITERS = 6
THETA = 1.25
DELTA = 0.75
SIGMA = THETA / DELTA
RHO = 1.0 / SIGMA
RHO_NEXT = 1.0 / (2.0 * SIGMA - RHO)
FIRST = 1.0 / THETA
KEEP = RHO_NEXT * RHO
GAIN = 2.0 * RHO_NEXT / DELTA

INNER = 16
OUTER = 16
F32 = jnp.float32
BF16 = jnp.bfloat16
VMEM = pl.BlockSpec(memory_space=pltpu.VMEM)
LIMIT = 20 * 1024 * 1024


def loop(first, end, body, carry, unroll=16):
    count = end - first
    while count % unroll:
        unroll -= 1

    def several(i, carry):
        for k in range(unroll):
            carry = body(first + i * unroll + k, carry)
        return carry

    return lax.fori_loop(0, count // unroll, several, carry)


def shift(value, by, axis):
    return pltpu.roll(value, by % value.shape[axis], axis)


def ahead(value, axis):
    return shift(value, -1, axis)


def behind(value, axis):
    return shift(value, 1, axis)


def iota(shape, axis):
    return lax.broadcasted_iota(jnp.int32, shape, axis)


def exact_dot(value, matrix):
    high = value.astype(BF16)
    rest = value - high.astype(F32)
    middle = rest.astype(BF16)
    low = (rest - middle.astype(F32)).astype(BF16)
    parts = [jnp.dot(part, matrix, preferred_element_type=F32) for part in (low, middle, high)]
    return parts[0] + parts[1] + parts[2]


def pick(condition, number):
    return jnp.where(condition, jnp.float32(number), jnp.float32(0.0))


def reciprocal(value):
    guess = pl.reciprocal(value, approx=True)
    for _ in range(2):
        guess = guess * (2.0 - value * guess)
    return guess


def refine_matrix(size, out_size):
    parent = iota((size, out_size), 0)
    child = iota((size, out_size), 1)
    own = lax.shift_right_arithmetic(child, 1)
    other = (own + 2 * (child & 1) - 1 + size) & (size - 1)
    wide = out_size // 2
    if wide < size:
        own = jnp.where(child >= out_size * 3 // 4, own + size - wide, own)
        other = (own + 2 * (child & 1) - 1 + size) & (size - 1)
    return (pick(parent == own, 0.75) + pick(parent == other, 0.25)).astype(BF16)


def ypack_kernel(mid, low, high, to_low, to_high):
    for part, ref in enumerate((low, mid, high)):
        to_low[:, 8 * part : 8 * part + 8] = ref[:, :, 0:8]
        to_high[:, 8 * part : 8 * part + 8] = ref[:, :, 24:32]


def xpack_kernel(mid, low, high, ylow, yhigh, window, to_left, to_right):
    for a in range(3):
        window[a * 24 : a * 24 + 8, 1:5] = low[a].reshape(8, 4, 8, 128)
        window[a * 24 + 8 : a * 24 + 16, 1:5] = mid[a].reshape(8, 4, 8, 128)
        window[a * 24 + 16 : a * 24 + 24, 1:5] = high[a].reshape(8, 4, 8, 128)
        window[a * 24 : a * 24 + 24, 0] = ylow[a]
        window[a * 24 : a * 24 + 24, 5] = yhigh[a]
    slot = lax.shift_right_logical(iota((8, 128), 1), 3)

    def group(i, carry):
        for packed in range(3):
            left = jnp.zeros((8, 128), F32)
            right = jnp.zeros((8, 128), F32)
            for s in range(16):
                j = packed * 16 + s
                tile = window[8 * i + j // 6, j % 6]
                left = jnp.where(slot == s, shift(tile, 8 * s, 1), left)
                right = jnp.where(slot == s, shift(tile, 8 * s + 8, 1), right)
            to_left[3 * i + packed] = left
            to_right[3 * i + packed] = right
        return carry

    loop(0, 9, group, 0)


def plane(ref, z):
    return ref[pl.ds(6 * z, 6)].reshape(48, 256)


def put(ref, z, value):
    ref[pl.ds(6 * z, 6)] = value.reshape(6, 8, 256)


def inner_flux(v, wx, wy):
    fx = wx * (ahead(v, 1) - v)
    fy = wy * (ahead(v, 0) - v)
    return (fx - behind(fx, 1)) + (fy - behind(fy, 0))


def sweep(first, last, source, wx, wy, wz, step):
    v = plane(source, first)
    carry = (v, plane(wz, first - 1) * (v - plane(source, first - 1)))

    def body(z, carry):
        v, below = carry
        after = plane(source, z + 1)
        above = plane(wz, z) * (after - v)
        step(z, v, inner_flux(v, plane(wx, z), plane(wy, z)) + (above - below))
        return (after, above)

    loop(first, last + 1, body, carry)


def zpair(low_face):
    pad = jnp.zeros((1,) + low_face.shape[1:], F32)
    return jnp.concatenate([low_face, pad], 0) - jnp.concatenate([pad, low_face], 0)


def middle_weights(kappa):
    half = 0.125 * kappa
    wx = half + ahead(half, 2)
    wy = half + ahead(half, 1)
    wz = half[:-1] + half[1:]
    pad = jnp.zeros((1,) + half.shape[1:], F32)
    diag = wx + behind(wx, 2) + wy + behind(wy, 1)
    diag = diag + jnp.concatenate([wz, pad], 0) + jnp.concatenate([pad, wz], 0)
    inside = kappa > 0.0
    inverse = jnp.where(inside, reciprocal(diag), 0.0)
    return wx, wy, wz, inverse


def middle_minus(v, weights):
    wx, wy, wz, _ = weights
    fx = wx * (ahead(v, 2) - v)
    fy = wy * (ahead(v, 1) - v)
    return (fx - behind(fx, 2)) + (fy - behind(fy, 1)) + zpair(wz * (v[1:] - v[:-1]))


def down_kernel(
    window, from_left, from_right,
    share, pair_out, k1_out, iterate, right, wx, wy, wz, inverse,
    kappa, guess, rest, update, second, sums_a, sums_b, line,
):
    lane = iota((8, 128), 1)

    def unpack(i, dest, base):
        for packed in range(3):
            hi = from_right[base * 9 + 3 * i + packed]
            lo = from_left[base * 9 + 3 * i + packed]
            for s in range(16):
                j = packed * 16 + s
                edge = jnp.where(lane < 8, shift(hi, -8 * s, 1), 0.0)
                edge = jnp.where(lane >= 120, shift(lo, 120 - 8 * s, 1), edge)
                dest[48 * i + j, :, 0:128] = window[base * 24 + 8 * i + j // 6, j % 6]
                dest[48 * i + j, :, 128:256] = edge

    def unpack_all(i, carry):
        unpack(i, guess, 0)
        unpack(i, right, 1)
        unpack(i, kappa, 2)
        return carry

    loop(0, 3, unpack_all, 0)

    def weights(z, carry):
        half, below = carry
        after = 0.5 * plane(kappa, z + 1)
        x = half + ahead(half, 1)
        y = half + ahead(half, 0)
        above = half + after
        diag = x + behind(x, 1) + y + behind(y, 0) + above + below
        inside = half > 0.0
        put(wx, z, x)
        put(wy, z, y)
        put(wz, z, above)
        put(inverse, z, jnp.where(inside, reciprocal(diag), 0.0))
        return (after, above)

    half0 = 0.5 * plane(kappa, 0)
    half1 = 0.5 * plane(kappa, 1)
    put(wz, 0, half0 + half1)
    loop(1, 23, weights, (half1, half0 + half1))

    def first(z, v, minus):
        r = plane(right, z) + minus
        put(rest, z, r)
        put(update, z, FIRST * r * plane(inverse, z))

    sweep(1, 22, guess, wx, wy, wz, first)

    def next_step(z, v, minus):
        r = plane(rest, z) + minus
        d = KEEP * v + GAIN * (r * plane(inverse, z))
        put(rest, z, r)
        put(second, z, d)
        put(iterate, z, plane(guess, z) + v + d)

    sweep(2, 21, update, wx, wy, wz, next_step)

    def last(z, v, minus):
        put(rest, z, plane(rest, z) + minus)

    sweep(3, 20, second, wx, wy, wz, last)

    def add_pairs(ref, start, count, at):
        def body(m, carry):
            pair = plane(ref, start + 2 * m) + plane(ref, start + 2 * m + 1)
            rows = pl.ds(pl.multiple_of((at + m) * 48, 48), 48)
            sums_a[rows, :] = pair[:, :128]
            sums_b[rows, :] = pair[:, 128:]
            return carry

        loop(0, count, body, 0)

    add_pairs(rest, 4, 8, 0)
    add_pairs(kappa, 0, 12, 8)

    def fold(ref):
        return ref[pl.ds(0, 480, stride=2), :] + ref[pl.ds(1, 480, stride=2), :]

    coarsen = pick(lax.shift_right_logical(iota((256, 128), 0), 1) == iota((256, 128), 1), 0.125)
    both = exact_dot(jnp.concatenate([fold(sums_a), fold(sums_b)], 1), coarsen.astype(BF16))
    both = both.reshape(20, 24, 128)
    kappa_one = both[8:]
    pad = jnp.zeros((2, 24, 128), F32)
    rhs = jnp.concatenate([pad, both[:8], pad], 0)
    weights_one = middle_weights(kappa_one)
    inverse_one = weights_one[3]
    d = FIRST * (rhs * inverse_one)
    r = rhs + middle_minus(d, weights_one)
    d2 = KEEP * d + GAIN * (r * inverse_one)
    r = r + middle_minus(d2, weights_one)
    wide = iota((12, 24, 128), 2)
    um = d + d2
    pair = jnp.where(wide < 64, um, shift(rhs, 64, 2))
    pair_out[...] = pair
    k1_out[...] = kappa_one

    cell = iota((128, 128), 0)
    place = iota((128, 128), 1)
    total = jnp.zeros((24, 128), F32)
    for q, field in enumerate((r[4] + r[5], r[6] + r[7], kappa_one[4] + kappa_one[5], kappa_one[6] + kappa_one[7])):
        to = (cell < 64) & (lax.shift_right_logical(cell, 1) + 32 * q == place)
        total = total + exact_dot(field, pick(to, 0.125).astype(BF16))
    line[...] = total
    cells = line[pl.ds(4, 8, stride=2), :] + line[pl.ds(5, 8, stride=2), :]
    cells = pltpu.roll(cells, 32 * lax.axis_index("gx"), 1)
    for slot in range(16):
        share[slot, 4] = cells
    gz = lax.axis_index("gz")
    for step, planes in ((1, (um[4], um[5], um[6], rhs[5])), (-1, (um[5], um[6], um[7], rhs[6]))):
        for k, value in enumerate(planes):
            rows = shift(value, -4, 0)
            share[(gz + step) & 15, k] = jnp.where(lane < 64, rows[:8], shift(rows[8:16], 64, 1))


def turn_kernel(gathered, pair, share, pair_out):
    lane = iota((8, 128), 1)
    row = iota((8, 128), 0)
    gy = lax.axis_index("gy")
    gz = lax.axis_index("gz")
    wide = iota((24, 128), 1)

    def spread(tile):
        value = jnp.concatenate([tile, shift(tile, 64, 1), jnp.zeros((8, 128), F32)], 0)
        return shift(value, 4, 0)

    planes = [pair[z] for z in range(12)]
    for step, first, where_rhs in ((-1, 0, 1), (1, 9, 10)):
        for k in range(3):
            planes[first + k] = jnp.where(wide < 64, spread(gathered[(gz + step) & 15, k]), planes[first + k])
        value = shift(spread(gathered[(gz + step) & 15, 3]), 64, 1)
        planes[where_rhs] = jnp.where(wide < 64, planes[where_rhs], value)
    for z in range(12):
        pair_out[z] = planes[z]
    for g in range(8):
        piece = gathered[2 * g + (gz & 1), 4]
        for slot in range(8):
            share[slot, 6 + g] = piece
    for k in range(6):
        one, two = planes[2 * k], planes[2 * k + 1]
        share[(gy - 1) & 7, k] = jnp.where(row < 4, shift(one[0:8], 4, 0), two[0:8])
        share[(gy + 1) & 7, k] = jnp.where(row < 4, one[16:24], shift(two[16:24], 4, 0))


def cross_kernel(gathered, pair, share, pair_out):
    lane = iota((8, 128), 1)
    row = iota((8, 128), 0)
    slot_of = lax.shift_right_logical(lane, 3)
    gx = lax.axis_index("gx")
    gy = lax.axis_index("gy")
    tiles = []
    for k in range(6):
        low = gathered[(gy - 1) & 7, k]
        high = gathered[(gy + 1) & 7, k]
        for odd in range(2):
            value = pair[2 * k + odd]
            above = low if odd == 0 else shift(low, 4, 0)
            below = shift(high, 4, 0) if odd == 0 else high
            tiles.append(jnp.where(row < 4, above, value[0:8]))
            tiles.append(value[8:16])
            tiles.append(jnp.where(row < 4, value[16:24], below))
    for z in range(12):
        for t in range(3):
            pair_out[z, 8 * t : 8 * t + 8] = tiles[3 * z + t]
    for packed in range(3):
        left = jnp.zeros((8, 128), F32)
        right = jnp.zeros((8, 128), F32)
        for s, tile in enumerate(tiles[16 * packed : 16 * packed + 16]):
            here = slot_of == s
            first = (lane & 7) < 4
            left = jnp.where(here, jnp.where(first, shift(tile, 8 * s, 1), shift(tile, 8 * s - 60, 1)), left)
            right = jnp.where(here, jnp.where(first, shift(tile, 8 * s - 60, 1), shift(tile, 8 * s - 120, 1)), right)
        share[(gx - 1) & 3, packed] = left
        share[(gx + 1) & 3, packed] = right
    for slot in range(4):
        for g in range(8):
            share[slot, 3 + 8 * g : 11 + 8 * g] = gathered[g, 6:14]


def cplane(ref, z):
    return ref[pl.ds(8 * z, 8)].reshape(64, 128)


def cput(ref, z, value):
    ref[pl.ds(8 * z, 8)] = value.reshape(8, 8, 128)


def conjugate(gathered, other, kappa, wx, wy, wz, diag, rest, direction, image, answer):
    lane = iota((8, 128), 1)
    group = lax.shift_right_logical(lane, 5)
    nothing = jnp.zeros((64, 128), F32)
    cput(kappa, 0, nothing)
    cput(kappa, 33, nothing)
    cput(rest, 32, nothing)
    cput(wz, 0, nothing)
    direction[...] = jnp.zeros_like(direction)

    for source, parity in ((gathered, lax.axis_index("gz") & 1), (other, 1 - (lax.axis_index("gz") & 1))):

        def assemble(g, carry):
            gz = 2 * g + parity
            for gy in range(8):
                pieces = [source[gx, 3 + gy * 8 + g] for gx in range(4)]
                for q in range(4):
                    merged = pieces[0]
                    for gx in range(1, 4):
                        merged = jnp.where(group == (q + gx) % 4, pieces[gx], merged)
                    merged = shift(merged, -32 * q, 1)
                    if q < 2:
                        rest[(2 * gz + q) * 8 + gy] = merged
                    else:
                        kappa[(2 * gz + q - 1) * 8 + gy] = merged
            return carry

        loop(0, 8, assemble, 0, 2)
    inner_x = iota((64, 128), 1) < 127
    inner_y = iota((64, 128), 0) < 63
    first_x = iota((64, 128), 1) > 0
    first_y = iota((64, 128), 0) > 0

    def weights(z, total):
        half = 0.03125 * cplane(kappa, z + 1)
        before = 0.03125 * cplane(kappa, z)
        after = 0.03125 * cplane(kappa, z + 2)
        x = jnp.where(inner_x, ahead(half, 1), 0.0)
        y = jnp.where(inner_y, ahead(half, 0), 0.0)
        cput(wx, z, jnp.where(inner_x, half + x, 0.0))
        cput(wy, z, jnp.where(inner_y, half + y, 0.0))
        cput(wz, z + 1, half + after)
        x = x + jnp.where(first_x, behind(half, 1), 0.0)
        y = y + jnp.where(first_y, behind(half, 0), 0.0)
        cput(diag, z, 6.0 * half + x + y + (before + after))
        r = cplane(rest, z)
        return total + (r * r).reshape(8, 8, 128).sum(0)

    zero = jnp.zeros((8, 128), F32)

    def whole(total):
        return jnp.sum(jnp.sum(total, axis=0, keepdims=True), axis=1, keepdims=True)

    norm = whole(loop(0, 32, weights, zero))

    def image_of(beta):
        def turned(z):
            v = cplane(rest, z) + beta * cplane(direction, z + 1)
            cput(direction, z + 1, v)
            return v

        def apply(z, carry):
            before, v, total = carry
            after = turned(z + 1)
            x = cplane(wx, z)
            y = cplane(wy, z)
            w = cplane(diag, z) * v
            w = w - (x * ahead(v, 1) + behind(x * v, 1))
            w = w - (y * ahead(v, 0) + behind(y * v, 0))
            w = w - (cplane(wz, z + 1) * after + cplane(wz, z) * before)
            cput(image, z, w)
            return v, after, total + (v * w).reshape(8, 8, 128).sum(0)

        return whole(loop(0, 32, apply, (nothing, turned(0), zero), INNER)[2])

    gx = lax.axis_index("gx")
    gy = lax.axis_index("gy")
    gz = lax.axis_index("gz")
    answer[...] = jnp.zeros_like(answer)
    picked = [(3 * z + t, 2 * gz - 3 + z, gy - 1 + t) for z in range(8) for t in range(3)]

    def add_answer(alpha):
        for k, z, y in picked:
            tile = direction[(jnp.clip(z, 0, 31) + 1) * 8 + jnp.clip(y, 0, 7)]
            answer[k] = answer[k] + alpha * tile

    def iterate(repeat, carry):
        norm, beta = carry
        alpha = norm / image_of(beta)

        def step(z, total):
            r = cplane(rest, z) - alpha * cplane(image, z)
            cput(rest, z, r)
            return total + (r * r).reshape(8, 8, 128).sum(0)

        add_answer(alpha)
        norm_next = whole(loop(0, 32, step, zero, OUTER))
        return norm_next, norm_next / norm

    norm, beta = lax.fori_loop(0, ITERS - 1, iterate, (norm, jnp.zeros((1, 1), F32)))
    add_answer(norm / image_of(beta))
    wide = iota((8, 128), 1)
    position = jnp.where(wide < 64, wide, wide - 128) + 32 * gx
    known = (position >= 0) & (position < 128)
    tiles = []
    for k, z, y in picked:
        inside = known & (z >= 0) & (z < 32) & (y >= 0) & (y < 8)
        tiles.append(jnp.where(inside, pltpu.roll(answer[k], (128 - 32 * gx) & 127, 1), 0.0))
    return jnp.stack(tiles).reshape(8, 24, 128)


def middle_fields(gathered, pair):
    lane = iota((8, 128), 1)
    gx = lax.axis_index("gx")
    both = [[], []]
    for v in range(36):
        packed, s = v // 16, v % 16
        low = gathered[(gx - 1) & 3, packed]
        high = gathered[(gx + 1) & 3, packed]
        tile = pair[v // 3, 8 * (v % 3) : 8 * (v % 3) + 8]
        for k in range(2):
            own = shift(tile, 64 * k, 1) if k else tile
            edge = jnp.where(lane < 68, shift(high, 64 - 8 * s - 4 * k, 1), shift(low, 124 - 8 * s - 4 * k, 1))
            both[k].append(jnp.where(lane < 64, own, edge))
    return [jnp.stack(tiles).reshape(12, 24, 128) for tiles in both]


def up_kernel(
    gathered, other, pair, k1, iterate, right, wx, wy, wz, inverse,
    solution_out, residual_out,
    line, fine_a, fine_b, current, rest, update, second, *grids,
):
    c = conjugate(gathered, other, *grids)
    um, mr = middle_fields(gathered, pair)
    even = 0.75 * c[1:7] + 0.25 * c[0:6]
    odd = 0.75 * c[1:7] + 0.25 * c[2:8]
    c = jnp.stack([even, odd], 1).reshape(12, 24, 128)
    matrix = refine_matrix(128, 128)
    line[pl.ds(0, 288, stride=2), :] = exact_dot((0.75 * c + 0.25 * behind(c, 1)).reshape(288, 128), matrix)
    line[pl.ds(1, 288, stride=2), :] = exact_dot((0.75 * c + 0.25 * ahead(c, 1)).reshape(288, 128), matrix)
    correction = shift(line[...].reshape(12, 48, 128), -12, 1)[:, :24]

    kappa_one = k1[...]
    weights = middle_weights(kappa_one)
    inverse_one = weights[3]
    u = jnp.where(kappa_one > 0.0, um + correction, 0.0)
    r = mr + middle_minus(u, weights)
    d = FIRST * (r * inverse_one)
    u = u + d
    r = r + middle_minus(d, weights)
    u = u + (KEEP * d + GAIN * (r * inverse_one))

    even = 0.75 * u[2:10] + 0.25 * u[1:9]
    odd = 0.75 * u[2:10] + 0.25 * u[3:11]
    m = jnp.stack([even, odd], 1).reshape(16, 24, 128)
    matrix = refine_matrix(128, 256)
    for parity, near in enumerate((behind(m, 1), ahead(m, 1))):
        value = exact_dot((0.75 * m + 0.25 * near).reshape(384, 128), matrix)
        fine_a[pl.ds(parity, 384, stride=2), :] = value[:, :128]
        fine_b[pl.ds(parity, 384, stride=2), :] = value[:, 128:]

    def begin(z, carry):
        rows = pl.ds(pl.multiple_of((z - 4) * 48, 48), 48)
        fine = jnp.concatenate([fine_a[rows, :], fine_b[rows, :]], 1)
        put(current, z, jnp.where(plane(inverse, z) > 0.0, plane(iterate, z) + fine, 0.0))
        return carry

    loop(4, 20, begin, 0)

    def first(z, v, minus):
        r = plane(right, z) + minus
        put(rest, z, r)
        put(update, z, FIRST * r * plane(inverse, z))

    sweep(5, 18, current, wx, wy, wz, first)

    def next_step(z, v, minus):
        r = plane(rest, z) + minus
        d = KEEP * v + GAIN * (r * plane(inverse, z))
        put(rest, z, r)
        put(second, z, d)
        put(current, z, plane(current, z) + v + d)

    sweep(6, 17, update, wx, wy, wz, next_step)

    def last(z, v, minus):
        residual_out[z - 8] = (plane(rest, z) + minus)[8:40, :128]
        solution_out[z - 8] = plane(current, z)[8:40, :128]

    sweep(8, 15, second, wx, wy, wz, last)


def run(kernel, outs, scratch, *args):
    return pl.pallas_call(
        kernel,
        out_shape=[jax.ShapeDtypeStruct(shape, F32) for shape in outs],
        in_specs=[VMEM] * len(args),
        out_specs=[VMEM] * len(outs),
        scratch_shapes=[pltpu.VMEM(shape, F32) for shape in scratch],
        compiler_params=pltpu.CompilerParams(vmem_limit_bytes=LIMIT),
    )(*args)


FINE = (144, 8, 256)
MIDDLE = (12, 24, 128)
COARSE = (256, 8, 128)
PADDED = (272, 8, 128)
YPACK = ([(3, 24, 8, 128)] * 2, [])
XPACK = ([(72, 6, 8, 128), (27, 8, 128), (27, 8, 128)], [])
DOWN = ([(16, 5, 8, 128), MIDDLE, MIDDLE] + [FINE] * 6, [FINE] * 5 + [(960, 128)] * 2 + [(24, 128)])
TURN = ([(8, 14, 8, 128), MIDDLE], [])
CROSS = ([(4, 67, 8, 128), MIDDLE], [])
UP = (
    [(8, 32, 128)] * 2,
    [(576, 128)] + [(768, 128)] * 2 + [FINE] * 4
    + [PADDED] + [COARSE] * 2 + [PADDED, COARSE] + [PADDED] * 2 + [COARSE, (24, 8, 128)],
)


def up(axis):
    return [(i, i + 1) for i in range(lax.axis_size(axis) - 1)]


def down(axis):
    return [(i + 1, i) for i in range(lax.axis_size(axis) - 1)]


def both_ways(to_low, to_high, axis):
    return lax.ppermute(to_high, axis, up(axis)), lax.ppermute(to_low, axis, down(axis))


def local(right_side, guess, coefficient):
    mine = jnp.stack([guess, right_side, coefficient])
    low, high = both_ways(mine, mine, "gz")
    ylow, yhigh = both_ways(*run(ypack_kernel, *YPACK, mine, low, high), "gy")
    window, to_left, to_right = run(
        xpack_kernel, *XPACK, mine, low, high, ylow, yhigh
    )
    from_left, from_right = both_ways(to_left, to_right, "gx")

    share, pair, k1, *arrays = run(down_kernel, *DOWN, window, from_left, from_right)
    share, pair = run(turn_kernel, *TURN, lax.all_to_all(share, "gz", 0, 0), pair)
    share, pair = run(cross_kernel, *CROSS, lax.all_to_all(share, "gy", 0, 0), pair)
    whole = lax.all_to_all(share, "gx", 0, 0)
    other = lax.ppermute(whole, "gz", [(i, i ^ 1) for i in range(16)])
    return run(up_kernel, *UP, whole, other, pair, k1, *arrays)


def solution(mesh):
    spec = P("gz", "gy", "gx")
    return jax.shard_map(
        local, mesh=mesh, in_specs=(spec, spec, spec), out_specs=(spec, spec), check_vma=False
    )
```

```python
import jax
import jax.numpy as jnp
from jax import lax
from jax.experimental import pallas as pl
from jax.experimental.pallas import tpu as pltpu
from jax.sharding import PartitionSpec as P


ITERS = 6
THETA = 1.25
DELTA = 0.75
SIGMA = THETA / DELTA
RHO = 1.0 / SIGMA
RHO_NEXT = 1.0 / (2.0 * SIGMA - RHO)
FIRST = 1.0 / THETA
KEEP = RHO_NEXT * RHO
GAIN = 2.0 * RHO_NEXT / DELTA

INNER = 16
OUTER = 16
F32 = jnp.float32
BF16 = jnp.bfloat16
VMEM = pl.BlockSpec(memory_space=pltpu.VMEM)
LIMIT = 20 * 1024 * 1024


def loop(first, end, body, carry, unroll=16):
    count = end - first
    while count % unroll:
        unroll -= 1

    def several(i, carry):
        for k in range(unroll):
            carry = body(first + i * unroll + k, carry)
        return carry

    return lax.fori_loop(0, count // unroll, several, carry)


def shift(value, by, axis):
    return pltpu.roll(value, by % value.shape[axis], axis)


def ahead(value, axis):
    return shift(value, -1, axis)


def behind(value, axis):
    return shift(value, 1, axis)


def iota(shape, axis):
    return lax.broadcasted_iota(jnp.int32, shape, axis)


def exact_dot(value, matrix):
    high = value.astype(BF16)
    rest = value - high.astype(F32)
    middle = rest.astype(BF16)
    low = (rest - middle.astype(F32)).astype(BF16)
    parts = [jnp.dot(part, matrix, preferred_element_type=F32) for part in (low, middle, high)]
    return parts[0] + parts[1] + parts[2]


def pick(condition, number):
    return jnp.where(condition, jnp.float32(number), jnp.float32(0.0))


def reciprocal(value):
    guess = pl.reciprocal(value, approx=True)
    for _ in range(2):
        guess = guess * (2.0 - value * guess)
    return guess


def refine_matrix(size, out_size):
    parent = iota((size, out_size), 0)
    child = iota((size, out_size), 1)
    own = lax.shift_right_arithmetic(child, 1)
    other = (own + 2 * (child & 1) - 1 + size) & (size - 1)
    wide = out_size // 2
    if wide < size:
        own = jnp.where(child >= out_size * 3 // 4, own + size - wide, own)
        other = (own + 2 * (child & 1) - 1 + size) & (size - 1)
    return (pick(parent == own, 0.75) + pick(parent == other, 0.25)).astype(BF16)


TRAVEL = [(a, z) for a, skip in enumerate((1, 2, 0)) for z in range(skip, 24 - skip)]


def window_rows(mine, chip, beside, a, z, rows):
    if z // 8 == 1:
        return mine[a, z - 8, rows]
    odd = (lax.axis_index("gz") & 1) == 1
    return jnp.where(odd == (z < 8), chip[a, z % 8, rows], beside[a, z % 8, rows])


def ypack_kernel(mine, chip, beside, to_high, to_low):
    for i, (a, z) in enumerate(TRAVEL):
        to_low[i] = window_rows(mine, chip, beside, a, z, slice(0, 8))
        to_high[i] = window_rows(mine, chip, beside, a, z, slice(24, 32))


def xpack_kernel(mine, chip, beside, ylow, yhigh, window, to_right, to_left):
    for i, (a, z) in enumerate(TRAVEL):
        window[24 * a + z, 0] = ylow[i]
        window[24 * a + z, 1:5] = window_rows(mine, chip, beside, a, z, slice(0, 32)).reshape(4, 8, 128)
        window[24 * a + z, 5] = yhigh[i]
    slot = lax.shift_right_logical(iota((8, 128), 1), 3)

    def group(i, carry):
        for packed in range(3):
            left = jnp.zeros((8, 128), F32)
            right = jnp.zeros((8, 128), F32)
            for s in range(16):
                j = packed * 16 + s
                tile = window[8 * i + j // 6, j % 6]
                left = jnp.where(slot == s, shift(tile, 8 * s, 1), left)
                right = jnp.where(slot == s, shift(tile, 8 * s + 8, 1), right)
            to_left[3 * i + packed] = left
            to_right[3 * i + packed] = right
        return carry

    loop(0, 9, group, 0)


def plane(ref, z):
    return ref[pl.ds(6 * z, 6)].reshape(48, 256)


def put(ref, z, value):
    ref[pl.ds(6 * z, 6)] = value.reshape(6, 8, 256)


def inner_flux(v, wx, wy):
    fx = wx * (ahead(v, 1) - v)
    fy = wy * (ahead(v, 0) - v)
    return (fx - behind(fx, 1)) + (fy - behind(fy, 0))


def sweep(first, last, source, wx, wy, wz, step):
    v = plane(source, first)
    carry = (v, plane(wz, first - 1) * (v - plane(source, first - 1)))

    def body(z, carry):
        v, below = carry
        after = plane(source, z + 1)
        above = plane(wz, z) * (after - v)
        step(z, v, inner_flux(v, plane(wx, z), plane(wy, z)) + (above - below))
        return (after, above)

    loop(first, last + 1, body, carry)


def zpair(low_face):
    pad = jnp.zeros((1,) + low_face.shape[1:], F32)
    return jnp.concatenate([low_face, pad], 0) - jnp.concatenate([pad, low_face], 0)


def middle_weights(kappa):
    half = 0.125 * kappa
    wx = half + ahead(half, 2)
    wy = half + ahead(half, 1)
    wz = half[:-1] + half[1:]
    pad = jnp.zeros((1,) + half.shape[1:], F32)
    diag = wx + behind(wx, 2) + wy + behind(wy, 1)
    diag = diag + jnp.concatenate([wz, pad], 0) + jnp.concatenate([pad, wz], 0)
    inside = kappa > 0.0
    inverse = jnp.where(inside, reciprocal(diag), 0.0)
    return wx, wy, wz, inverse


def middle_minus(v, weights):
    wx, wy, wz, _ = weights
    fx = wx * (ahead(v, 2) - v)
    fy = wy * (ahead(v, 1) - v)
    return (fx - behind(fx, 2)) + (fy - behind(fy, 1)) + zpair(wz * (v[1:] - v[:-1]))


def down_kernel(
    window, from_left, from_right,
    share, pair_out, k1_out, iterate, right, wx, wy, wz, inverse,
    kappa, guess, rest, update, second, sums_a, sums_b, line,
):
    lane = iota((8, 128), 1)

    def unpack(i, dest, base):
        for packed in range(3):
            hi = from_right[base * 9 + 3 * i + packed]
            lo = from_left[base * 9 + 3 * i + packed]
            for s in range(16):
                j = packed * 16 + s
                edge = jnp.where(lane < 8, shift(hi, -8 * s, 1), 0.0)
                edge = jnp.where(lane >= 120, shift(lo, 120 - 8 * s, 1), edge)
                dest[48 * i + j, :, 0:128] = window[base * 24 + 8 * i + j // 6, j % 6]
                dest[48 * i + j, :, 128:256] = edge

    def unpack_all(i, carry):
        unpack(i, guess, 0)
        unpack(i, right, 1)
        unpack(i, kappa, 2)
        return carry

    loop(0, 3, unpack_all, 0)

    def weights(z, carry):
        half, below = carry
        after = 0.5 * plane(kappa, z + 1)
        x = half + ahead(half, 1)
        y = half + ahead(half, 0)
        above = half + after
        diag = x + behind(x, 1) + y + behind(y, 0) + above + below
        inside = half > 0.0
        put(wx, z, x)
        put(wy, z, y)
        put(wz, z, above)
        put(inverse, z, jnp.where(inside, reciprocal(diag), 0.0))
        return (after, above)

    half1 = 0.5 * plane(kappa, 1)
    half2 = 0.5 * plane(kappa, 2)
    put(wz, 1, half1 + half2)
    loop(2, 22, weights, (half2, half1 + half2))

    def first(z, v, minus):
        r = plane(right, z) + minus
        put(rest, z, r)
        put(update, z, FIRST * r * plane(inverse, z))

    sweep(2, 21, guess, wx, wy, wz, first)

    def next_step(z, v, minus):
        r = plane(rest, z) + minus
        d = KEEP * v + GAIN * (r * plane(inverse, z))
        put(rest, z, r)
        put(second, z, d)
        put(iterate, z, plane(guess, z) + v + d)

    sweep(3, 20, update, wx, wy, wz, next_step)

    def last(z, v, minus):
        put(rest, z, plane(rest, z) + minus)

    sweep(4, 19, second, wx, wy, wz, last)

    def add_pairs(ref, start, count, at):
        def body(m, carry):
            pair = plane(ref, start + 2 * m) + plane(ref, start + 2 * m + 1)
            rows = pl.ds(pl.multiple_of((at + m) * 48, 48), 48)
            sums_a[rows, :] = pair[:, :128]
            sums_b[rows, :] = pair[:, 128:]
            return carry

        loop(0, count, body, 0)

    add_pairs(rest, 4, 8, 0)
    add_pairs(kappa, 0, 12, 8)

    def fold(ref):
        return ref[pl.ds(0, 480, stride=2), :] + ref[pl.ds(1, 480, stride=2), :]

    coarsen = pick(lax.shift_right_logical(iota((256, 128), 0), 1) == iota((256, 128), 1), 0.125)
    both = exact_dot(jnp.concatenate([fold(sums_a), fold(sums_b)], 1), coarsen.astype(BF16))
    both = both.reshape(20, 24, 128)
    kappa_one = both[8:]
    pad = jnp.zeros((2, 24, 128), F32)
    rhs = jnp.concatenate([pad, both[:8], pad], 0)
    weights_one = middle_weights(kappa_one)
    inverse_one = weights_one[3]
    d = FIRST * (rhs * inverse_one)
    r = rhs + middle_minus(d, weights_one)
    d2 = KEEP * d + GAIN * (r * inverse_one)
    r = r + middle_minus(d2, weights_one)
    wide = iota((12, 24, 128), 2)
    um = d + d2
    pair = jnp.where(wide < 64, um, shift(rhs, 64, 2))
    pair_out[...] = pair
    k1_out[...] = kappa_one

    cell = iota((128, 128), 0)
    place = iota((128, 128), 1)
    total = jnp.zeros((24, 128), F32)
    for q, field in enumerate((r[4] + r[5], r[6] + r[7], kappa_one[4] + kappa_one[5], kappa_one[6] + kappa_one[7])):
        to = (cell < 64) & (lax.shift_right_logical(cell, 1) + 32 * q == place)
        total = total + exact_dot(field, pick(to, 0.125).astype(BF16))
    line[...] = total
    cells = line[pl.ds(4, 8, stride=2), :] + line[pl.ds(5, 8, stride=2), :]
    cells = pltpu.roll(cells, 32 * lax.axis_index("gx"), 1)
    for slot in range(16):
        share[slot, 4] = cells
    gz = lax.axis_index("gz")
    for step, planes in ((1, (um[4], um[5], um[6], rhs[5])), (-1, (um[5], um[6], um[7], rhs[6]))):
        for k, value in enumerate(planes):
            rows = shift(value, -4, 0)
            share[(gz + step) & 15, k] = jnp.where(lane < 64, rows[:8], shift(rows[8:16], 64, 1))


def turn_kernel(gathered, pair, share, pair_out):
    lane = iota((8, 128), 1)
    row = iota((8, 128), 0)
    gy = lax.axis_index("gy")
    gz = lax.axis_index("gz")
    wide = iota((24, 128), 1)

    def spread(tile):
        value = jnp.concatenate([tile, shift(tile, 64, 1), jnp.zeros((8, 128), F32)], 0)
        return shift(value, 4, 0)

    planes = [pair[z] for z in range(12)]
    for step, first, where_rhs in ((-1, 0, 1), (1, 9, 10)):
        for k in range(3):
            planes[first + k] = jnp.where(wide < 64, spread(gathered[(gz + step) & 15, k]), planes[first + k])
        value = shift(spread(gathered[(gz + step) & 15, 3]), 64, 1)
        planes[where_rhs] = jnp.where(wide < 64, planes[where_rhs], value)
    for z in range(12):
        pair_out[z] = planes[z]
    for g in range(8):
        piece = gathered[2 * g + (gz & 1), 4]
        for slot in range(8):
            share[slot, 6 + g] = piece
    for k in range(6):
        one, two = planes[2 * k], planes[2 * k + 1]
        share[(gy - 1) & 7, k] = jnp.where(row < 4, shift(one[0:8], 4, 0), two[0:8])
        share[(gy + 1) & 7, k] = jnp.where(row < 4, one[16:24], shift(two[16:24], 4, 0))


def cross_kernel(gathered, pair, share, pair_out):
    lane = iota((8, 128), 1)
    row = iota((8, 128), 0)
    slot_of = lax.shift_right_logical(lane, 3)
    gx = lax.axis_index("gx")
    gy = lax.axis_index("gy")
    tiles = []
    for k in range(6):
        low = gathered[(gy - 1) & 7, k]
        high = gathered[(gy + 1) & 7, k]
        for odd in range(2):
            value = pair[2 * k + odd]
            above = low if odd == 0 else shift(low, 4, 0)
            below = shift(high, 4, 0) if odd == 0 else high
            tiles.append(jnp.where(row < 4, above, value[0:8]))
            tiles.append(value[8:16])
            tiles.append(jnp.where(row < 4, value[16:24], below))
    for z in range(12):
        for t in range(3):
            pair_out[z, 8 * t : 8 * t + 8] = tiles[3 * z + t]
    for packed in range(3):
        left = jnp.zeros((8, 128), F32)
        right = jnp.zeros((8, 128), F32)
        for s, tile in enumerate(tiles[16 * packed : 16 * packed + 16]):
            here = slot_of == s
            first = (lane & 7) < 4
            left = jnp.where(here, jnp.where(first, shift(tile, 8 * s, 1), shift(tile, 8 * s - 60, 1)), left)
            right = jnp.where(here, jnp.where(first, shift(tile, 8 * s - 60, 1), shift(tile, 8 * s - 120, 1)), right)
        share[(gx - 1) & 3, packed] = left
        share[(gx + 1) & 3, packed] = right
    for slot in range(4):
        for g in range(8):
            share[slot, 3 + 8 * g : 11 + 8 * g] = gathered[g, 6:14]


def cplane(ref, z):
    return ref[pl.ds(8 * z, 8)].reshape(64, 128)


def cput(ref, z, value):
    ref[pl.ds(8 * z, 8)] = value.reshape(8, 8, 128)


def conjugate(gathered, other, kappa, wx, wy, wz, diag, rest, direction, image, answer):
    lane = iota((8, 128), 1)
    group = lax.shift_right_logical(lane, 5)
    nothing = jnp.zeros((64, 128), F32)
    cput(kappa, 0, nothing)
    cput(kappa, 33, nothing)
    cput(rest, 32, nothing)
    cput(wz, 0, nothing)
    direction[...] = jnp.zeros_like(direction)

    for source, parity in ((gathered, lax.axis_index("gz") & 1), (other, 1 - (lax.axis_index("gz") & 1))):

        def assemble(g, carry):
            gz = 2 * g + parity
            for gy in range(8):
                pieces = [source[gx, 3 + gy * 8 + g] for gx in range(4)]
                for q in range(4):
                    merged = pieces[0]
                    for gx in range(1, 4):
                        merged = jnp.where(group == (q + gx) % 4, pieces[gx], merged)
                    merged = shift(merged, -32 * q, 1)
                    if q < 2:
                        rest[(2 * gz + q) * 8 + gy] = merged
                    else:
                        kappa[(2 * gz + q - 1) * 8 + gy] = merged
            return carry

        loop(0, 8, assemble, 0, 2)
    inner_x = iota((64, 128), 1) < 127
    inner_y = iota((64, 128), 0) < 63
    first_x = iota((64, 128), 1) > 0
    first_y = iota((64, 128), 0) > 0

    def weights(z, total):
        half = 0.03125 * cplane(kappa, z + 1)
        before = 0.03125 * cplane(kappa, z)
        after = 0.03125 * cplane(kappa, z + 2)
        x = jnp.where(inner_x, ahead(half, 1), 0.0)
        y = jnp.where(inner_y, ahead(half, 0), 0.0)
        cput(wx, z, jnp.where(inner_x, half + x, 0.0))
        cput(wy, z, jnp.where(inner_y, half + y, 0.0))
        cput(wz, z + 1, half + after)
        x = x + jnp.where(first_x, behind(half, 1), 0.0)
        y = y + jnp.where(first_y, behind(half, 0), 0.0)
        cput(diag, z, 6.0 * half + x + y + (before + after))
        r = cplane(rest, z)
        return total + (r * r).reshape(8, 8, 128).sum(0)

    zero = jnp.zeros((8, 128), F32)

    def whole(total):
        return jnp.sum(jnp.sum(total, axis=0, keepdims=True), axis=1, keepdims=True)

    norm = whole(loop(0, 32, weights, zero))

    def image_of(beta):
        def turned(z):
            v = cplane(rest, z) + beta * cplane(direction, z + 1)
            cput(direction, z + 1, v)
            return v

        def apply(z, carry):
            before, v, total = carry
            after = turned(z + 1)
            x = cplane(wx, z)
            y = cplane(wy, z)
            w = cplane(diag, z) * v
            w = w - (x * ahead(v, 1) + behind(x * v, 1))
            w = w - (y * ahead(v, 0) + behind(y * v, 0))
            w = w - (cplane(wz, z + 1) * after + cplane(wz, z) * before)
            cput(image, z, w)
            return v, after, total + (v * w).reshape(8, 8, 128).sum(0)

        return whole(loop(0, 32, apply, (nothing, turned(0), zero), INNER)[2])

    gx = lax.axis_index("gx")
    gy = lax.axis_index("gy")
    gz = lax.axis_index("gz")
    answer[...] = jnp.zeros_like(answer)
    picked = [(3 * z + t, 2 * gz - 3 + z, gy - 1 + t) for z in range(8) for t in range(3)]

    def add_answer(alpha):
        for k, z, y in picked:
            tile = direction[(jnp.clip(z, 0, 31) + 1) * 8 + jnp.clip(y, 0, 7)]
            answer[k] = answer[k] + alpha * tile

    def iterate(repeat, carry):
        norm, beta = carry
        alpha = norm / image_of(beta)

        def step(z, total):
            r = cplane(rest, z) - alpha * cplane(image, z)
            cput(rest, z, r)
            return total + (r * r).reshape(8, 8, 128).sum(0)

        add_answer(alpha)
        norm_next = whole(loop(0, 32, step, zero, OUTER))
        return norm_next, norm_next / norm

    norm, beta = lax.fori_loop(0, ITERS - 1, iterate, (norm, jnp.zeros((1, 1), F32)))
    add_answer(norm / image_of(beta))
    wide = iota((8, 128), 1)
    position = jnp.where(wide < 64, wide, wide - 128) + 32 * gx
    known = (position >= 0) & (position < 128)
    tiles = []
    for k, z, y in picked:
        inside = known & (z >= 0) & (z < 32) & (y >= 0) & (y < 8)
        tiles.append(jnp.where(inside, pltpu.roll(answer[k], (128 - 32 * gx) & 127, 1), 0.0))
    return jnp.stack(tiles).reshape(8, 24, 128)


def middle_fields(gathered, pair):
    lane = iota((8, 128), 1)
    gx = lax.axis_index("gx")
    both = [[], []]
    for v in range(36):
        packed, s = v // 16, v % 16
        low = gathered[(gx - 1) & 3, packed]
        high = gathered[(gx + 1) & 3, packed]
        tile = pair[v // 3, 8 * (v % 3) : 8 * (v % 3) + 8]
        for k in range(2):
            own = shift(tile, 64 * k, 1) if k else tile
            edge = jnp.where(lane < 68, shift(high, 64 - 8 * s - 4 * k, 1), shift(low, 124 - 8 * s - 4 * k, 1))
            both[k].append(jnp.where(lane < 64, own, edge))
    return [jnp.stack(tiles).reshape(12, 24, 128) for tiles in both]


def up_kernel(
    gathered, other, pair, k1, iterate, right, wx, wy, wz, inverse,
    solution_out, residual_out,
    line, fine_a, fine_b, current, rest, update, second, *grids,
):
    c = conjugate(gathered, other, *grids)
    um, mr = middle_fields(gathered, pair)
    even = 0.75 * c[1:7] + 0.25 * c[0:6]
    odd = 0.75 * c[1:7] + 0.25 * c[2:8]
    c = jnp.stack([even, odd], 1).reshape(12, 24, 128)
    matrix = refine_matrix(128, 128)
    line[pl.ds(0, 288, stride=2), :] = exact_dot((0.75 * c + 0.25 * behind(c, 1)).reshape(288, 128), matrix)
    line[pl.ds(1, 288, stride=2), :] = exact_dot((0.75 * c + 0.25 * ahead(c, 1)).reshape(288, 128), matrix)
    correction = shift(line[...].reshape(12, 48, 128), -12, 1)[:, :24]

    kappa_one = k1[...]
    weights = middle_weights(kappa_one)
    inverse_one = weights[3]
    u = jnp.where(kappa_one > 0.0, um + correction, 0.0)
    r = mr + middle_minus(u, weights)
    d = FIRST * (r * inverse_one)
    u = u + d
    r = r + middle_minus(d, weights)
    u = u + (KEEP * d + GAIN * (r * inverse_one))

    even = 0.75 * u[2:10] + 0.25 * u[1:9]
    odd = 0.75 * u[2:10] + 0.25 * u[3:11]
    m = jnp.stack([even, odd], 1).reshape(16, 24, 128)
    matrix = refine_matrix(128, 256)
    for parity, near in enumerate((behind(m, 1), ahead(m, 1))):
        value = exact_dot((0.75 * m + 0.25 * near).reshape(384, 128), matrix)
        fine_a[pl.ds(parity, 384, stride=2), :] = value[:, :128]
        fine_b[pl.ds(parity, 384, stride=2), :] = value[:, 128:]

    def begin(z, carry):
        rows = pl.ds(pl.multiple_of((z - 4) * 48, 48), 48)
        fine = jnp.concatenate([fine_a[rows, :], fine_b[rows, :]], 1)
        put(current, z, jnp.where(plane(inverse, z) > 0.0, plane(iterate, z) + fine, 0.0))
        return carry

    loop(4, 20, begin, 0)

    def first(z, v, minus):
        r = plane(right, z) + minus
        put(rest, z, r)
        put(update, z, FIRST * r * plane(inverse, z))

    sweep(5, 18, current, wx, wy, wz, first)

    def next_step(z, v, minus):
        r = plane(rest, z) + minus
        d = KEEP * v + GAIN * (r * plane(inverse, z))
        put(rest, z, r)
        put(second, z, d)
        put(current, z, plane(current, z) + v + d)

    sweep(6, 17, update, wx, wy, wz, next_step)

    def last(z, v, minus):
        residual_out[z - 8] = (plane(rest, z) + minus)[8:40, :128]
        solution_out[z - 8] = plane(current, z)[8:40, :128]

    sweep(8, 15, second, wx, wy, wz, last)


def run(kernel, outs, scratch, *args):
    return pl.pallas_call(
        kernel,
        out_shape=[jax.ShapeDtypeStruct(shape, F32) for shape in outs],
        in_specs=[VMEM] * len(args),
        out_specs=[VMEM] * len(outs),
        scratch_shapes=[pltpu.VMEM(shape, F32) for shape in scratch],
        compiler_params=pltpu.CompilerParams(vmem_limit_bytes=LIMIT),
    )(*args)


FINE = (144, 8, 256)
MIDDLE = (12, 24, 128)
COARSE = (256, 8, 128)
PADDED = (272, 8, 128)
YPACK = ([(66, 8, 128)] * 2, [])
XPACK = ([(72, 6, 8, 128), (27, 8, 128), (27, 8, 128)], [])
DOWN = ([(16, 5, 8, 128), MIDDLE, MIDDLE] + [FINE] * 6, [FINE] * 5 + [(960, 128)] * 2 + [(24, 128)])
TURN = ([(8, 14, 8, 128), MIDDLE], [])
CROSS = ([(4, 67, 8, 128), MIDDLE], [])
UP = (
    [(8, 32, 128)] * 2,
    [(576, 128)] + [(768, 128)] * 2 + [FINE] * 4
    + [PADDED] + [COARSE] * 2 + [PADDED, COARSE] + [PADDED] * 2 + [COARSE, (24, 8, 128)],
)


def up(axis):
    return [(i, i + 1) for i in range(lax.axis_size(axis) - 1)]


def down(axis):
    return [(i + 1, i) for i in range(lax.axis_size(axis) - 1)]


def both_ways(to_low, to_high, axis):
    return lax.ppermute(to_high, axis, up(axis)), lax.ppermute(to_low, axis, down(axis))


def local(right_side, guess, coefficient):
    mine = jnp.stack([guess, right_side, coefficient])
    beside = lax.ppermute(mine, "gz", [(i, ((i + 1) ^ 1) - 1) for i in range(1, 15)])
    chip = lax.ppermute(mine, "gz", [(i, i ^ 1) for i in range(16)])
    to_high, to_low = run(ypack_kernel, *YPACK, mine, chip, beside)
    ylow, yhigh = both_ways(to_low, to_high, "gy")
    window, to_right, to_left = run(
        xpack_kernel, *XPACK, mine, chip, beside, ylow, yhigh
    )
    from_left, from_right = both_ways(to_left, to_right, "gx")

    share, pair, k1, *arrays = run(down_kernel, *DOWN, window, from_left, from_right)
    share, pair = run(turn_kernel, *TURN, lax.all_to_all(share, "gz", 0, 0), pair)
    share, pair = run(cross_kernel, *CROSS, lax.all_to_all(share, "gy", 0, 0), pair)
    whole = lax.all_to_all(share, "gx", 0, 0)
    other = lax.ppermute(whole, "gz", [(i, i ^ 1) for i in range(16)])
    return run(up_kernel, *UP, whole, other, pair, k1, *arrays)


def solution(mesh):
    spec = P("gz", "gy", "gx")
    return jax.shard_map(
        local, mesh=mesh, in_specs=(spec, spec, spec), out_specs=(spec, spec), check_vma=False
    )
```

```python
import jax
import jax.numpy as jnp
from jax import lax
from jax.experimental import pallas as pl
from jax.experimental.pallas import tpu as pltpu
from jax.sharding import PartitionSpec as P


ITERS = 6
THETA = 1.25
DELTA = 0.75
SIGMA = THETA / DELTA
RHO = 1.0 / SIGMA
RHO_NEXT = 1.0 / (2.0 * SIGMA - RHO)
FIRST = 1.0 / THETA
KEEP = RHO_NEXT * RHO
GAIN = 2.0 * RHO_NEXT / DELTA

INNER = 16
SWEEP = 8
SWEEP_UP = 16
OUTER = 16
F32 = jnp.float32
BF16 = jnp.bfloat16
VMEM = pl.BlockSpec(memory_space=pltpu.VMEM)
LIMIT = 20 * 1024 * 1024


def loop(first, end, body, carry, unroll=16):
    count = end - first
    while count % unroll:
        unroll -= 1

    def several(i, carry):
        for k in range(unroll):
            carry = body(first + i * unroll + k, carry)
        return carry

    return lax.fori_loop(0, count // unroll, several, carry)


def shift(value, by, axis):
    return pltpu.roll(value, by % value.shape[axis], axis)


def ahead(value, axis):
    return shift(value, -1, axis)


def behind(value, axis):
    return shift(value, 1, axis)


def iota(shape, axis):
    return lax.broadcasted_iota(jnp.int32, shape, axis)


def exact_dot(value, matrix):
    high = value.astype(BF16)
    rest = value - high.astype(F32)
    middle = rest.astype(BF16)
    low = (rest - middle.astype(F32)).astype(BF16)
    parts = [jnp.dot(part, matrix, preferred_element_type=F32) for part in (low, middle, high)]
    return parts[0] + parts[1] + parts[2]


def pick(condition, number):
    return jnp.where(condition, jnp.float32(number), jnp.float32(0.0))


def reciprocal(value):
    guess = pl.reciprocal(value, approx=True)
    for _ in range(2):
        guess = guess * (2.0 - value * guess)
    return guess


def refine_matrix(size, out_size):
    parent = iota((size, out_size), 0)
    child = iota((size, out_size), 1)
    own = lax.shift_right_arithmetic(child, 1)
    other = (own + 2 * (child & 1) - 1 + size) & (size - 1)
    wide = out_size // 2
    if wide < size:
        own = jnp.where(child >= out_size * 3 // 4, own + size - wide, own)
        other = (own + 2 * (child & 1) - 1 + size) & (size - 1)
    return (pick(parent == own, 0.75) + pick(parent == other, 0.25)).astype(BF16)


TRAVEL = [(a, z) for a, skip in enumerate((1, 2, 0)) for z in range(skip, 24 - skip)]


def window_rows(mine, chip, beside, a, z, rows):
    if z // 8 == 1:
        return mine[a, z - 8, rows]
    odd = (lax.axis_index("gz") & 1) == 1
    return jnp.where(odd == (z < 8), chip[a, z % 8, rows], beside[a, z % 8, rows])


def ypack_kernel(mine, chip, beside, to_high, to_low):
    for i, (a, z) in enumerate(TRAVEL):
        to_low[i] = window_rows(mine, chip, beside, a, z, slice(0, 8))
        to_high[i] = window_rows(mine, chip, beside, a, z, slice(24, 32))


def xpack_kernel(mine, chip, beside, ylow, yhigh, window, to_right, to_left):
    for i, (a, z) in enumerate(TRAVEL):
        window[24 * a + z, 0] = ylow[i]
        window[24 * a + z, 1:5] = window_rows(mine, chip, beside, a, z, slice(0, 32)).reshape(4, 8, 128)
        window[24 * a + z, 5] = yhigh[i]
    slot = lax.shift_right_logical(iota((8, 128), 1), 3)

    def group(i, carry):
        for packed in range(3):
            left = jnp.zeros((8, 128), F32)
            right = jnp.zeros((8, 128), F32)
            for s in range(16):
                j = packed * 16 + s
                tile = window[8 * i + j // 6, j % 6]
                rolled = shift(tile, 8 * s, 1)
                left = jnp.where(slot == s, rolled, left)
                right = jnp.where(slot == (s - 1) % 16, rolled, right)
            to_left[3 * i + packed] = left
            to_right[3 * i + packed] = right
        return carry

    loop(0, 9, group, 0)


def plane(ref, z):
    return ref[pl.ds(6 * z, 6)].reshape(48, 256)


def put(ref, z, value):
    ref[pl.ds(6 * z, 6)] = value.reshape(6, 8, 256)


def put_own(ref, z, value):
    ref[pl.ds(6 * z + 1, 4), :, :128] = value[8:40, :128].reshape(4, 8, 128)


def inner_flux(v, wx, wy):
    fx = wx * (ahead(v, 1) - v)
    fy = wy * (ahead(v, 0) - v)
    return (fx - behind(fx, 1)) + (fy - behind(fy, 0))


def sweep(first, last, source, wx, wy, wz, step, unroll):
    v = plane(source, first)
    carry = (v, plane(wz, first - 1) * (v - plane(source, first - 1)))

    def body(z, carry):
        v, below = carry
        after = plane(source, z + 1)
        above = plane(wz, z) * (after - v)
        step(z, v, inner_flux(v, plane(wx, z), plane(wy, z)) + (above - below))
        return (after, above)

    loop(first, last + 1, body, carry, unroll)


def zpair(low_face):
    pad = jnp.zeros((1,) + low_face.shape[1:], F32)
    return jnp.concatenate([low_face, pad], 0) - jnp.concatenate([pad, low_face], 0)


def middle_weights(kappa):
    half = 0.125 * kappa
    wx = half + ahead(half, 2)
    wy = half + ahead(half, 1)
    wz = half[:-1] + half[1:]
    pad = jnp.zeros((1,) + half.shape[1:], F32)
    diag = wx + behind(wx, 2) + wy + behind(wy, 1)
    diag = diag + jnp.concatenate([wz, pad], 0) + jnp.concatenate([pad, wz], 0)
    inside = kappa > 0.0
    inverse = jnp.where(inside, reciprocal(diag), 0.0)
    return wx, wy, wz, inverse


def middle_minus(v, weights):
    wx, wy, wz, _ = weights
    fx = wx * (ahead(v, 2) - v)
    fy = wy * (ahead(v, 1) - v)
    return (fx - behind(fx, 2)) + (fy - behind(fy, 1)) + zpair(wz * (v[1:] - v[:-1]))


def down_kernel(
    window, from_left, from_right,
    share, pair_out, k1_out, iterate, right, wx, wy, wz, inverse,
    kappa, guess, rest, update, second, sums_a, sums_b, line,
):
    lane = iota((8, 128), 1)
    slot_of = lax.shift_right_logical(lane, 3)
    beside = (lane < 8) | (lane >= 120)

    def unpack(i, dest, base):
        for packed in range(3):
            hi = from_right[base * 9 + 3 * i + packed]
            lo = from_left[base * 9 + 3 * i + packed]
            for s in range(16):
                j = packed * 16 + s
                edge = jnp.where(beside, shift(jnp.where(slot_of == s, hi, lo), -8 * s, 1), 0.0)
                dest[48 * i + j, :, 0:128] = window[base * 24 + 8 * i + j // 6, j % 6]
                dest[48 * i + j, :, 128:256] = edge

    def unpack_all(i, carry):
        unpack(i, guess, 0)
        unpack(i, right, 1)
        unpack(i, kappa, 2)
        return carry

    loop(0, 3, unpack_all, 0)

    def weights(z, carry):
        half, below = carry
        after = 0.5 * plane(kappa, z + 1)
        x = half + ahead(half, 1)
        y = half + ahead(half, 0)
        above = half + after
        diag = x + behind(x, 1) + y + behind(y, 0) + above + below
        inside = half > 0.0
        put(wx, z, x)
        put(wy, z, y)
        put(wz, z, above)
        put(inverse, z, jnp.where(inside, reciprocal(diag), 0.0))
        return (after, above)

    half1 = 0.5 * plane(kappa, 1)
    half2 = 0.5 * plane(kappa, 2)
    put(wz, 1, half1 + half2)
    loop(2, 22, weights, (half2, half1 + half2), SWEEP)

    def first(z, v, minus):
        r = plane(right, z) + minus
        put(rest, z, r)
        put(update, z, FIRST * r * plane(inverse, z))

    sweep(2, 21, guess, wx, wy, wz, first, SWEEP)

    def next_step(z, v, minus):
        r = plane(rest, z) + minus
        d = KEEP * v + GAIN * (r * plane(inverse, z))
        put(rest, z, r)
        put(second, z, d)
        put(iterate, z, plane(guess, z) + v + d)

    sweep(3, 20, update, wx, wy, wz, next_step, SWEEP)

    def last(z, v, minus):
        put(rest, z, plane(rest, z) + minus)

    sweep(4, 19, second, wx, wy, wz, last, SWEEP)

    def add_pairs(ref, start, count, at):
        def body(m, carry):
            pair = plane(ref, start + 2 * m) + plane(ref, start + 2 * m + 1)
            rows = pl.ds(pl.multiple_of((at + m) * 48, 48), 48)
            sums_a[rows, :] = pair[:, :128]
            sums_b[rows, :] = pair[:, 128:]
            return carry

        loop(0, count, body, 0)

    add_pairs(rest, 4, 8, 0)
    add_pairs(kappa, 0, 12, 8)

    def fold(ref):
        return ref[pl.ds(0, 480, stride=2), :] + ref[pl.ds(1, 480, stride=2), :]

    coarsen = pick(lax.shift_right_logical(iota((256, 128), 0), 1) == iota((256, 128), 1), 0.125)
    both = exact_dot(jnp.concatenate([fold(sums_a), fold(sums_b)], 1), coarsen.astype(BF16))
    both = both.reshape(20, 24, 128)
    kappa_one = both[8:]
    pad = jnp.zeros((2, 24, 128), F32)
    rhs = jnp.concatenate([pad, both[:8], pad], 0)
    weights_one = middle_weights(kappa_one)
    inverse_one = weights_one[3]
    d = FIRST * (rhs * inverse_one)
    r = rhs + middle_minus(d, weights_one)
    d2 = KEEP * d + GAIN * (r * inverse_one)
    r = r + middle_minus(d2, weights_one)
    wide = iota((12, 24, 128), 2)
    um = d + d2
    pair = jnp.where(wide < 64, um, shift(rhs, 64, 2))
    pair_out[...] = pair
    k1_out[...] = kappa_one

    cell = iota((128, 128), 0)
    place = iota((128, 128), 1)
    total = jnp.zeros((24, 128), F32)
    for q, field in enumerate((r[4] + r[5], r[6] + r[7], kappa_one[4] + kappa_one[5], kappa_one[6] + kappa_one[7])):
        to = (cell < 64) & (lax.shift_right_logical(cell, 1) + 32 * q == place)
        total = total + exact_dot(field, pick(to, 0.125).astype(BF16))
    line[...] = total
    cells = line[pl.ds(4, 8, stride=2), :] + line[pl.ds(5, 8, stride=2), :]
    cells = pltpu.roll(cells, 32 * lax.axis_index("gx"), 1)
    for slot in range(16):
        share[slot, 4] = cells
    gz = lax.axis_index("gz")
    for step, planes in ((1, (um[4], um[5], um[6], rhs[5])), (-1, (um[5], um[6], um[7], rhs[6]))):
        for k, value in enumerate(planes):
            rows = shift(value, -4, 0)
            share[(gz + step) & 15, k] = jnp.where(lane < 64, rows[:8], shift(rows[8:16], 64, 1))


def turn_kernel(gathered, pair, share, pair_out):
    lane = iota((8, 128), 1)
    row = iota((8, 128), 0)
    gy = lax.axis_index("gy")
    gz = lax.axis_index("gz")
    wide = iota((24, 128), 1)

    def spread(tile):
        value = jnp.concatenate([tile, shift(tile, 64, 1), jnp.zeros((8, 128), F32)], 0)
        return shift(value, 4, 0)

    planes = [pair[z] for z in range(12)]
    for step, first, where_rhs in ((-1, 0, 1), (1, 9, 10)):
        for k in range(3):
            planes[first + k] = jnp.where(wide < 64, spread(gathered[(gz + step) & 15, k]), planes[first + k])
        value = shift(spread(gathered[(gz + step) & 15, 3]), 64, 1)
        planes[where_rhs] = jnp.where(wide < 64, planes[where_rhs], value)
    for z in range(12):
        pair_out[z] = planes[z]
    for g in range(8):
        piece = gathered[2 * g + (gz & 1), 4]
        for slot in range(8):
            share[slot, 6 + g] = piece
    for k in range(6):
        one, two = planes[2 * k], planes[2 * k + 1]
        share[(gy - 1) & 7, k] = jnp.where(row < 4, shift(one[0:8], 4, 0), two[0:8])
        share[(gy + 1) & 7, k] = jnp.where(row < 4, one[16:24], shift(two[16:24], 4, 0))


def cross_kernel(gathered, pair, share, pair_out):
    lane = iota((8, 128), 1)
    row = iota((8, 128), 0)
    slot_of = lax.shift_right_logical(lane, 3)
    gx = lax.axis_index("gx")
    gy = lax.axis_index("gy")
    tiles = []
    for k in range(6):
        low = gathered[(gy - 1) & 7, k]
        high = gathered[(gy + 1) & 7, k]
        for odd in range(2):
            value = pair[2 * k + odd]
            above = low if odd == 0 else shift(low, 4, 0)
            below = shift(high, 4, 0) if odd == 0 else high
            tiles.append(jnp.where(row < 4, above, value[0:8]))
            tiles.append(value[8:16])
            tiles.append(jnp.where(row < 4, value[16:24], below))
    for z in range(12):
        for t in range(3):
            pair_out[z, 8 * t : 8 * t + 8] = tiles[3 * z + t]
    for packed in range(3):
        left = jnp.zeros((8, 128), F32)
        right = jnp.zeros((8, 128), F32)
        for s, tile in enumerate(tiles[16 * packed : 16 * packed + 16]):
            here = slot_of == s
            first = (lane & 7) < 4
            left = jnp.where(here, jnp.where(first, shift(tile, 8 * s, 1), shift(tile, 8 * s - 60, 1)), left)
            right = jnp.where(here, jnp.where(first, shift(tile, 8 * s - 60, 1), shift(tile, 8 * s - 120, 1)), right)
        share[(gx - 1) & 3, packed] = left
        share[(gx + 1) & 3, packed] = right
    for slot in range(4):
        for g in range(8):
            share[slot, 3 + 8 * g : 11 + 8 * g] = gathered[g, 6:14]


def cplane(ref, z):
    return ref[pl.ds(8 * z, 8)].reshape(64, 128)


def cput(ref, z, value):
    ref[pl.ds(8 * z, 8)] = value.reshape(8, 8, 128)


def conjugate(gathered, other, kappa, wx, wy, wz, diag, rest, direction, image, answer):
    lane = iota((8, 128), 1)
    group = lax.shift_right_logical(lane, 5)
    nothing = jnp.zeros((64, 128), F32)
    cput(kappa, 0, nothing)
    cput(kappa, 33, nothing)
    cput(rest, 32, nothing)
    cput(wz, 0, nothing)
    direction[...] = jnp.zeros_like(direction)

    for source, parity in ((gathered, lax.axis_index("gz") & 1), (other, 1 - (lax.axis_index("gz") & 1))):

        def assemble(g, carry):
            gz = 2 * g + parity
            for gy in range(8):
                pieces = [source[gx, 3 + gy * 8 + g] for gx in range(4)]
                for q in range(4):
                    merged = pieces[0]
                    for gx in range(1, 4):
                        merged = jnp.where(group == (q + gx) % 4, pieces[gx], merged)
                    merged = shift(merged, -32 * q, 1)
                    if q < 2:
                        rest[(2 * gz + q) * 8 + gy] = merged
                    else:
                        kappa[(2 * gz + q - 1) * 8 + gy] = merged
            return carry

        loop(0, 8, assemble, 0, 2)
    inner_x = iota((64, 128), 1) < 127
    inner_y = iota((64, 128), 0) < 63
    first_x = iota((64, 128), 1) > 0
    first_y = iota((64, 128), 0) > 0

    def weights(z, total):
        half = 0.03125 * cplane(kappa, z + 1)
        before = 0.03125 * cplane(kappa, z)
        after = 0.03125 * cplane(kappa, z + 2)
        x = jnp.where(inner_x, ahead(half, 1), 0.0)
        y = jnp.where(inner_y, ahead(half, 0), 0.0)
        cput(wx, z, jnp.where(inner_x, half + x, 0.0))
        cput(wy, z, jnp.where(inner_y, half + y, 0.0))
        cput(wz, z + 1, half + after)
        x = x + jnp.where(first_x, behind(half, 1), 0.0)
        y = y + jnp.where(first_y, behind(half, 0), 0.0)
        cput(diag, z, 6.0 * half + x + y + (before + after))
        r = cplane(rest, z)
        return total + (r * r).reshape(8, 8, 128).sum(0)

    zero = jnp.zeros((8, 128), F32)

    def whole(total):
        return jnp.sum(jnp.sum(total, axis=0, keepdims=True), axis=1, keepdims=True)

    norm = whole(loop(0, 32, weights, zero))

    def image_of(beta):
        def turned(z):
            v = cplane(rest, z) + beta * cplane(direction, z + 1)
            cput(direction, z + 1, v)
            return v

        def apply(z, carry):
            before, v, total = carry
            after = turned(z + 1)
            x = cplane(wx, z)
            y = cplane(wy, z)
            w = cplane(diag, z) * v
            w = w - (x * ahead(v, 1) + behind(x * v, 1))
            w = w - (y * ahead(v, 0) + behind(y * v, 0))
            w = w - (cplane(wz, z + 1) * after + cplane(wz, z) * before)
            cput(image, z, w)
            return v, after, total + (v * w).reshape(8, 8, 128).sum(0)

        return whole(loop(0, 32, apply, (nothing, turned(0), zero), INNER)[2])

    gx = lax.axis_index("gx")
    gy = lax.axis_index("gy")
    gz = lax.axis_index("gz")
    answer[...] = jnp.zeros_like(answer)
    picked = [(3 * z + t, 2 * gz - 3 + z, gy - 1 + t) for z in range(8) for t in range(3)]

    def add_answer(alpha):
        for k, z, y in picked:
            tile = direction[(jnp.clip(z, 0, 31) + 1) * 8 + jnp.clip(y, 0, 7)]
            answer[k] = answer[k] + alpha * tile

    def iterate(repeat, carry):
        norm, beta = carry
        alpha = norm / image_of(beta)

        def step(z, total):
            r = cplane(rest, z) - alpha * cplane(image, z)
            cput(rest, z, r)
            return total + (r * r).reshape(8, 8, 128).sum(0)

        add_answer(alpha)
        norm_next = whole(loop(0, 32, step, zero, OUTER))
        return norm_next, norm_next / norm

    norm, beta = lax.fori_loop(0, ITERS - 1, iterate, (norm, jnp.zeros((1, 1), F32)))
    add_answer(norm / image_of(beta))
    wide = iota((8, 128), 1)
    position = jnp.where(wide < 64, wide, wide - 128) + 32 * gx
    known = (position >= 0) & (position < 128)
    tiles = []
    for k, z, y in picked:
        inside = known & (z >= 0) & (z < 32) & (y >= 0) & (y < 8)
        tiles.append(jnp.where(inside, pltpu.roll(answer[k], (128 - 32 * gx) & 127, 1), 0.0))
    return jnp.stack(tiles).reshape(8, 24, 128)


def middle_fields(gathered, pair):
    lane = iota((8, 128), 1)
    gx = lax.axis_index("gx")
    both = [[], []]
    for v in range(36):
        packed, s = v // 16, v % 16
        low = gathered[(gx - 1) & 3, packed]
        high = gathered[(gx + 1) & 3, packed]
        tile = pair[v // 3, 8 * (v % 3) : 8 * (v % 3) + 8]
        for k in range(2):
            own = shift(tile, 64 * k, 1) if k else tile
            edge = jnp.where(lane < 68, shift(high, 64 - 8 * s - 4 * k, 1), shift(low, 124 - 8 * s - 4 * k, 1))
            both[k].append(jnp.where(lane < 64, own, edge))
    return [jnp.stack(tiles).reshape(12, 24, 128) for tiles in both]


def up_kernel(
    gathered, other, pair, k1, iterate, right, wx, wy, wz, inverse,
    solution_out, residual_out,
    line, fine_a, fine_b, current, rest, update, second, *grids,
):
    c = conjugate(gathered, other, *grids)
    um, mr = middle_fields(gathered, pair)
    even = 0.75 * c[1:7] + 0.25 * c[0:6]
    odd = 0.75 * c[1:7] + 0.25 * c[2:8]
    c = jnp.stack([even, odd], 1).reshape(12, 24, 128)
    matrix = refine_matrix(128, 128)
    line[pl.ds(0, 288, stride=2), :] = exact_dot((0.75 * c + 0.25 * behind(c, 1)).reshape(288, 128), matrix)
    line[pl.ds(1, 288, stride=2), :] = exact_dot((0.75 * c + 0.25 * ahead(c, 1)).reshape(288, 128), matrix)
    correction = shift(line[...].reshape(12, 48, 128), -12, 1)[:, :24]

    kappa_one = k1[...]
    weights = middle_weights(kappa_one)
    inverse_one = weights[3]
    u = jnp.where(kappa_one > 0.0, um + correction, 0.0)
    r = mr + middle_minus(u, weights)
    d = FIRST * (r * inverse_one)
    u = u + d
    r = r + middle_minus(d, weights)
    u = u + (KEEP * d + GAIN * (r * inverse_one))

    even = 0.75 * u[2:10] + 0.25 * u[1:9]
    odd = 0.75 * u[2:10] + 0.25 * u[3:11]
    m = jnp.stack([even, odd], 1).reshape(16, 24, 128)
    matrix = refine_matrix(128, 256)
    for parity, near in enumerate((behind(m, 1), ahead(m, 1))):
        value = exact_dot((0.75 * m + 0.25 * near).reshape(384, 128), matrix)
        fine_a[pl.ds(parity, 384, stride=2), :] = value[:, :128]
        fine_b[pl.ds(parity, 384, stride=2), :] = value[:, 128:]

    def begin(z, carry):
        rows = pl.ds(pl.multiple_of((z - 4) * 48, 48), 48)
        fine = jnp.concatenate([fine_a[rows, :], fine_b[rows, :]], 1)
        put(current, z, jnp.where(plane(inverse, z) > 0.0, plane(iterate, z) + fine, 0.0))
        return carry

    loop(4, 20, begin, 0)

    def first(z, v, minus):
        r = plane(right, z) + minus
        put(rest, z, r)
        put(update, z, FIRST * r * plane(inverse, z))

    sweep(5, 18, current, wx, wy, wz, first, SWEEP_UP)

    def next_step(z, v, minus):
        r = plane(rest, z) + minus
        d = KEEP * v + GAIN * (r * plane(inverse, z))
        put(second, z, d)
        put_own(rest, z, r)
        put_own(current, z, plane(current, z) + v + d)

    sweep(6, 17, update, wx, wy, wz, next_step, SWEEP_UP)

    def last(z, v, minus):
        residual_out[z - 8] = (plane(rest, z) + minus)[8:40, :128]
        solution_out[z - 8] = plane(current, z)[8:40, :128]

    sweep(8, 15, second, wx, wy, wz, last, SWEEP_UP)


def run(kernel, outs, scratch, *args):
    return pl.pallas_call(
        kernel,
        out_shape=[jax.ShapeDtypeStruct(shape, F32) for shape in outs],
        in_specs=[VMEM] * len(args),
        out_specs=[VMEM] * len(outs),
        scratch_shapes=[pltpu.VMEM(shape, F32) for shape in scratch],
        compiler_params=pltpu.CompilerParams(vmem_limit_bytes=LIMIT),
    )(*args)


FINE = (144, 8, 256)
MIDDLE = (12, 24, 128)
COARSE = (256, 8, 128)
PADDED = (272, 8, 128)
YPACK = ([(66, 8, 128)] * 2, [])
XPACK = ([(72, 6, 8, 128), (27, 8, 128), (27, 8, 128)], [])
DOWN = ([(16, 5, 8, 128), MIDDLE, MIDDLE] + [FINE] * 6, [FINE] * 5 + [(960, 128)] * 2 + [(24, 128)])
TURN = ([(8, 14, 8, 128), MIDDLE], [])
CROSS = ([(4, 67, 8, 128), MIDDLE], [])
UP = (
    [(8, 32, 128)] * 2,
    [(576, 128)] + [(768, 128)] * 2 + [FINE] * 4
    + [PADDED] + [COARSE] * 2 + [PADDED, COARSE] + [PADDED] * 2 + [COARSE, (24, 8, 128)],
)


def up(axis):
    return [(i, i + 1) for i in range(lax.axis_size(axis) - 1)]


def down(axis):
    return [(i + 1, i) for i in range(lax.axis_size(axis) - 1)]


def both_ways(to_low, to_high, axis):
    return lax.ppermute(to_high, axis, up(axis)), lax.ppermute(to_low, axis, down(axis))


def local(right_side, guess, coefficient):
    mine = jnp.stack([guess, right_side, coefficient])
    beside = lax.ppermute(mine, "gz", [(i, ((i + 1) ^ 1) - 1) for i in range(1, 15)])
    chip = lax.ppermute(mine, "gz", [(i, i ^ 1) for i in range(16)])
    to_high, to_low = run(ypack_kernel, *YPACK, mine, chip, beside)
    ylow, yhigh = both_ways(to_low, to_high, "gy")
    window, to_right, to_left = run(
        xpack_kernel, *XPACK, mine, chip, beside, ylow, yhigh
    )
    from_left, from_right = both_ways(to_left, to_right, "gx")

    share, pair, k1, *arrays = run(down_kernel, *DOWN, window, from_left, from_right)
    share, pair = run(turn_kernel, *TURN, lax.all_to_all(share, "gz", 0, 0), pair)
    share, pair = run(cross_kernel, *CROSS, lax.all_to_all(share, "gy", 0, 0), pair)
    whole = lax.all_to_all(share, "gx", 0, 0)
    other = lax.ppermute(whole, "gz", [(i, i ^ 1) for i in range(16)])
    return run(up_kernel, *UP, whole, other, pair, k1, *arrays)


def solution(mesh):
    spec = P("gz", "gy", "gx")
    return jax.shard_map(
        local, mesh=mesh, in_specs=(spec, spec, spec), out_specs=(spec, spec), check_vma=False
    )
```

```python
import jax
import jax.numpy as jnp
from jax import lax
from jax.experimental import pallas as pl
from jax.experimental.pallas import tpu as pltpu
from jax.sharding import PartitionSpec as P


ITERS = 6
THETA = 1.25
DELTA = 0.75
SIGMA = THETA / DELTA
RHO = 1.0 / SIGMA
RHO_NEXT = 1.0 / (2.0 * SIGMA - RHO)
FIRST = 1.0 / THETA
KEEP = RHO_NEXT * RHO
GAIN = 2.0 * RHO_NEXT / DELTA

INNER = 16
SWEEP = 8
SWEEP_UP = 16
OUTER = 16
F32 = jnp.float32
BF16 = jnp.bfloat16
VMEM = pl.BlockSpec(memory_space=pltpu.VMEM)
LIMIT = 20 * 1024 * 1024


def loop(first, end, body, carry, unroll=16):
    count = end - first
    while count % unroll:
        unroll -= 1

    def several(i, carry):
        for k in range(unroll):
            carry = body(first + i * unroll + k, carry)
        return carry

    return lax.fori_loop(0, count // unroll, several, carry)


def shift(value, by, axis):
    return pltpu.roll(value, by % value.shape[axis], axis)


def ahead(value, axis):
    return shift(value, -1, axis)


def behind(value, axis):
    return shift(value, 1, axis)


def iota(shape, axis):
    return lax.broadcasted_iota(jnp.int32, shape, axis)


def exact_dot(value, matrix):
    high = value.astype(BF16)
    rest = value - high.astype(F32)
    middle = rest.astype(BF16)
    low = (rest - middle.astype(F32)).astype(BF16)
    parts = [jnp.dot(part, matrix, preferred_element_type=F32) for part in (low, middle, high)]
    return parts[0] + parts[1] + parts[2]


def pick(condition, number):
    return jnp.where(condition, jnp.float32(number), jnp.float32(0.0))


def reciprocal(value):
    guess = pl.reciprocal(value, approx=True)
    for _ in range(2):
        guess = guess * (2.0 - value * guess)
    return guess


def refine_matrix(size, out_size):
    parent = iota((size, out_size), 0)
    child = iota((size, out_size), 1)
    own = lax.shift_right_arithmetic(child, 1)
    other = (own + 2 * (child & 1) - 1 + size) & (size - 1)
    wide = out_size // 2
    if wide < size:
        own = jnp.where(child >= out_size * 3 // 4, own + size - wide, own)
        other = (own + 2 * (child & 1) - 1 + size) & (size - 1)
    return (pick(parent == own, 0.75) + pick(parent == other, 0.25)).astype(BF16)


TRAVEL = [(a, z) for a, skip in enumerate((1, 2, 0)) for z in range(skip, 24 - skip)]


def window_rows(mine, chip, beside, a, z, rows):
    if z // 8 == 1:
        return mine[a, z - 8, rows]
    odd = (lax.axis_index("gz") & 1) == 1
    return jnp.where(odd == (z < 8), chip[a, z % 8, rows], beside[a, z % 8, rows])


def ypack_kernel(mine, chip, beside, to_high, to_low):
    for i, (a, z) in enumerate(TRAVEL):
        to_low[i] = window_rows(mine, chip, beside, a, z, slice(0, 8))
        to_high[i] = window_rows(mine, chip, beside, a, z, slice(24, 32))


def xpack_kernel(mine, chip, beside, yhigh, ylow, window, to_right, to_left):
    for i, (a, z) in enumerate(TRAVEL):
        window[24 * a + z, 0] = ylow[i]
        window[24 * a + z, 1:5] = window_rows(mine, chip, beside, a, z, slice(0, 32)).reshape(4, 8, 128)
        window[24 * a + z, 5] = yhigh[i]
    slot = lax.shift_right_logical(iota((8, 128), 1), 3)

    def group(i, carry):
        for packed in range(3):
            left = jnp.zeros((8, 128), F32)
            right = jnp.zeros((8, 128), F32)
            for s in range(16):
                j = packed * 16 + s
                tile = window[8 * i + j // 6, j % 6]
                rolled = shift(tile, 8 * s, 1)
                left = jnp.where(slot == s, rolled, left)
                right = jnp.where(slot == (s - 1) % 16, rolled, right)
            to_left[3 * i + packed] = left
            to_right[3 * i + packed] = right
        return carry

    loop(0, 9, group, 0)


def plane(ref, z):
    return ref[pl.ds(6 * z, 6)].reshape(48, 256)


def put(ref, z, value):
    ref[pl.ds(6 * z, 6)] = value.reshape(6, 8, 256)


def put_own(ref, z, value):
    ref[pl.ds(6 * z + 1, 4), :, :128] = value[8:40, :128].reshape(4, 8, 128)


def inner_flux(v, wx, wy):
    fx = wx * (ahead(v, 1) - v)
    fy = wy * (ahead(v, 0) - v)
    return (fx - behind(fx, 1)) + (fy - behind(fy, 0))


def sweep(first, last, source, wx, wy, wz, step, unroll):
    v = plane(source, first)
    carry = (v, plane(wz, first - 1) * (v - plane(source, first - 1)))

    def body(z, carry):
        v, below = carry
        after = plane(source, z + 1)
        above = plane(wz, z) * (after - v)
        step(z, v, inner_flux(v, plane(wx, z), plane(wy, z)) + (above - below))
        return (after, above)

    loop(first, last + 1, body, carry, unroll)


def zpair(low_face):
    pad = jnp.zeros((1,) + low_face.shape[1:], F32)
    return jnp.concatenate([low_face, pad], 0) - jnp.concatenate([pad, low_face], 0)


def middle_weights(kappa):
    half = 0.125 * kappa
    wx = half + ahead(half, 2)
    wy = half + ahead(half, 1)
    wz = half[:-1] + half[1:]
    pad = jnp.zeros((1,) + half.shape[1:], F32)
    diag = wx + behind(wx, 2) + wy + behind(wy, 1)
    diag = diag + jnp.concatenate([wz, pad], 0) + jnp.concatenate([pad, wz], 0)
    inside = kappa > 0.0
    inverse = jnp.where(inside, reciprocal(diag), 0.0)
    return wx, wy, wz, inverse


def middle_minus(v, weights):
    wx, wy, wz, _ = weights
    fx = wx * (ahead(v, 2) - v)
    fy = wy * (ahead(v, 1) - v)
    return (fx - behind(fx, 2)) + (fy - behind(fy, 1)) + zpair(wz * (v[1:] - v[:-1]))


def down_kernel(
    window, from_right, from_left,
    share, pair_out, k1_out, iterate, right, wx, wy, wz, inverse,
    kappa, guess, rest, update, second, sums_a, sums_b, line,
):
    lane = iota((8, 128), 1)
    slot_of = lax.shift_right_logical(lane, 3)
    beside = (lane < 8) | (lane >= 120)

    def unpack(i, dest, base):
        for packed in range(3):
            hi = from_right[base * 9 + 3 * i + packed]
            lo = from_left[base * 9 + 3 * i + packed]
            for s in range(16):
                j = packed * 16 + s
                edge = jnp.where(beside, shift(jnp.where(slot_of == s, hi, lo), -8 * s, 1), 0.0)
                dest[48 * i + j, :, 0:128] = window[base * 24 + 8 * i + j // 6, j % 6]
                dest[48 * i + j, :, 128:256] = edge

    def unpack_all(i, carry):
        unpack(i, guess, 0)
        unpack(i, right, 1)
        unpack(i, kappa, 2)
        return carry

    loop(0, 3, unpack_all, 0)

    def weights(z, carry):
        half, below = carry
        after = 0.5 * plane(kappa, z + 1)
        x = half + ahead(half, 1)
        y = half + ahead(half, 0)
        above = half + after
        diag = x + behind(x, 1) + y + behind(y, 0) + above + below
        inside = half > 0.0
        put(wx, z, x)
        put(wy, z, y)
        put(wz, z, above)
        put(inverse, z, jnp.where(inside, reciprocal(diag), 0.0))
        return (after, above)

    half1 = 0.5 * plane(kappa, 1)
    half2 = 0.5 * plane(kappa, 2)
    put(wz, 1, half1 + half2)
    loop(2, 22, weights, (half2, half1 + half2), SWEEP)

    def first(z, v, minus):
        r = plane(right, z) + minus
        put(rest, z, r)
        put(update, z, FIRST * r * plane(inverse, z))

    sweep(2, 21, guess, wx, wy, wz, first, SWEEP)

    def next_step(z, v, minus):
        r = plane(rest, z) + minus
        d = KEEP * v + GAIN * (r * plane(inverse, z))
        put(rest, z, r)
        put(second, z, d)
        put(iterate, z, plane(guess, z) + v + d)

    sweep(3, 20, update, wx, wy, wz, next_step, SWEEP)

    def last(z, v, minus):
        put(rest, z, plane(rest, z) + minus)

    sweep(4, 19, second, wx, wy, wz, last, SWEEP)

    def add_pairs(ref, start, count, at):
        def body(m, carry):
            pair = plane(ref, start + 2 * m) + plane(ref, start + 2 * m + 1)
            rows = pl.ds(pl.multiple_of((at + m) * 48, 48), 48)
            sums_a[rows, :] = pair[:, :128]
            sums_b[rows, :] = pair[:, 128:]
            return carry

        loop(0, count, body, 0)

    add_pairs(rest, 4, 8, 0)
    add_pairs(kappa, 0, 12, 8)

    def fold(ref):
        return ref[pl.ds(0, 480, stride=2), :] + ref[pl.ds(1, 480, stride=2), :]

    coarsen = pick(lax.shift_right_logical(iota((256, 128), 0), 1) == iota((256, 128), 1), 0.125)
    both = exact_dot(jnp.concatenate([fold(sums_a), fold(sums_b)], 1), coarsen.astype(BF16))
    both = both.reshape(20, 24, 128)
    kappa_one = both[8:]
    pad = jnp.zeros((2, 24, 128), F32)
    rhs = jnp.concatenate([pad, both[:8], pad], 0)
    weights_one = middle_weights(kappa_one)
    inverse_one = weights_one[3]
    d = FIRST * (rhs * inverse_one)
    r = rhs + middle_minus(d, weights_one)
    d2 = KEEP * d + GAIN * (r * inverse_one)
    r = r + middle_minus(d2, weights_one)
    wide = iota((12, 24, 128), 2)
    um = d + d2
    pair = jnp.where(wide < 64, um, shift(rhs, 64, 2))
    pair_out[...] = pair
    k1_out[...] = kappa_one

    cell = iota((128, 128), 0)
    place = iota((128, 128), 1)
    total = jnp.zeros((24, 128), F32)
    for q, field in enumerate((r[4] + r[5], r[6] + r[7], kappa_one[4] + kappa_one[5], kappa_one[6] + kappa_one[7])):
        to = (cell < 64) & (lax.shift_right_logical(cell, 1) + 32 * q == place)
        total = total + exact_dot(field, pick(to, 0.125).astype(BF16))
    line[...] = total
    cells = line[pl.ds(4, 8, stride=2), :] + line[pl.ds(5, 8, stride=2), :]
    cells = pltpu.roll(cells, 32 * lax.axis_index("gx"), 1)
    for slot in range(16):
        share[slot, 4] = cells
    gz = lax.axis_index("gz")
    for step, planes in ((1, (um[4], um[5], um[6], rhs[5])), (-1, (um[5], um[6], um[7], rhs[6]))):
        for k, value in enumerate(planes):
            rows = shift(value, -4, 0)
            share[(gz + step) & 15, k] = jnp.where(lane < 64, rows[:8], shift(rows[8:16], 64, 1))


def turn_kernel(gathered, pair, share, pair_out):
    lane = iota((8, 128), 1)
    row = iota((8, 128), 0)
    gy = lax.axis_index("gy")
    gz = lax.axis_index("gz")
    wide = iota((24, 128), 1)

    def spread(tile):
        value = jnp.concatenate([tile, shift(tile, 64, 1), jnp.zeros((8, 128), F32)], 0)
        return shift(value, 4, 0)

    planes = [pair[z] for z in range(12)]
    for step, first, where_rhs in ((-1, 0, 1), (1, 9, 10)):
        for k in range(3):
            planes[first + k] = jnp.where(wide < 64, spread(gathered[(gz + step) & 15, k]), planes[first + k])
        value = shift(spread(gathered[(gz + step) & 15, 3]), 64, 1)
        planes[where_rhs] = jnp.where(wide < 64, planes[where_rhs], value)
    for z in range(12):
        pair_out[z] = planes[z]
    for g in range(8):
        piece = gathered[2 * g + (gz & 1), 4]
        for slot in range(8):
            share[slot, 6 + g] = piece
    for k in range(6):
        one, two = planes[2 * k], planes[2 * k + 1]
        share[(gy - 1) & 7, k] = jnp.where(row < 4, shift(one[0:8], 4, 0), two[0:8])
        share[(gy + 1) & 7, k] = jnp.where(row < 4, one[16:24], shift(two[16:24], 4, 0))


def cross_kernel(gathered, pair, share, pair_out):
    lane = iota((8, 128), 1)
    row = iota((8, 128), 0)
    slot_of = lax.shift_right_logical(lane, 3)
    gx = lax.axis_index("gx")
    gy = lax.axis_index("gy")
    tiles = []
    for k in range(6):
        low = gathered[(gy - 1) & 7, k]
        high = gathered[(gy + 1) & 7, k]
        for odd in range(2):
            value = pair[2 * k + odd]
            above = low if odd == 0 else shift(low, 4, 0)
            below = shift(high, 4, 0) if odd == 0 else high
            tiles.append(jnp.where(row < 4, above, value[0:8]))
            tiles.append(value[8:16])
            tiles.append(jnp.where(row < 4, value[16:24], below))
    for z in range(12):
        for t in range(3):
            pair_out[z, 8 * t : 8 * t + 8] = tiles[3 * z + t]
    for packed in range(3):
        left = jnp.zeros((8, 128), F32)
        right = jnp.zeros((8, 128), F32)
        for s, tile in enumerate(tiles[16 * packed : 16 * packed + 16]):
            here = slot_of == s
            first = (lane & 7) < 4
            left = jnp.where(here, jnp.where(first, shift(tile, 8 * s, 1), shift(tile, 8 * s - 60, 1)), left)
            right = jnp.where(here, jnp.where(first, shift(tile, 8 * s - 60, 1), shift(tile, 8 * s - 120, 1)), right)
        share[(gx - 1) & 3, packed] = left
        share[(gx + 1) & 3, packed] = right
    for slot in range(4):
        for g in range(8):
            share[slot, 3 + 8 * g : 11 + 8 * g] = gathered[g, 6:14]


def cplane(ref, z):
    return ref[pl.ds(8 * z, 8)].reshape(64, 128)


def cput(ref, z, value):
    ref[pl.ds(8 * z, 8)] = value.reshape(8, 8, 128)


def conjugate(gathered, other, kappa, wx, wy, wz, diag, rest, direction, image, answer):
    lane = iota((8, 128), 1)
    group = lax.shift_right_logical(lane, 5)
    nothing = jnp.zeros((64, 128), F32)
    cput(kappa, 0, nothing)
    cput(kappa, 33, nothing)
    cput(rest, 32, nothing)
    cput(wz, 0, nothing)
    direction[...] = jnp.zeros_like(direction)

    for source, parity in ((gathered, lax.axis_index("gz") & 1), (other, 1 - (lax.axis_index("gz") & 1))):

        def assemble(g, carry):
            gz = 2 * g + parity
            for gy in range(8):
                pieces = [source[gx, 3 + gy * 8 + g] for gx in range(4)]
                for q in range(4):
                    merged = pieces[0]
                    for gx in range(1, 4):
                        merged = jnp.where(group == (q + gx) % 4, pieces[gx], merged)
                    merged = shift(merged, -32 * q, 1)
                    if q < 2:
                        rest[(2 * gz + q) * 8 + gy] = merged
                    else:
                        kappa[(2 * gz + q - 1) * 8 + gy] = merged
            return carry

        loop(0, 8, assemble, 0, 2)
    inner_x = iota((64, 128), 1) < 127
    inner_y = iota((64, 128), 0) < 63
    first_x = iota((64, 128), 1) > 0
    first_y = iota((64, 128), 0) > 0

    def weights(z, total):
        half = 0.03125 * cplane(kappa, z + 1)
        before = 0.03125 * cplane(kappa, z)
        after = 0.03125 * cplane(kappa, z + 2)
        x = jnp.where(inner_x, ahead(half, 1), 0.0)
        y = jnp.where(inner_y, ahead(half, 0), 0.0)
        cput(wx, z, jnp.where(inner_x, half + x, 0.0))
        cput(wy, z, jnp.where(inner_y, half + y, 0.0))
        cput(wz, z + 1, half + after)
        x = x + jnp.where(first_x, behind(half, 1), 0.0)
        y = y + jnp.where(first_y, behind(half, 0), 0.0)
        cput(diag, z, 6.0 * half + x + y + (before + after))
        r = cplane(rest, z)
        return total + (r * r).reshape(8, 8, 128).sum(0)

    zero = jnp.zeros((8, 128), F32)

    def whole(total):
        return jnp.sum(jnp.sum(total, axis=0, keepdims=True), axis=1, keepdims=True)

    norm = whole(loop(0, 32, weights, zero))

    def image_of(beta):
        def turned(z):
            v = cplane(rest, z) + beta * cplane(direction, z + 1)
            cput(direction, z + 1, v)
            return v

        def apply(z, carry):
            before, v, total = carry
            after = turned(z + 1)
            x = cplane(wx, z)
            y = cplane(wy, z)
            w = cplane(diag, z) * v
            w = w - (x * ahead(v, 1) + behind(x * v, 1))
            w = w - (y * ahead(v, 0) + behind(y * v, 0))
            w = w - (cplane(wz, z + 1) * after + cplane(wz, z) * before)
            cput(image, z, w)
            return v, after, total + (v * w).reshape(8, 8, 128).sum(0)

        return whole(loop(0, 32, apply, (nothing, turned(0), zero), INNER)[2])

    gx = lax.axis_index("gx")
    gy = lax.axis_index("gy")
    gz = lax.axis_index("gz")
    answer[...] = jnp.zeros_like(answer)
    picked = [(3 * z + t, 2 * gz - 3 + z, gy - 1 + t) for z in range(8) for t in range(3)]

    def add_answer(alpha):
        for k, z, y in picked:
            tile = direction[(jnp.clip(z, 0, 31) + 1) * 8 + jnp.clip(y, 0, 7)]
            answer[k] = answer[k] + alpha * tile

    def iterate(repeat, carry):
        norm, beta = carry
        alpha = norm / image_of(beta)

        def step(z, total):
            r = cplane(rest, z) - alpha * cplane(image, z)
            cput(rest, z, r)
            return total + (r * r).reshape(8, 8, 128).sum(0)

        add_answer(alpha)
        norm_next = whole(loop(0, 32, step, zero, OUTER))
        return norm_next, norm_next / norm

    norm, beta = lax.fori_loop(0, ITERS - 1, iterate, (norm, jnp.zeros((1, 1), F32)))
    add_answer(norm / image_of(beta))
    wide = iota((8, 128), 1)
    position = jnp.where(wide < 64, wide, wide - 128) + 32 * gx
    known = (position >= 0) & (position < 128)
    tiles = []
    for k, z, y in picked:
        inside = known & (z >= 0) & (z < 32) & (y >= 0) & (y < 8)
        tiles.append(jnp.where(inside, pltpu.roll(answer[k], (128 - 32 * gx) & 127, 1), 0.0))
    return jnp.stack(tiles).reshape(8, 24, 128)


def middle_fields(gathered, pair):
    lane = iota((8, 128), 1)
    gx = lax.axis_index("gx")
    both = [[], []]
    for v in range(36):
        packed, s = v // 16, v % 16
        low = gathered[(gx - 1) & 3, packed]
        high = gathered[(gx + 1) & 3, packed]
        tile = pair[v // 3, 8 * (v % 3) : 8 * (v % 3) + 8]
        for k in range(2):
            own = shift(tile, 64 * k, 1) if k else tile
            edge = jnp.where(lane < 68, shift(high, 64 - 8 * s - 4 * k, 1), shift(low, 124 - 8 * s - 4 * k, 1))
            both[k].append(jnp.where(lane < 64, own, edge))
    return [jnp.stack(tiles).reshape(12, 24, 128) for tiles in both]


def up_kernel(
    gathered, other, pair, k1, iterate, right, wx, wy, wz, inverse,
    solution_out, residual_out,
    line, fine_a, fine_b, current, rest, update, second, *grids,
):
    c = conjugate(gathered, other, *grids)
    um, mr = middle_fields(gathered, pair)
    even = 0.75 * c[1:7] + 0.25 * c[0:6]
    odd = 0.75 * c[1:7] + 0.25 * c[2:8]
    c = jnp.stack([even, odd], 1).reshape(12, 24, 128)
    matrix = refine_matrix(128, 128)
    line[pl.ds(0, 288, stride=2), :] = exact_dot((0.75 * c + 0.25 * behind(c, 1)).reshape(288, 128), matrix)
    line[pl.ds(1, 288, stride=2), :] = exact_dot((0.75 * c + 0.25 * ahead(c, 1)).reshape(288, 128), matrix)
    correction = shift(line[...].reshape(12, 48, 128), -12, 1)[:, :24]

    kappa_one = k1[...]
    weights = middle_weights(kappa_one)
    inverse_one = weights[3]
    u = jnp.where(kappa_one > 0.0, um + correction, 0.0)
    r = mr + middle_minus(u, weights)
    d = FIRST * (r * inverse_one)
    u = u + d
    r = r + middle_minus(d, weights)
    u = u + (KEEP * d + GAIN * (r * inverse_one))

    even = 0.75 * u[2:10] + 0.25 * u[1:9]
    odd = 0.75 * u[2:10] + 0.25 * u[3:11]
    m = jnp.stack([even, odd], 1).reshape(16, 24, 128)
    matrix = refine_matrix(128, 256)
    for parity, near in enumerate((behind(m, 1), ahead(m, 1))):
        value = exact_dot((0.75 * m + 0.25 * near).reshape(384, 128), matrix)
        fine_a[pl.ds(parity, 384, stride=2), :] = value[:, :128]
        fine_b[pl.ds(parity, 384, stride=2), :] = value[:, 128:]

    def begin(z, carry):
        rows = pl.ds(pl.multiple_of((z - 4) * 48, 48), 48)
        fine = jnp.concatenate([fine_a[rows, :], fine_b[rows, :]], 1)
        put(current, z, jnp.where(plane(inverse, z) > 0.0, plane(iterate, z) + fine, 0.0))
        return carry

    loop(4, 20, begin, 0)

    def first(z, v, minus):
        r = plane(right, z) + minus
        put(rest, z, r)
        put(update, z, FIRST * r * plane(inverse, z))

    sweep(5, 18, current, wx, wy, wz, first, SWEEP_UP)

    def next_step(z, v, minus):
        r = plane(rest, z) + minus
        d = KEEP * v + GAIN * (r * plane(inverse, z))
        put(second, z, d)
        put_own(rest, z, r)
        put_own(current, z, plane(current, z) + v + d)

    sweep(6, 17, update, wx, wy, wz, next_step, SWEEP_UP)

    def last(z, v, minus):
        residual_out[z - 8] = (plane(rest, z) + minus)[8:40, :128]
        solution_out[z - 8] = plane(current, z)[8:40, :128]

    sweep(8, 15, second, wx, wy, wz, last, SWEEP_UP)


def run(kernel, outs, scratch, *args):
    return pl.pallas_call(
        kernel,
        out_shape=[jax.ShapeDtypeStruct(shape, F32) for shape in outs],
        in_specs=[VMEM] * len(args),
        out_specs=[VMEM] * len(outs),
        scratch_shapes=[pltpu.VMEM(shape, F32) for shape in scratch],
        compiler_params=pltpu.CompilerParams(vmem_limit_bytes=LIMIT),
    )(*args)


FINE = (144, 8, 256)
MIDDLE = (12, 24, 128)
COARSE = (256, 8, 128)
PADDED = (272, 8, 128)
YPACK = ([(66, 8, 128)] * 2, [])
XPACK = ([(72, 6, 8, 128), (27, 8, 128), (27, 8, 128)], [])
DOWN = ([(16, 5, 8, 128), MIDDLE, MIDDLE] + [FINE] * 6, [FINE] * 5 + [(960, 128)] * 2 + [(24, 128)])
TURN = ([(8, 14, 8, 128), MIDDLE], [])
CROSS = ([(4, 67, 8, 128), MIDDLE], [])
UP = (
    [(8, 32, 128)] * 2,
    [(576, 128)] + [(768, 128)] * 2 + [FINE] * 4
    + [PADDED] + [COARSE] * 2 + [PADDED, COARSE] + [PADDED] * 2 + [COARSE, (24, 8, 128)],
)


def up(axis):
    return [(i, i + 1) for i in range(lax.axis_size(axis) - 1)]


def down(axis):
    return [(i + 1, i) for i in range(lax.axis_size(axis) - 1)]


def both_ways(to_low, to_high, axis):
    return lax.ppermute(to_high, axis, up(axis)), lax.ppermute(to_low, axis, down(axis))


def local(right_side, guess, coefficient):
    mine = jnp.stack([guess, right_side, coefficient])
    beside = lax.ppermute(mine, "gz", [(i, ((i + 1) ^ 1) - 1) for i in range(1, 15)])
    chip = lax.ppermute(mine, "gz", [(i, i ^ 1) for i in range(16)])
    to_high, to_low = run(ypack_kernel, *YPACK, mine, chip, beside)
    ylow, yhigh = both_ways(to_low, to_high, "gy")
    window, to_right, to_left = run(
        xpack_kernel, *XPACK, mine, chip, beside, yhigh, ylow
    )
    from_left, from_right = both_ways(to_left, to_right, "gx")

    share, pair, k1, *arrays = run(down_kernel, *DOWN, window, from_right, from_left)
    share, pair = run(turn_kernel, *TURN, lax.all_to_all(share, "gz", 0, 0), pair)
    share, pair = run(cross_kernel, *CROSS, lax.all_to_all(share, "gy", 0, 0), pair)
    whole = lax.all_to_all(share, "gx", 0, 0)
    other = lax.ppermute(whole, "gz", [(i, i ^ 1) for i in range(16)])
    return run(up_kernel, *UP, whole, other, pair, k1, *arrays)


def solution(mesh):
    spec = P("gz", "gy", "gx")
    return jax.shard_map(
        local, mesh=mesh, in_specs=(spec, spec, spec), out_specs=(spec, spec), check_vma=False
    )
```

```python
import jax
import jax.numpy as jnp
from jax import lax
from jax.experimental import pallas as pl
from jax.experimental.pallas import tpu as pltpu
from jax.sharding import PartitionSpec as P


ITERS = 6
THETA = 1.25
DELTA = 0.75
SIGMA = THETA / DELTA
RHO = 1.0 / SIGMA
RHO_NEXT = 1.0 / (2.0 * SIGMA - RHO)
FIRST = 1.0 / THETA
KEEP = RHO_NEXT * RHO
GAIN = 2.0 * RHO_NEXT / DELTA

INNER = 16
SWEEP = 8
SWEEP_UP = 16
OUTER = 16
F32 = jnp.float32
BF16 = jnp.bfloat16
VMEM = pl.BlockSpec(memory_space=pltpu.VMEM)
LIMIT = 20 * 1024 * 1024


def loop(first, end, body, carry, unroll=16):
    count = end - first
    while count % unroll:
        unroll -= 1

    def several(i, carry):
        for k in range(unroll):
            carry = body(first + i * unroll + k, carry)
        return carry

    return lax.fori_loop(0, count // unroll, several, carry)


def shift(value, by, axis):
    return pltpu.roll(value, by % value.shape[axis], axis)


def ahead(value, axis):
    return shift(value, -1, axis)


def behind(value, axis):
    return shift(value, 1, axis)


def iota(shape, axis):
    return lax.broadcasted_iota(jnp.int32, shape, axis)


def exact_dot(value, matrix):
    high = value.astype(BF16)
    rest = value - high.astype(F32)
    middle = rest.astype(BF16)
    low = (rest - middle.astype(F32)).astype(BF16)
    parts = [jnp.dot(part, matrix, preferred_element_type=F32) for part in (low, middle, high)]
    return parts[0] + parts[1] + parts[2]


def pick(condition, number):
    return jnp.where(condition, jnp.float32(number), jnp.float32(0.0))


def reciprocal(value):
    guess = pl.reciprocal(value, approx=True)
    for _ in range(2):
        guess = guess * (2.0 - value * guess)
    return guess


def refine_matrix(size, out_size):
    parent = iota((size, out_size), 0)
    child = iota((size, out_size), 1)
    own = lax.shift_right_arithmetic(child, 1)
    other = (own + 2 * (child & 1) - 1 + size) & (size - 1)
    wide = out_size // 2
    if wide < size:
        own = jnp.where(child >= out_size * 3 // 4, own + size - wide, own)
        other = (own + 2 * (child & 1) - 1 + size) & (size - 1)
    return (pick(parent == own, 0.75) + pick(parent == other, 0.25)).astype(BF16)


TRAVEL = [(a, z) for a, skip in enumerate((1, 2, 0)) for z in range(skip, 24 - skip)]


DEPTH = (7, 6, 8)
START = (0, 7, 13)


def zpack_kernel(mine, to_chip, to_beside):
    odd = (lax.axis_index("gz") & 1) == 1
    for a in range(3):
        for z in range(DEPTH[a]):
            low = mine[a, z]
            high = mine[a, 8 - DEPTH[a] + z]
            to_chip[START[a] + z] = jnp.where(odd, low, high)
            to_beside[START[a] + z] = jnp.where(odd, high, low)


def window_rows(mine, chip, beside, a, z, rows):
    if z // 8 == 1:
        return mine[a, z - 8, rows]
    i = START[a] + (z - 8 + DEPTH[a] if z < 8 else z - 16)
    odd = (lax.axis_index("gz") & 1) == 1
    return jnp.where(odd == (z < 8), chip[i, rows], beside[i, rows])


def ypack_kernel(mine, chip, beside, to_high, to_low):
    for i, (a, z) in enumerate(TRAVEL):
        to_low[i] = window_rows(mine, chip, beside, a, z, slice(0, 8))
        to_high[i] = window_rows(mine, chip, beside, a, z, slice(24, 32))


def xpack_kernel(mine, chip, beside, yhigh, ylow, window, to_right, to_left):
    for i, (a, z) in enumerate(TRAVEL):
        window[24 * a + z, 0] = ylow[i]
        window[24 * a + z, 1:5] = window_rows(mine, chip, beside, a, z, slice(0, 32)).reshape(4, 8, 128)
        window[24 * a + z, 5] = yhigh[i]
    slot = lax.shift_right_logical(iota((8, 128), 1), 3)

    def group(i, carry):
        for packed in range(3):
            left = jnp.zeros((8, 128), F32)
            right = jnp.zeros((8, 128), F32)
            for s in range(16):
                j = packed * 16 + s
                tile = window[8 * i + j // 6, j % 6]
                rolled = shift(tile, 8 * s, 1)
                left = jnp.where(slot == s, rolled, left)
                right = jnp.where(slot == (s - 1) % 16, rolled, right)
            to_left[3 * i + packed] = left
            to_right[3 * i + packed] = right
        return carry

    loop(0, 9, group, 0)


def plane(ref, z):
    return ref[pl.ds(6 * z, 6)].reshape(48, 256)


def put(ref, z, value):
    ref[pl.ds(6 * z, 6)] = value.reshape(6, 8, 256)


def put_own(ref, z, value):
    ref[pl.ds(6 * z + 1, 4), :, :128] = value[8:40, :128].reshape(4, 8, 128)


def inner_flux(v, wx, wy):
    fx = wx * (ahead(v, 1) - v)
    fy = wy * (ahead(v, 0) - v)
    return (fx - behind(fx, 1)) + (fy - behind(fy, 0))


def sweep(first, last, source, wx, wy, wz, step, unroll):
    v = plane(source, first)
    carry = (v, plane(wz, first - 1) * (v - plane(source, first - 1)))

    def body(z, carry):
        v, below = carry
        after = plane(source, z + 1)
        above = plane(wz, z) * (after - v)
        step(z, v, inner_flux(v, plane(wx, z), plane(wy, z)) + (above - below))
        return (after, above)

    loop(first, last + 1, body, carry, unroll)


def zpair(low_face):
    pad = jnp.zeros((1,) + low_face.shape[1:], F32)
    return jnp.concatenate([low_face, pad], 0) - jnp.concatenate([pad, low_face], 0)


def middle_weights(kappa):
    half = 0.125 * kappa
    wx = half + ahead(half, 2)
    wy = half + ahead(half, 1)
    wz = half[:-1] + half[1:]
    pad = jnp.zeros((1,) + half.shape[1:], F32)
    diag = wx + behind(wx, 2) + wy + behind(wy, 1)
    diag = diag + jnp.concatenate([wz, pad], 0) + jnp.concatenate([pad, wz], 0)
    inside = kappa > 0.0
    inverse = jnp.where(inside, reciprocal(diag), 0.0)
    return wx, wy, wz, inverse


def middle_minus(v, weights):
    wx, wy, wz, _ = weights
    fx = wx * (ahead(v, 2) - v)
    fy = wy * (ahead(v, 1) - v)
    return (fx - behind(fx, 2)) + (fy - behind(fy, 1)) + zpair(wz * (v[1:] - v[:-1]))


def down_kernel(
    window, from_right, from_left,
    share, pair_out, k1_out, iterate, right, wx, wy, wz, inverse,
    kappa, guess, rest, update, second, sums_a, sums_b, line,
):
    lane = iota((8, 128), 1)
    slot_of = lax.shift_right_logical(lane, 3)
    beside = (lane < 8) | (lane >= 120)

    def unpack(i, dest, base):
        for packed in range(3):
            hi = from_right[base * 9 + 3 * i + packed]
            lo = from_left[base * 9 + 3 * i + packed]
            for s in range(16):
                j = packed * 16 + s
                edge = jnp.where(beside, shift(jnp.where(slot_of == s, hi, lo), -8 * s, 1), 0.0)
                dest[48 * i + j, :, 0:128] = window[base * 24 + 8 * i + j // 6, j % 6]
                dest[48 * i + j, :, 128:256] = edge

    def unpack_all(i, carry):
        unpack(i, guess, 0)
        unpack(i, right, 1)
        unpack(i, kappa, 2)
        return carry

    loop(0, 3, unpack_all, 0)

    def weights(z, carry):
        half, below = carry
        after = 0.5 * plane(kappa, z + 1)
        x = half + ahead(half, 1)
        y = half + ahead(half, 0)
        above = half + after
        diag = x + behind(x, 1) + y + behind(y, 0) + above + below
        inside = half > 0.0
        put(wx, z, x)
        put(wy, z, y)
        put(wz, z, above)
        put(inverse, z, jnp.where(inside, reciprocal(diag), 0.0))
        return (after, above)

    half1 = 0.5 * plane(kappa, 1)
    half2 = 0.5 * plane(kappa, 2)
    put(wz, 1, half1 + half2)
    loop(2, 22, weights, (half2, half1 + half2), SWEEP)

    def first(z, v, minus):
        r = plane(right, z) + minus
        put(rest, z, r)
        put(update, z, FIRST * r * plane(inverse, z))

    sweep(2, 21, guess, wx, wy, wz, first, SWEEP)

    def next_step(z, v, minus):
        r = plane(rest, z) + minus
        d = KEEP * v + GAIN * (r * plane(inverse, z))
        put(rest, z, r)
        put(second, z, d)
        put(iterate, z, plane(guess, z) + v + d)

    sweep(3, 20, update, wx, wy, wz, next_step, SWEEP)

    def last(z, v, minus):
        put(rest, z, plane(rest, z) + minus)

    sweep(4, 19, second, wx, wy, wz, last, SWEEP)

    def add_pairs(ref, start, count, at):
        def body(m, carry):
            pair = plane(ref, start + 2 * m) + plane(ref, start + 2 * m + 1)
            rows = pl.ds(pl.multiple_of((at + m) * 48, 48), 48)
            sums_a[rows, :] = pair[:, :128]
            sums_b[rows, :] = pair[:, 128:]
            return carry

        loop(0, count, body, 0)

    add_pairs(rest, 4, 8, 0)
    add_pairs(kappa, 0, 12, 8)

    def fold(ref):
        return ref[pl.ds(0, 480, stride=2), :] + ref[pl.ds(1, 480, stride=2), :]

    coarsen = pick(lax.shift_right_logical(iota((256, 128), 0), 1) == iota((256, 128), 1), 0.125)
    both = exact_dot(jnp.concatenate([fold(sums_a), fold(sums_b)], 1), coarsen.astype(BF16))
    both = both.reshape(20, 24, 128)
    kappa_one = both[8:]
    pad = jnp.zeros((2, 24, 128), F32)
    rhs = jnp.concatenate([pad, both[:8], pad], 0)
    weights_one = middle_weights(kappa_one)
    inverse_one = weights_one[3]
    d = FIRST * (rhs * inverse_one)
    r = rhs + middle_minus(d, weights_one)
    d2 = KEEP * d + GAIN * (r * inverse_one)
    r = r + middle_minus(d2, weights_one)
    wide = iota((12, 24, 128), 2)
    um = d + d2
    pair = jnp.where(wide < 64, um, shift(rhs, 64, 2))
    pair_out[...] = pair
    k1_out[...] = kappa_one

    cell = iota((128, 128), 0)
    place = iota((128, 128), 1)
    total = jnp.zeros((24, 128), F32)
    for q, field in enumerate((r[4] + r[5], r[6] + r[7], kappa_one[4] + kappa_one[5], kappa_one[6] + kappa_one[7])):
        to = (cell < 64) & (lax.shift_right_logical(cell, 1) + 32 * q == place)
        total = total + exact_dot(field, pick(to, 0.125).astype(BF16))
    line[...] = total
    cells = line[pl.ds(4, 8, stride=2), :] + line[pl.ds(5, 8, stride=2), :]
    cells = pltpu.roll(cells, 32 * lax.axis_index("gx"), 1)
    for slot in range(16):
        share[slot, 4] = cells
    gz = lax.axis_index("gz")
    for step, planes in ((1, (um[4], um[5], um[6], rhs[5])), (-1, (um[5], um[6], um[7], rhs[6]))):
        for k, value in enumerate(planes):
            rows = shift(value, -4, 0)
            share[(gz + step) & 15, k] = jnp.where(lane < 64, rows[:8], shift(rows[8:16], 64, 1))


def turn_kernel(gathered, pair, share, pair_out):
    lane = iota((8, 128), 1)
    row = iota((8, 128), 0)
    gy = lax.axis_index("gy")
    gz = lax.axis_index("gz")
    wide = iota((24, 128), 1)

    def spread(tile):
        value = jnp.concatenate([tile, shift(tile, 64, 1), jnp.zeros((8, 128), F32)], 0)
        return shift(value, 4, 0)

    planes = [pair[z] for z in range(12)]
    for step, first, where_rhs in ((-1, 0, 1), (1, 9, 10)):
        for k in range(3):
            planes[first + k] = jnp.where(wide < 64, spread(gathered[(gz + step) & 15, k]), planes[first + k])
        value = shift(spread(gathered[(gz + step) & 15, 3]), 64, 1)
        planes[where_rhs] = jnp.where(wide < 64, planes[where_rhs], value)
    for z in range(12):
        pair_out[z] = planes[z]
    for g in range(8):
        piece = gathered[2 * g + (gz & 1), 4]
        for slot in range(8):
            share[slot, 6 + g] = piece
    for k in range(6):
        one, two = planes[2 * k], planes[2 * k + 1]
        share[(gy - 1) & 7, k] = jnp.where(row < 4, shift(one[0:8], 4, 0), two[0:8])
        share[(gy + 1) & 7, k] = jnp.where(row < 4, one[16:24], shift(two[16:24], 4, 0))


def cross_kernel(gathered, pair, share, pair_out):
    lane = iota((8, 128), 1)
    row = iota((8, 128), 0)
    slot_of = lax.shift_right_logical(lane, 3)
    gx = lax.axis_index("gx")
    gy = lax.axis_index("gy")
    tiles = []
    for k in range(6):
        low = gathered[(gy - 1) & 7, k]
        high = gathered[(gy + 1) & 7, k]
        for odd in range(2):
            value = pair[2 * k + odd]
            above = low if odd == 0 else shift(low, 4, 0)
            below = shift(high, 4, 0) if odd == 0 else high
            tiles.append(jnp.where(row < 4, above, value[0:8]))
            tiles.append(value[8:16])
            tiles.append(jnp.where(row < 4, value[16:24], below))
    for z in range(12):
        for t in range(3):
            pair_out[z, 8 * t : 8 * t + 8] = tiles[3 * z + t]
    for packed in range(3):
        left = jnp.zeros((8, 128), F32)
        right = jnp.zeros((8, 128), F32)
        for s, tile in enumerate(tiles[16 * packed : 16 * packed + 16]):
            here = slot_of == s
            first = (lane & 7) < 4
            left = jnp.where(here, jnp.where(first, shift(tile, 8 * s, 1), shift(tile, 8 * s - 60, 1)), left)
            right = jnp.where(here, jnp.where(first, shift(tile, 8 * s - 60, 1), shift(tile, 8 * s - 120, 1)), right)
        share[(gx - 1) & 3, packed] = left
        share[(gx + 1) & 3, packed] = right
    for slot in range(4):
        for g in range(8):
            share[slot, 3 + 8 * g : 11 + 8 * g] = gathered[g, 6:14]


def cplane(ref, z):
    return ref[pl.ds(8 * z, 8)].reshape(64, 128)


def cput(ref, z, value):
    ref[pl.ds(8 * z, 8)] = value.reshape(8, 8, 128)


def conjugate(gathered, other, kappa, wx, wy, wz, diag, rest, direction, image, answer):
    lane = iota((8, 128), 1)
    group = lax.shift_right_logical(lane, 5)
    nothing = jnp.zeros((64, 128), F32)
    cput(kappa, 0, nothing)
    cput(kappa, 33, nothing)
    cput(rest, 32, nothing)
    cput(wz, 0, nothing)
    direction[...] = jnp.zeros_like(direction)

    for source, parity in ((gathered, lax.axis_index("gz") & 1), (other, 1 - (lax.axis_index("gz") & 1))):

        def assemble(g, carry):
            gz = 2 * g + parity
            for gy in range(8):
                pieces = [source[gx, 3 + gy * 8 + g] for gx in range(4)]
                for q in range(4):
                    merged = pieces[0]
                    for gx in range(1, 4):
                        merged = jnp.where(group == (q + gx) % 4, pieces[gx], merged)
                    merged = shift(merged, -32 * q, 1)
                    if q < 2:
                        rest[(2 * gz + q) * 8 + gy] = merged
                    else:
                        kappa[(2 * gz + q - 1) * 8 + gy] = merged
            return carry

        loop(0, 8, assemble, 0, 2)
    inner_x = iota((64, 128), 1) < 127
    inner_y = iota((64, 128), 0) < 63
    first_x = iota((64, 128), 1) > 0
    first_y = iota((64, 128), 0) > 0

    def weights(z, total):
        half = 0.03125 * cplane(kappa, z + 1)
        before = 0.03125 * cplane(kappa, z)
        after = 0.03125 * cplane(kappa, z + 2)
        x = jnp.where(inner_x, ahead(half, 1), 0.0)
        y = jnp.where(inner_y, ahead(half, 0), 0.0)
        cput(wx, z, jnp.where(inner_x, half + x, 0.0))
        cput(wy, z, jnp.where(inner_y, half + y, 0.0))
        cput(wz, z + 1, half + after)
        x = x + jnp.where(first_x, behind(half, 1), 0.0)
        y = y + jnp.where(first_y, behind(half, 0), 0.0)
        cput(diag, z, 6.0 * half + x + y + (before + after))
        r = cplane(rest, z)
        return total + (r * r).reshape(8, 8, 128).sum(0)

    zero = jnp.zeros((8, 128), F32)

    def whole(total):
        return jnp.sum(jnp.sum(total, axis=0, keepdims=True), axis=1, keepdims=True)

    norm = whole(loop(0, 32, weights, zero))

    def image_of(beta):
        def turned(z):
            v = cplane(rest, z) + beta * cplane(direction, z + 1)
            cput(direction, z + 1, v)
            return v

        def apply(z, carry):
            before, v, total = carry
            after = turned(z + 1)
            x = cplane(wx, z)
            y = cplane(wy, z)
            w = cplane(diag, z) * v
            w = w - (x * ahead(v, 1) + behind(x * v, 1))
            w = w - (y * ahead(v, 0) + behind(y * v, 0))
            w = w - (cplane(wz, z + 1) * after + cplane(wz, z) * before)
            cput(image, z, w)
            return v, after, total + (v * w).reshape(8, 8, 128).sum(0)

        return whole(loop(0, 32, apply, (nothing, turned(0), zero), INNER)[2])

    gx = lax.axis_index("gx")
    gy = lax.axis_index("gy")
    gz = lax.axis_index("gz")
    answer[...] = jnp.zeros_like(answer)
    picked = [(3 * z + t, 2 * gz - 3 + z, gy - 1 + t) for z in range(8) for t in range(3)]

    def add_answer(alpha):
        for k, z, y in picked:
            tile = direction[(jnp.clip(z, 0, 31) + 1) * 8 + jnp.clip(y, 0, 7)]
            answer[k] = answer[k] + alpha * tile

    def iterate(repeat, carry):
        norm, beta = carry
        alpha = norm / image_of(beta)

        def step(z, total):
            r = cplane(rest, z) - alpha * cplane(image, z)
            cput(rest, z, r)
            return total + (r * r).reshape(8, 8, 128).sum(0)

        add_answer(alpha)
        norm_next = whole(loop(0, 32, step, zero, OUTER))
        return norm_next, norm_next / norm

    norm, beta = lax.fori_loop(0, ITERS - 1, iterate, (norm, jnp.zeros((1, 1), F32)))
    add_answer(norm / image_of(beta))
    wide = iota((8, 128), 1)
    position = jnp.where(wide < 64, wide, wide - 128) + 32 * gx
    known = (position >= 0) & (position < 128)
    tiles = []
    for k, z, y in picked:
        inside = known & (z >= 0) & (z < 32) & (y >= 0) & (y < 8)
        tiles.append(jnp.where(inside, pltpu.roll(answer[k], (128 - 32 * gx) & 127, 1), 0.0))
    return jnp.stack(tiles).reshape(8, 24, 128)


def middle_fields(gathered, pair):
    lane = iota((8, 128), 1)
    gx = lax.axis_index("gx")
    both = [[], []]
    for v in range(36):
        packed, s = v // 16, v % 16
        low = gathered[(gx - 1) & 3, packed]
        high = gathered[(gx + 1) & 3, packed]
        tile = pair[v // 3, 8 * (v % 3) : 8 * (v % 3) + 8]
        for k in range(2):
            own = shift(tile, 64 * k, 1) if k else tile
            edge = jnp.where(lane < 68, shift(high, 64 - 8 * s - 4 * k, 1), shift(low, 124 - 8 * s - 4 * k, 1))
            both[k].append(jnp.where(lane < 64, own, edge))
    return [jnp.stack(tiles).reshape(12, 24, 128) for tiles in both]


def up_kernel(
    gathered, other, pair, k1, iterate, right, wx, wy, wz, inverse,
    solution_out, residual_out,
    line, fine_a, fine_b, current, rest, update, second, *grids,
):
    c = conjugate(gathered, other, *grids)
    um, mr = middle_fields(gathered, pair)
    even = 0.75 * c[1:7] + 0.25 * c[0:6]
    odd = 0.75 * c[1:7] + 0.25 * c[2:8]
    c = jnp.stack([even, odd], 1).reshape(12, 24, 128)
    matrix = refine_matrix(128, 128)
    line[pl.ds(0, 288, stride=2), :] = exact_dot((0.75 * c + 0.25 * behind(c, 1)).reshape(288, 128), matrix)
    line[pl.ds(1, 288, stride=2), :] = exact_dot((0.75 * c + 0.25 * ahead(c, 1)).reshape(288, 128), matrix)
    correction = shift(line[...].reshape(12, 48, 128), -12, 1)[:, :24]

    kappa_one = k1[...]
    weights = middle_weights(kappa_one)
    inverse_one = weights[3]
    u = jnp.where(kappa_one > 0.0, um + correction, 0.0)
    r = mr + middle_minus(u, weights)
    d = FIRST * (r * inverse_one)
    u = u + d
    r = r + middle_minus(d, weights)
    u = u + (KEEP * d + GAIN * (r * inverse_one))

    even = 0.75 * u[2:10] + 0.25 * u[1:9]
    odd = 0.75 * u[2:10] + 0.25 * u[3:11]
    m = jnp.stack([even, odd], 1).reshape(16, 24, 128)
    matrix = refine_matrix(128, 256)
    for parity, near in enumerate((behind(m, 1), ahead(m, 1))):
        value = exact_dot((0.75 * m + 0.25 * near).reshape(384, 128), matrix)
        fine_a[pl.ds(parity, 384, stride=2), :] = value[:, :128]
        fine_b[pl.ds(parity, 384, stride=2), :] = value[:, 128:]

    def begin(z, carry):
        rows = pl.ds(pl.multiple_of((z - 4) * 48, 48), 48)
        fine = jnp.concatenate([fine_a[rows, :], fine_b[rows, :]], 1)
        put(current, z, jnp.where(plane(inverse, z) > 0.0, plane(iterate, z) + fine, 0.0))
        return carry

    loop(4, 20, begin, 0)

    def first(z, v, minus):
        r = plane(right, z) + minus
        put(rest, z, r)
        put(update, z, FIRST * r * plane(inverse, z))

    sweep(5, 18, current, wx, wy, wz, first, SWEEP_UP)

    def next_step(z, v, minus):
        r = plane(rest, z) + minus
        d = KEEP * v + GAIN * (r * plane(inverse, z))
        put(second, z, d)
        put_own(rest, z, r)
        put_own(current, z, plane(current, z) + v + d)

    sweep(6, 17, update, wx, wy, wz, next_step, SWEEP_UP)

    def last(z, v, minus):
        residual_out[z - 8] = (plane(rest, z) + minus)[8:40, :128]
        solution_out[z - 8] = plane(current, z)[8:40, :128]

    sweep(8, 15, second, wx, wy, wz, last, SWEEP_UP)


def run(kernel, outs, scratch, *args):
    return pl.pallas_call(
        kernel,
        out_shape=[jax.ShapeDtypeStruct(shape, F32) for shape in outs],
        in_specs=[VMEM] * len(args),
        out_specs=[VMEM] * len(outs),
        scratch_shapes=[pltpu.VMEM(shape, F32) for shape in scratch],
        compiler_params=pltpu.CompilerParams(vmem_limit_bytes=LIMIT),
    )(*args)


FINE = (144, 8, 256)
MIDDLE = (12, 24, 128)
COARSE = (256, 8, 128)
PADDED = (272, 8, 128)
YPACK = ([(66, 8, 128)] * 2, [])
XPACK = ([(72, 6, 8, 128), (27, 8, 128), (27, 8, 128)], [])
DOWN = ([(16, 5, 8, 128), MIDDLE, MIDDLE] + [FINE] * 6, [FINE] * 5 + [(960, 128)] * 2 + [(24, 128)])
TURN = ([(8, 14, 8, 128), MIDDLE], [])
CROSS = ([(4, 67, 8, 128), MIDDLE], [])
UP = (
    [(8, 32, 128)] * 2,
    [(576, 128)] + [(768, 128)] * 2 + [FINE] * 4
    + [PADDED] + [COARSE] * 2 + [PADDED, COARSE] + [PADDED] * 2 + [COARSE, (24, 8, 128)],
)


def up(axis):
    return [(i, i + 1) for i in range(lax.axis_size(axis) - 1)]


def down(axis):
    return [(i + 1, i) for i in range(lax.axis_size(axis) - 1)]


def both_ways(to_low, to_high, axis):
    return lax.ppermute(to_high, axis, up(axis)), lax.ppermute(to_low, axis, down(axis))


def local(right_side, guess, coefficient):
    mine = jnp.stack([guess, right_side, coefficient])
    to_chip, to_beside = run(zpack_kernel, [(21, 32, 128)] * 2, [], mine)
    beside = lax.ppermute(to_beside, "gz", [(i, ((i + 1) ^ 1) - 1) for i in range(1, 15)])
    chip = lax.ppermute(to_chip, "gz", [(i, i ^ 1) for i in range(16)])
    to_high, to_low = run(ypack_kernel, *YPACK, mine, chip, beside)
    ylow, yhigh = both_ways(to_low, to_high, "gy")
    window, to_right, to_left = run(
        xpack_kernel, *XPACK, mine, chip, beside, yhigh, ylow
    )
    from_left, from_right = both_ways(to_left, to_right, "gx")

    share, pair, k1, *arrays = run(down_kernel, *DOWN, window, from_right, from_left)
    share, pair = run(turn_kernel, *TURN, lax.all_to_all(share, "gz", 0, 0), pair)
    share, pair = run(cross_kernel, *CROSS, lax.all_to_all(share, "gy", 0, 0), pair)
    whole = lax.all_to_all(share, "gx", 0, 0)
    other = lax.ppermute(whole, "gz", [(i, i ^ 1) for i in range(16)])
    return run(up_kernel, *UP, whole, other, pair, k1, *arrays)


def solution(mesh):
    spec = P("gz", "gy", "gx")
    return jax.shard_map(
        local, mesh=mesh, in_specs=(spec, spec, spec), out_specs=(spec, spec), check_vma=False
    )
```
